32 devices in a mesh: dp: 8 (over y, x, core), seq: 4 (over z).
Axes of the slice: x: 2, y: 2, z: 4, core: 2. Of those that a mesh axis runs over, the one named last changes fastest.
Arguments:
- tokens: bfloat16 [16, 1024, 2048], P('dp', 'seq'), may hold values from -40 to 40
- exit_layer: int32 [16, 1024], P('dp', 'seq'), may hold values from 1 to 24, as said below
- first_gain: bfloat16 [2048], P(('dp', 'seq')), may hold values from 0.099609375 to 1.8984375
- first_shift: bfloat16 [2048], P(('dp', 'seq')), may hold values from -1.75 to 1.75
- query_weight: bfloat16 [2048, 2048], P(('dp', 'seq')), may hold values from -0.125 to 0.125
- query_bias: bfloat16 [2048], P(('dp', 'seq')), may hold values from -3 to 3
- key_weight: bfloat16 [2048, 2048], P(('dp', 'seq')), may hold values from -0.125 to 0.125
- value_weight: bfloat16 [2048, 2048], P(('dp', 'seq')), may hold values from -0.125 to 0.125
- value_bias: bfloat16 [2048], P(('dp', 'seq')), may hold values from -3 to 3
- output_weight: bfloat16 [2048, 2048], P(('dp', 'seq')), may hold values from -0.75 to 0.75
- output_bias: bfloat16 [2048], P(('dp', 'seq')), may hold values from -1.75 to 1.75
- second_gain: bfloat16 [2048], P(('dp', 'seq')), may hold values from 0.099609375 to 1.8984375
- second_shift: bfloat16 [2048], P(('dp', 'seq')), may hold values from -1.75 to 1.75
- expand_weight: bfloat16 [8192, 2048], P(('dp', 'seq')), may hold values from -0.125 to 0.125
- expand_bias: bfloat16 [8192], P(('dp', 'seq')), may hold values from -3 to 3
- shrink_weight: bfloat16 [2048, 8192], P(('dp', 'seq')), may hold values from -0.0625 to 0.0625
- shrink_bias: bfloat16 [2048], P(('dp', 'seq')), may hold values from -1.75 to 1.75
- cotangent: bfloat16 [16, 1024, 2048], P('dp', 'seq'), may hold values from -8 to 8
Outputs:
- layer_out: bfloat16 [16, 1024, 2048], P('dp', 'seq')
- tokens_grad: bfloat16 [16, 1024, 2048], P('dp', 'seq')
- first_gain_grad: float32 [2048], P(('dp', 'seq'))
- first_shift_grad: float32 [2048], P(('dp', 'seq'))
- query_weight_grad: float32 [2048, 2048], P(('dp', 'seq'))
- query_bias_grad: float32 [2048], P(('dp', 'seq'))
- key_weight_grad: float32 [2048, 2048], P(('dp', 'seq'))
- value_weight_grad: float32 [2048, 2048], P(('dp', 'seq'))
- value_bias_grad: float32 [2048], P(('dp', 'seq'))
- output_weight_grad: float32 [2048, 2048], P(('dp', 'seq'))
- output_bias_grad: float32 [2048], P(('dp', 'seq'))
- second_gain_grad: float32 [2048], P(('dp', 'seq'))
- second_shift_grad: float32 [2048], P(('dp', 'seq'))
- expand_weight_grad: float32 [8192, 2048], P(('dp', 'seq'))
- expand_bias_grad: float32 [8192], P(('dp', 'seq'))
- shrink_weight_grad: float32 [2048, 8192], P(('dp', 'seq'))
- shrink_bias_grad: float32 [2048], P(('dp', 'seq'))
The draws below stay inside these ranges and needn't reach their ends.
Inputs may be any that keep to these rules, and one draw needn't show every extreme that they name: `exit_layer`: within each sequence the exit layer never rises from one position to the next; the first position of every sequence has 24; of the 2 sequences on each index of dp, one has every position above 12 except its last 16 positions, which are at or below 12.
All inputs are finite; a program needn't handle non-finite values.
Results may differ from the reference program's by a relative error of at most 0.012.
Values may be sent and summed in bfloat16 or wider, within the bound.
No kernel may reach another device: no remote copies, remote signals or barrier semaphores. Data moves between devices by JAX's collectives and lax.ppermute only.
A program may use at most 640 MiB of HBM per device.

```python
import jax
import jax.numpy as jnp
from jax import lax

D = 2048
HEADS = 32
HEAD_DIM = 64
FF = 8192
SEQS = 2
SEQ_LEN = 1024
LAYER = 12
LAYERS = 24
SEQUENCES = 16


def draw_tokens(key, part):
    key = jax.random.fold_in(key, 5)
    key_base, key_rows, key_cols = jax.random.split(key, 3)
    shape = (SEQUENCES, SEQ_LEN, D)
    row_scale = jnp.exp(jax.random.uniform(key_rows, (SEQUENCES, SEQ_LEN, 1), jnp.float32, -1.15, 1.15))
    col_scale = jnp.exp(jax.random.uniform(key_cols, (1, 1, D), jnp.float32, -1.15, 1.15))
    base = jnp.clip(jax.random.normal(key_base, shape, jnp.float32), -4.0, 4.0)
    return (base * row_scale * col_scale).astype(jnp.bfloat16)


def draw_exit_layer(key, part):
    key = jax.random.fold_in(key, 9)
    key_len, key_pick = jax.random.split(key)
    lengths = jax.random.randint(key_len, (SEQUENCES,), SEQ_LEN // 8, SEQ_LEN + 1, dtype=jnp.int32)
    chosen = jax.random.randint(key_pick, (SEQUENCES // SEQS,), 0, SEQS, dtype=jnp.int32)
    slots = jnp.arange(SEQUENCES, dtype=jnp.int32) % SEQS
    chosen_len = SEQ_LEN - max(1, SEQ_LEN // 64)
    lengths = jnp.where(slots == jnp.repeat(chosen, SEQS), chosen_len, lengths)
    position = jnp.arange(SEQ_LEN, dtype=jnp.int32)[None, :]
    limit = lengths[:, None]
    upper = LAYER + 1 + (limit - position) * (LAYERS - LAYER - 1) // limit
    lower = LAYER - (position - limit) * (LAYER - 1) // SEQ_LEN
    return jnp.where(position < limit, upper, lower).astype(jnp.int32)


def spiked(values, rng, source, target, shards_of, factor):
    owner, partner = [(jnp.arange(values.shape[dim]) // (values.shape[dim] // shards_of)).reshape([-1 if axis == dim else 1 for axis in range(values.ndim)]) for dim in (source, target)]
    chosen = jax.random.permutation(rng, shards_of)[partner]
    strong = (owner == chosen) | (owner == (partner + shards_of // 2) % shards_of)
    return jnp.where(strong, factor * values, values)


def block_scale(stream_key, dims, cuts, least, top_value):
    gain, own = 1.0, jax.random.fold_in(stream_key, 6)
    for dim, shards_of in cuts:
        heights = jnp.exp(jax.random.uniform(jax.random.fold_in(own, dim), (shards_of,), jnp.float32, least / len(cuts), top_value / len(cuts)))
        gain = gain * jnp.repeat(heights, dims[dim] // shards_of).reshape([-1 if axis == dim else 1 for axis in range(len(dims))])
    return gain


def bell_draw(rng, dims, deviation, most, cuts=(), kind=jnp.bfloat16):
    values = jax.random.normal(rng, dims, jnp.float32) * deviation
    if len(cuts) > 0:
        values = block_scale(rng, dims, cuts, -0.22, 0.18) * values
    return jnp.clip(values, min=-most, max=most).astype(kind)


def heavy_noise(stream_key, shape, scale, most, cuts, heavy, kind=jnp.bfloat16):
    entries = scale * jax.random.normal(stream_key, shape, jnp.float32)
    if cuts:
        entries = entries * block_scale(stream_key, shape, cuts, -0.22, 0.18)
    return jnp.clip(spiked(entries, jax.random.fold_in(stream_key, 3), *heavy), -most, most).astype(kind)


def setup_inputs(seed: int = 0) -> dict:
    key_list = jax.random.split(jax.random.key(seed), 19)
    tokens = draw_tokens(jax.random.fold_in(key_list[18], 71), 0)
    exit_layer = draw_exit_layer(jax.random.fold_in(key_list[18], 71), 0)
    first_gain = jnp.clip(1.0 + 0.18 * jax.random.normal(key_list[2], (D,), jnp.float32), 0.099609375, 1.8984375).astype(jnp.bfloat16)
    first_shift = bell_draw(key_list[3], (D,), 0.3, 1.75, ((0, 32),))
    query_weight = bell_draw(key_list[4], (D, D), D ** -0.5, 0.125, ((0, 32),))
    query_bias = bell_draw(key_list[5], (D,), 0.5, 3.0, ((0, 32),))
    key_weight = bell_draw(key_list[6], (D, D), D ** -0.5, 0.125, ((0, 32),))
    value_weight = bell_draw(key_list[7], (D, D), D ** -0.5, 0.125, ((0, 32),))
    value_bias = bell_draw(key_list[8], (D,), 0.5, 3.0, ((0, 32),))
    output_weight = bell_draw(key_list[9], (D, D), (D // 32) ** -0.5, 0.75, ((0, 32),))
    output_bias = bell_draw(key_list[10], (D,), 0.3, 1.75, ((0, 32),))
    second_gain = jnp.clip(1.0 + 0.18 * jax.random.normal(key_list[11], (D,), jnp.float32), 0.099609375, 1.8984375).astype(jnp.bfloat16)
    second_shift = bell_draw(key_list[12], (D,), 0.3, 1.75, ((0, 32),))
    expand_weight = bell_draw(key_list[13], (FF, D), D ** -0.5, 0.125, ((0, 32),))
    expand_bias = bell_draw(key_list[14], (FF,), 0.5, 3.0, ((0, 32),))
    shrink_weight = bell_draw(key_list[15], (D, FF), FF ** -0.5, 0.0625, ((0, 32),))
    shrink_bias = bell_draw(key_list[16], (D,), 0.3, 1.75, ((0, 32),))
    cotangent = heavy_noise(key_list[17], (SEQUENCES, SEQ_LEN, D), 1.0, 8.0, ((0, 8), (1, 4)), (0, 2, 8, 2.0))
    return {"tokens": tokens, "exit_layer": exit_layer, "first_gain": first_gain, "first_shift": first_shift, "query_weight": query_weight, "query_bias": query_bias, "key_weight": key_weight, "value_weight": value_weight, "value_bias": value_bias, "output_weight": output_weight, "output_bias": output_bias, "second_gain": second_gain, "second_shift": second_shift, "expand_weight": expand_weight, "expand_bias": expand_bias, "shrink_weight": shrink_weight, "shrink_bias": shrink_bias, "cotangent": cotangent}


@jax.custom_vjp
def low(v):
    return lax.optimization_barrier(v.astype(jnp.bfloat16)).astype(jnp.float32)

@jax.custom_vjp
def low_back(v):
    return v

def low_keep(v):
    return (low(v), None)

def low_pass(kept, grad):
    return (grad,)

def back_keep(v):
    return (v, None)

def back_low(kept, grad):
    return (low(grad),)
low.defvjp(low_keep, low_pass)
low_back.defvjp(back_keep, back_low)
EPS = 1e-05
HIGH = lax.Precision.HIGHEST

def normalize(values):
    center = values - lax.optimization_barrier(jnp.mean(values, axis=-1, keepdims=True))
    spread = lax.optimization_barrier(jnp.mean(center * center, axis=-1, keepdims=True))
    return center * lax.rsqrt(spread + EPS)

def linear(inputs, weight):
    return jnp.dot(inputs, weight.T, precision=HIGH, preferred_element_type=jnp.float32)

def attend_block(query_rows, first_row, key_rows, value_rows, alive):
    factor = HEAD_DIM ** (-0.5)
    scores = jnp.einsum('qhd,khd->hqk', query_rows, key_rows, precision=HIGH) * factor
    positions = first_row + jnp.arange(query_rows.shape[0], dtype=jnp.int32)
    columns = jnp.arange(key_rows.shape[0], dtype=jnp.int32)
    allowed = (columns[None, :] <= positions[:, None]) & (alive[None, :] > 0.5)
    scores = low_back(jnp.where(allowed[None], scores, jnp.float32(-1e+30)))
    row_max = lax.optimization_barrier(jnp.max(scores, axis=-1, keepdims=True))
    raised = jnp.exp(scores - row_max)
    weights_low = low(raised / lax.optimization_barrier(jnp.sum(raised, axis=-1, keepdims=True)))
    return jnp.einsum('hqk,khd->qhd', weights_low, value_rows, precision=HIGH)

def layer_sequence(params, inputs, alive):
    first_gain, first_shift, query_weight, query_bias, key_weight, value_weight, value_bias, output_weight, output_bias, second_gain, second_shift, expand_weight, expand_bias, shrink_weight, shrink_bias = params
    first_rows = low(normalize(inputs) * first_gain + first_shift)
    queries = low_back(low(linear(first_rows, query_weight) + query_bias))
    key_rows = low_back(low(linear(first_rows, key_weight)))
    value_rows = low_back(low(linear(first_rows, value_weight) + value_bias))
    block_rows = min(512, SEQ_LEN)
    block_total = SEQ_LEN // block_rows
    query_blocks = queries.reshape(block_total, block_rows, HEADS, HEAD_DIM)
    key_heads = key_rows.reshape(SEQ_LEN, HEADS, HEAD_DIM)
    value_heads = value_rows.reshape(SEQ_LEN, HEADS, HEAD_DIM)
    first_rows_list = jnp.arange(block_total, dtype=jnp.int32) * block_rows
    checked = jax.checkpoint(attend_block)
    attended = lax.map(lambda pair: checked(pair[0], pair[1], key_heads, value_heads, alive), (query_blocks, first_rows_list))
    mixed = low_back(low(attended.reshape(SEQ_LEN, D)))
    branch = low_back(linear(mixed, output_weight) + output_bias)
    middle = inputs + alive[:, None] * branch
    second_rows = low(normalize(middle) * second_gain + second_shift)
    hidden_pre = low_back(linear(second_rows, expand_weight) + expand_bias)
    activated = low(jax.nn.gelu(hidden_pre, approximate=False))
    shrunk = low_back(linear(activated, shrink_weight) + shrink_bias)
    return middle + alive[:, None] * shrunk

def whole_layer(inputs_all, params, alive_all):
    per_sequence = jax.checkpoint(layer_sequence)
    return lax.map(lambda pair: per_sequence(params, pair[0], pair[1]), (inputs_all, alive_all))

def reference(tokens, exit_layer, first_gain, first_shift, query_weight, query_bias, key_weight, value_weight, value_bias, output_weight, output_bias, second_gain, second_shift, expand_weight, expand_bias, shrink_weight, shrink_bias, cotangent):
    params = (first_gain.astype(jnp.float32), first_shift.astype(jnp.float32), query_weight.astype(jnp.float32), query_bias.astype(jnp.float32), key_weight.astype(jnp.float32), value_weight.astype(jnp.float32), value_bias.astype(jnp.float32), output_weight.astype(jnp.float32), output_bias.astype(jnp.float32), second_gain.astype(jnp.float32), second_shift.astype(jnp.float32), expand_weight.astype(jnp.float32), expand_bias.astype(jnp.float32), shrink_weight.astype(jnp.float32), shrink_bias.astype(jnp.float32))
    inputs_all = tokens.astype(jnp.float32)
    alive_all = (exit_layer > LAYER).astype(jnp.float32)
    outputs, pullback = jax.vjp(lambda values, weights: whole_layer(values, weights, alive_all), inputs_all, params)
    grad_inputs, grads = pullback(cotangent.astype(jnp.float32))
    return (outputs.astype(jnp.bfloat16), grad_inputs.astype(jnp.bfloat16), grads[0], grads[1], grads[2], grads[3], grads[4], grads[5], grads[6], grads[7], grads[8], grads[9], grads[10], grads[11], grads[12], grads[13], grads[14])
```

```python
import math

import jax
import jax.numpy as jnp
from jax import lax
from jax.experimental import pallas as pl
from jax.experimental.pallas import tpu as pltpu
from jax.sharding import PartitionSpec as P

HEAD_DIM = 64
LAYER = 12


EPS = 1e-05


def normalize(values):
    center = values - jnp.mean(values, axis=-1, keepdims=True)
    spread = jnp.mean(center * center, axis=-1, keepdims=True)
    return center * lax.rsqrt(spread + EPS)


def project(left, weight):
    return lax.dot_general(
        left, weight, (((1,), (1,)), ((), ())), preferred_element_type=jnp.float32
    )


def through(left, weight):
    return jnp.dot(left, weight, preferred_element_type=jnp.float32)


def outer_rows(grad_cols, inputs):
    return lax.dot_general(
        grad_cols, inputs, (((0,), (0,)), ((), ())), preferred_element_type=jnp.float32
    )


def place_cols(buffer, piece):
    return piece.astype(buffer.dtype)


def column_total(matrix):
    return jnp.sum(matrix, axis=0, dtype=jnp.float32)


def swap(values, bit):
    size = lax.axis_size("dp")
    return lax.ppermute(values, "dp", [(i, i ^ bit) for i in range(size)])


CORE, ALONG_X, ALONG_Y = 1, 2, 4


def pick(flag, first, second):
    return jnp.where(flag == 0, first, second)


def ordered(flag, own, other, axis):
    return pick(
        flag, jnp.concatenate([own, other], axis), jnp.concatenate([other, own], axis)
    )


def arrange_kernel(place_ref, own, beside, across, corner, out, sems):
    copies = [
        pltpu.make_async_copy(piece, out.at[place_ref[0] ^ index], sems.at[index])
        for index, piece in enumerate((own, beside, across, corner))
    ]
    for copy in copies:
        copy.start()
    for copy in copies:
        copy.wait()


def arrange(place, pieces):
    shape = pieces[0].shape
    size = 4 * math.prod(shape) * pieces[0].dtype.itemsize
    return pl.pallas_call(
        arrange_kernel,
        out_shape=jax.ShapeDtypeStruct((4,) + shape, pieces[0].dtype),
        in_specs=[pl.BlockSpec(memory_space=pltpu.SMEM)]
        + [pl.BlockSpec(memory_space=pl.ANY)] * 4,
        out_specs=pl.BlockSpec(memory_space=pl.ANY),
        scratch_shapes=[pltpu.SemaphoreType.DMA((4,))],
        cost_estimate=pl.CostEstimate(flops=0, bytes_accessed=2 * size, transcendentals=0),
        name="arrange",
    )(place.reshape(1), *pieces)


def spread(values, place, corner_by):
    beside = swap(values, ALONG_X)
    across = swap(values, ALONG_Y)
    corner = swap(beside, ALONG_Y) if corner_by == ALONG_Y else swap(across, ALONG_X)
    return arrange(place, (values, beside, across, corner))


def total_plane(pieces, corner_by):
    own, beside, across, corner = pieces
    if corner_by == ALONG_Y:
        beside = add_low(beside, swap(corner, ALONG_Y))
    else:
        across = add_low(across, swap(corner, ALONG_X))
    got_x = swap(beside, ALONG_X)
    got_y = swap(across, ALONG_Y)
    return (
        own.astype(jnp.float32) + got_x.astype(jnp.float32) + got_y.astype(jnp.float32)
    ).astype(jnp.bfloat16)


def add_low(left, right):
    return (left.astype(jnp.float32) + right.astype(jnp.float32)).astype(jnp.bfloat16)


BLOCK = 256


def softmax_block(index, keys_wide, query_wide):
    start = index * BLOCK
    tiles = []
    if index > 0:
        tiles.append(
            lax.dot_general(
                keys_wide[:start],
                query_wide,
                (((1,), (1,)), ((), ())),
                preferred_element_type=jnp.float32,
            )
        )
    last = lax.dot_general(
        keys_wide[start : start + BLOCK],
        query_wide,
        (((1,), (1,)), ((), ())),
        preferred_element_type=jnp.float32,
    )
    key_pos = lax.broadcasted_iota(jnp.int32, last.shape, 0)
    query_pos = lax.broadcasted_iota(jnp.int32, last.shape, 1)
    tiles.append(jnp.where(key_pos <= query_pos, last, jnp.float32(-1e30)))
    peak = jnp.max(tiles[-1], axis=0, keepdims=True)
    if index > 0:
        peak = jnp.maximum(peak, jnp.max(tiles[0], axis=0, keepdims=True))
    tiles = [jnp.exp(tile - peak) for tile in tiles]
    total = sum(jnp.sum(tile, axis=0, keepdims=True) for tile in tiles)
    inverse = 1.0 / total
    return [tile * inverse for tile in tiles]


def widen(head, rows_ref, mask_ref):
    first = 3 * HEAD_DIM * head
    query = rows_ref[:, first : first + HEAD_DIM] * jnp.bfloat16(HEAD_DIM**-0.5)
    keys = rows_ref[:, first + HEAD_DIM : first + 2 * HEAD_DIM]
    values = rows_ref[:, first + 2 * HEAD_DIM : first + 3 * HEAD_DIM]
    even = jnp.full(query.shape, 1.0 / HEAD_DIM, jnp.bfloat16)
    query_wide = jnp.concatenate([query, even], axis=1)
    keys_wide = jnp.concatenate([keys, mask_ref[...]], axis=1)
    return query, keys, values, query_wide, keys_wide


def attend_kernel(rows_ref, mask_ref, out_ref):
    blocks = rows_ref.shape[0] // BLOCK
    results = [[], []]
    for head in range(2):
        _, _, values, query_wide, keys_wide = widen(head, rows_ref, mask_ref)
        for index in range(blocks):
            start, stop = index * BLOCK, (index + 1) * BLOCK
            tiles = softmax_block(index, keys_wide, query_wide[start:stop])
            low = jnp.concatenate([tile.astype(jnp.bfloat16) for tile in tiles], axis=0)
            outcome = lax.dot_general(
                values[:stop], low, (((0,), (0,)), ((), ())), preferred_element_type=jnp.float32
            )
            results[head].append(outcome.T)
    for index in range(blocks):
        both = jnp.concatenate([results[0][index], results[1][index]], axis=1)
        out_ref[index * BLOCK : (index + 1) * BLOCK, :] = both.astype(jnp.bfloat16)


def attend_back_kernel(rows_ref, grad_ref, mask_ref, out_ref, key_sum, value_sum):
    blocks = rows_ref.shape[0] // BLOCK
    columns = []
    for head in range(2):
        query, keys, values, query_wide, keys_wide = widen(head, rows_ref, mask_ref)
        grad = grad_ref[:, head * HEAD_DIM : (head + 1) * HEAD_DIM]
        query_parts = []
        for index in reversed(range(blocks)):
            start, stop = index * BLOCK, (index + 1) * BLOCK
            tiles = softmax_block(index, keys_wide, query_wide[start:stop])
            soft = jnp.concatenate(tiles, axis=0)
            grad_rows = grad[start:stop]
            grad_probs = lax.dot_general(
                values[:stop],
                grad_rows,
                (((1,), (1,)), ((), ())),
                preferred_element_type=jnp.float32,
            )
            weighted = soft * grad_probs
            delta = jnp.sum(weighted, axis=0, keepdims=True)
            grad_scores = (weighted - soft * delta).astype(jnp.bfloat16)
            value_term = jnp.dot(
                soft.astype(jnp.bfloat16), grad_rows, preferred_element_type=jnp.float32
            )
            key_term = jnp.dot(
                grad_scores, query[start:stop], preferred_element_type=jnp.float32
            )
            if index == blocks - 1:
                value_sum[...] = value_term
                key_sum[...] = key_term
            else:
                value_sum[:stop, :] += value_term
                key_sum[:stop, :] += key_term
            outcome = lax.dot_general(
                keys[:stop],
                grad_scores,
                (((0,), (0,)), ((), ())),
                preferred_element_type=jnp.float32,
            )
            query_parts.insert(0, outcome.T * jnp.float32(HEAD_DIM**-0.5))
        columns += [jnp.concatenate(query_parts, axis=0), key_sum[...], value_sum[...]]
    out_ref[...] = jnp.concatenate([part.astype(jnp.bfloat16) for part in columns], axis=1)


def attend(rows, mask):
    count, columns = rows.shape
    pairs = columns // (6 * HEAD_DIM)
    work = pairs * 2 * count * count * HEAD_DIM
    return pl.pallas_call(
        attend_kernel,
        grid=(pairs,),
        in_specs=[
            pl.BlockSpec((count, 6 * HEAD_DIM), lambda i: (0, i)),
            pl.BlockSpec((count, HEAD_DIM), lambda i: (0, 0)),
        ],
        out_specs=pl.BlockSpec((count, 2 * HEAD_DIM), lambda i: (0, i)),
        out_shape=jax.ShapeDtypeStruct((count, pairs * 2 * HEAD_DIM), jnp.bfloat16),
        compiler_params=pltpu.CompilerParams(vmem_limit_bytes=48 << 20),
        cost_estimate=pl.CostEstimate(
            flops=16 * work, bytes_accessed=8 * count * columns, transcendentals=0
        ),
        name="attend",
    )(rows, mask)


def attend_back(rows, grad, mask):
    count, columns = rows.shape
    pairs = columns // (6 * HEAD_DIM)
    work = pairs * 2 * count * count * HEAD_DIM
    return pl.pallas_call(
        attend_back_kernel,
        grid=(pairs,),
        in_specs=[
            pl.BlockSpec((count, 6 * HEAD_DIM), lambda i: (0, i)),
            pl.BlockSpec((count, 2 * HEAD_DIM), lambda i: (0, i)),
            pl.BlockSpec((count, HEAD_DIM), lambda i: (0, 0)),
        ],
        out_specs=pl.BlockSpec((count, 6 * HEAD_DIM), lambda i: (0, i)),
        out_shape=jax.ShapeDtypeStruct((count, columns), jnp.bfloat16),
        scratch_shapes=[pltpu.VMEM((count, HEAD_DIM), jnp.float32)] * 2,
        compiler_params=pltpu.CompilerParams(vmem_limit_bytes=48 << 20),
        cost_estimate=pl.CostEstimate(
            flops=40 * work, bytes_accessed=8 * count * columns, transcendentals=0
        ),
        name="attend_back",
    )(rows, grad, mask)


def normal_parts(values):
    center = values - jnp.mean(values, axis=-1, keepdims=True)
    spread_of = jnp.mean(center * center, axis=-1, keepdims=True)
    scale = lax.rsqrt(spread_of + EPS)
    return center * scale, scale


def normal_back(normed, scale, grad):
    mean_grad = jnp.mean(grad, axis=-1, keepdims=True)
    mean_product = jnp.mean(grad * normed, axis=-1, keepdims=True)
    return (grad - mean_grad - normed * mean_product) * scale


def whole_sequence_device(
    tokens,
    exit_layer,
    first_gain,
    first_shift,
    query_weight,
    query_bias,
    key_weight,
    value_weight,
    value_bias,
    output_weight,
    output_bias,
    second_gain,
    second_shift,
    expand_weight,
    expand_bias,
    shrink_weight,
    shrink_bias,
    cotangent,
):
    seq_count, local_len, width = tokens.shape
    heads_rows = query_weight.shape[0]
    hidden_rows = expand_weight.shape[0]
    dp_size, seq_size = lax.axis_size("dp"), lax.axis_size("seq")
    dp, depth = lax.axis_index("dp"), lax.axis_index("seq")
    core, place = dp % 2, dp // 2
    parity = depth % 2
    full_len = local_len * seq_size
    half_len = full_len // 2
    f32, low = jnp.float32, jnp.bfloat16

    def route(flip):
        pairs = []
        for i in range(dp_size):
            for j in range(seq_size):
                target = 2 * (i % 2) + (j % 2 if not flip else 1 - j % 2)
                pairs.append((i * seq_size + j, (i // 2 * 2 + j // 2) * seq_size + target))
        return pairs

    def to_chips(values):
        first = pick(parity, values[0], values[1])
        second = pick(parity, values[1], values[0])
        first = lax.ppermute(first, ("dp", "seq"), route(False))
        second = lax.ppermute(second, ("dp", "seq"), route(True))
        half = ordered(parity, first[None], second[None], 0)
        return ordered(core, half, swap(half, CORE), 0)

    def from_chips(half):
        half = half.reshape(2, local_len, width)
        first = pick(parity, half[0], half[1])
        second = pick(parity, half[1], half[0])
        first = lax.ppermute(first, ("dp", "seq"), [(b, a) for a, b in route(False)])
        second = lax.ppermute(second, ("dp", "seq"), [(b, a) for a, b in route(True)])
        return ordered(parity, first[None], second[None], 0)

    alive = (exit_layer > LAYER).astype(low)
    flag_rows = jnp.broadcast_to(alive[:, None, :], (seq_count, 16, local_len))
    flag_rows = jnp.pad(flag_rows, ((0, 0), (0, 0), (0, width - local_len)))
    arrived = to_chips(jnp.concatenate([tokens, flag_rows], axis=1))
    inputs = arrived[:, :local_len].reshape(full_len, width).astype(f32)
    alive = arrived[:, local_len, :local_len].reshape(full_len, 1)
    active = alive.astype(f32)
    mask = jnp.broadcast_to((alive - 1) * jnp.bfloat16(1e30), (full_len, HEAD_DIM))
    cotangent_full = to_chips(cotangent).reshape(full_len, width)

    vectors = jnp.concatenate(
        [
            first_gain,
            first_shift,
            query_bias,
            value_bias,
            output_bias,
            second_gain,
            second_shift,
            shrink_bias,
            expand_bias,
        ]
    )
    vectors = lax.all_gather(vectors, ("dp", "seq"), axis=0, tiled=True)
    vectors = vectors.reshape(dp_size * seq_size, -1).astype(f32)

    def vector(index):
        return vectors[:, index * heads_rows : (index + 1) * heads_rows].reshape(-1)

    def of_core(matrix):
        cut = matrix.reshape(4, 2, seq_size, -1)
        return lax.dynamic_index_in_dim(cut, core, 1, False).reshape(4 * seq_size, -1)

    gain_one, shift_one = vector(0), vector(1)
    bias_query = of_core(vectors[:, 2 * heads_rows : 3 * heads_rows])
    bias_value = of_core(vectors[:, 3 * heads_rows : 4 * heads_rows])
    bias_rows = jnp.stack([bias_query, jnp.zeros_like(bias_query), bias_value], 1).reshape(-1)
    bias_out, gain_two, shift_two, bias_shrink = vector(4), vector(5), vector(6), vector(7)
    bias_expand = of_core(vectors[:, 8 * heads_rows :]).reshape(-1)

    def through_z(shard):
        return lax.all_gather(shard, "seq", axis=0, tiled=True)

    def core_columns(rows):
        cut = rows.reshape(rows.shape[0], 4, 2, -1)
        mine = lax.dynamic_index_in_dim(cut, core, 2, False).reshape(rows.shape[0], -1)
        theirs = lax.dynamic_index_in_dim(cut, 1 - core, 2, False).reshape(rows.shape[0], -1)
        return ordered(core, mine, swap(theirs, CORE), 0)

    w_qkv = spread(
        through_z(jnp.concatenate([query_weight, key_weight, value_weight], 0)), place, ALONG_X
    ).reshape(-1, width)
    w_out = spread(core_columns(through_z(output_weight)), place, ALONG_Y).reshape(width, -1)
    w_expand = spread(through_z(expand_weight), place, ALONG_X).reshape(-1, width)
    w_shrink = spread(core_columns(through_z(shrink_weight)), place, ALONG_Y).reshape(width, -1)

    normed_in, scale_in = normal_parts(inputs)
    first_rows = (normed_in * gain_one + shift_one).astype(low)
    qkv = (project(first_rows, w_qkv) + bias_rows).astype(low)
    mixed = attend(qkv, mask)

    def both_cores(left, weight, dot):
        parts = []
        for start in (0, half_len):
            own = dot(left[start : start + half_len], weight).astype(low)
            parts.append(own.astype(f32) + swap(own, CORE).astype(f32))
        return jnp.concatenate(parts, 0)

    def half_rows(matrix, which):
        return lax.dynamic_slice_in_dim(matrix, which * half_len, half_len, 0)

    def own_half(left, weight, dot):
        got = swap(dot(half_rows(left, 1 - core), weight).astype(low), CORE)
        return dot(half_rows(left, core), weight) + got.astype(f32)

    branch = both_cores(mixed, w_out, project) + bias_out
    middle = inputs + active * branch
    normed_mid, scale_mid = normal_parts(middle)
    second_rows = (normed_mid * gain_two + shift_two).astype(low)
    hidden_pre = project(second_rows, w_expand) + bias_expand
    lifted = 0.5 * (1.0 + lax.erf(hidden_pre * (0.5**0.5)))
    activated = (hidden_pre * lifted).astype(low)
    slope = lifted + hidden_pre * jnp.exp(-0.5 * hidden_pre * hidden_pre) * ((0.5 / math.pi) ** 0.5)
    slope = slope.astype(low)
    shrunk = own_half(activated, w_shrink, project) + bias_shrink
    out_half = (half_rows(middle, core) + half_rows(active, core) * shrunk).astype(low)
    layer_out = from_chips(out_half)

    def plane_pieces(matrix):
        cut = matrix.reshape(matrix.shape[0], 4, -1)
        return [lax.dynamic_index_in_dim(cut, place ^ d, 1, False) for d in range(4)]

    def z_major(matrix):
        cut = matrix.reshape(matrix.shape[0], 2, seq_size, heads_rows)
        return cut.reshape(matrix.shape[0], -1)

    def rows_total(grad, inputs_low, corner_by):
        pieces = [outer_rows(part, inputs_low).astype(low) for part in plane_pieces(grad)]
        return total_plane(pieces, corner_by)

    def join_cores(total):
        cut = total.reshape(2, -1, total.shape[1])
        mine = lax.dynamic_index_in_dim(cut, core, 0, False)
        theirs = swap(lax.dynamic_index_in_dim(cut, 1 - core, 0, False), CORE)
        mine, theirs = (part.reshape(part.shape[0], 4, 1, -1) for part in (mine, theirs))
        return ordered(core, mine, theirs, 2).reshape(mine.shape[0], -1)

    def scatter_z(total):
        return lax.psum_scatter(total, "seq", scatter_dimension=0, tiled=True).astype(f32)

    grad_out = cotangent_full.astype(f32)
    grad_shrunk = (active * grad_out).astype(low)
    grad_units = through(grad_shrunk, w_shrink)
    grad_pre = (grad_units * slope.astype(f32)).astype(low)
    shrink_weight_grad = scatter_z(join_cores(rows_total(grad_shrunk, activated, ALONG_Y)))
    grad_second = both_cores(grad_pre, w_expand, through)
    expand_weight_grad = scatter_z(rows_total(grad_pre, second_rows, ALONG_X))
    grad_middle = grad_out + normal_back(normed_mid, scale_mid, grad_second * gain_two)
    grad_branch = (active * grad_middle).astype(low)
    grad_mixed = through(grad_branch, w_out).astype(low)
    output_weight_grad = scatter_z(join_cores(rows_total(grad_branch, mixed, ALONG_Y)))
    grad_qkv = attend_back(qkv, grad_mixed, mask)
    qkv_weight_grad = scatter_z(rows_total(grad_qkv, first_rows, ALONG_X))
    grad_first = own_half(grad_qkv, w_qkv, through)
    normed_half, scale_half = half_rows(normed_in, core), half_rows(scale_in, core)
    grad_half = half_rows(grad_middle, core) + normal_back(
        normed_half, scale_half, grad_first * gain_one
    )
    tokens_grad = from_chips(grad_half.astype(low))

    def column_sum(matrix):
        return jnp.sum(matrix.astype(f32), axis=0)

    def all_devices(totals, rows):
        return totals.reshape(dp_size * seq_size, rows)

    def core_devices(totals, rows):
        cut = totals.reshape(4, 1, seq_size, rows)
        return ordered(core, cut, jnp.zeros_like(cut), 1).reshape(dp_size * seq_size, rows)

    qkv_sums = column_sum(grad_qkv).reshape(4 * seq_size, 3, heads_rows)
    sums = jnp.concatenate(
        [
            all_devices(column_sum(grad_first * normed_half), heads_rows),
            all_devices(column_sum(grad_first), heads_rows),
            core_devices(qkv_sums[:, 0], heads_rows),
            core_devices(qkv_sums[:, 2], heads_rows),
            all_devices(0.5 * column_sum(grad_branch), heads_rows),
            all_devices(0.5 * column_sum(grad_second * normed_mid), heads_rows),
            all_devices(0.5 * column_sum(grad_second), heads_rows),
            all_devices(0.5 * column_sum(grad_shrunk), heads_rows),
            core_devices(column_sum(grad_pre), hidden_rows),
        ],
        axis=1,
    )
    sums = lax.psum_scatter(sums.reshape(-1), ("dp", "seq"), scatter_dimension=0, tiled=True)

    def vector_grad(index):
        return sums[index * heads_rows : (index + 1) * heads_rows]

    return (
        layer_out,
        tokens_grad,
        vector_grad(0),
        vector_grad(1),
        qkv_weight_grad[:heads_rows],
        vector_grad(2),
        qkv_weight_grad[heads_rows : 2 * heads_rows],
        qkv_weight_grad[2 * heads_rows :],
        vector_grad(3),
        output_weight_grad,
        vector_grad(4),
        vector_grad(5),
        vector_grad(6),
        expand_weight_grad,
        sums[8 * heads_rows :],
        shrink_weight_grad,
        vector_grad(7),
    )


def general_device(
    tokens,
    exit_layer,
    first_gain,
    first_shift,
    query_weight,
    query_bias,
    key_weight,
    value_weight,
    value_bias,
    output_weight,
    output_bias,
    second_gain,
    second_shift,
    expand_weight,
    expand_bias,
    shrink_weight,
    shrink_bias,
    cotangent,
):
    seq_count, local_len, width = tokens.shape
    hidden_width = shrink_weight.shape[1]
    total_rows = seq_count * local_len
    heads = width // HEAD_DIM
    inputs = tokens.reshape(total_rows, width).astype(jnp.float32)
    active = (exit_layer > LAYER).astype(jnp.float32).reshape(total_rows, 1)
    gain_one, shift_one = (
        lax.all_gather(first_gain, ("dp", "seq"), axis=0, tiled=True),
        lax.all_gather(first_shift, ("dp", "seq"), axis=0, tiled=True),
    )
    gain_one = gain_one.astype(jnp.float32)
    shift_one = shift_one.astype(jnp.float32)
    normed_in = normalize(inputs)
    first_rows = (normed_in * gain_one + shift_one).astype(jnp.bfloat16)
    blank = jnp.zeros((total_rows, width), jnp.bfloat16)
    attention_init = (blank, blank, blank) + ()
    w_query = lax.all_gather(query_weight, ("dp", "seq"), axis=0, tiled=True)
    b_query = lax.all_gather(query_bias, ("dp", "seq"), axis=0, tiled=True)
    w_key = lax.all_gather(key_weight, ("dp", "seq"), axis=0, tiled=True)
    w_value = lax.all_gather(value_weight, ("dp", "seq"), axis=0, tiled=True)
    b_value = lax.all_gather(value_bias, ("dp", "seq"), axis=0, tiled=True)
    queries = place_cols(
        attention_init[0], project(first_rows, w_query) + b_query.astype(jnp.float32)
    )
    key_rows = place_cols(attention_init[1], project(first_rows, w_key))
    value_rows = place_cols(
        attention_init[2], project(first_rows, w_value) + b_value.astype(jnp.float32)
    )
    stored = attention_init[3:]
    gathered = (queries, key_rows, value_rows) + stored
    queries, key_rows, value_rows = (gathered[0], gathered[1], gathered[2])
    query_local = queries.reshape(seq_count, local_len, width)
    key_local = key_rows.reshape(seq_count, local_len, width)
    value_local = value_rows.reshape(seq_count, local_len, width)
    alive_local = active.reshape(seq_count, local_len)
    key_all, value_all, alive_all = (
        lax.all_gather(key_local, "seq", axis=1, tiled=True),
        lax.all_gather(value_local, "seq", axis=1, tiled=True),
        lax.all_gather(alive_local.astype(jnp.bfloat16), "seq", axis=1, tiled=True),
    )
    full_len = key_all.shape[1]
    offset = lax.axis_index("seq") * local_len
    query_pos = offset + jnp.arange(local_len, dtype=jnp.int32)
    key_pos = jnp.arange(full_len, dtype=jnp.int32)
    causal = key_pos[None, :] <= query_pos[:, None]
    allowed = causal[None, None] & (alive_all.astype(jnp.float32)[:, None, None, :] > 0.5)
    factor = HEAD_DIM ** (-0.5)
    group = min(8, heads)
    group_width = group * HEAD_DIM
    group_total = heads // group

    def group_parts(start_col):
        q_part = lax.dynamic_slice_in_dim(query_local, start_col, group_width, 2).reshape(
            seq_count, local_len, group, HEAD_DIM
        )
        k_part = lax.dynamic_slice_in_dim(key_all, start_col, group_width, 2).reshape(
            seq_count, full_len, group, HEAD_DIM
        )
        v_part = lax.dynamic_slice_in_dim(value_all, start_col, group_width, 2).reshape(
            seq_count, full_len, group, HEAD_DIM
        )
        scores = (
            jnp.einsum("sqhd,skhd->shqk", q_part, k_part, preferred_element_type=jnp.float32)
            * factor
        )
        scores = jnp.where(allowed, scores, jnp.float32(-1e30))
        return (q_part, k_part, v_part, scores)

    def forward_group(group_index, state):
        mixed_all, log_total = state
        start_col = group_index * group_width
        q_part, k_part, v_part, scores = group_parts(start_col)
        row_max = jnp.max(scores, axis=-1, keepdims=True)
        raised = jnp.exp(scores - row_max)
        totals = jnp.sum(raised, axis=-1, keepdims=True)
        weights_low = (raised / totals).astype(jnp.bfloat16)
        outcome = jnp.einsum(
            "shqk,skhd->sqhd", weights_low, v_part, preferred_element_type=jnp.float32
        )
        mixed_all = lax.dynamic_update_slice_in_dim(
            mixed_all,
            outcome.reshape(seq_count, local_len, group_width).astype(jnp.bfloat16),
            start_col,
            2,
        )
        log_total = lax.dynamic_update_slice_in_dim(
            log_total, (row_max + jnp.log(totals))[..., 0], group_index * group, 1
        )
        return (mixed_all, log_total)

    mixed_all, log_total = lax.fori_loop(
        0,
        group_total,
        forward_group,
        (
            jnp.zeros((seq_count, local_len, width), jnp.bfloat16),
            jnp.zeros((seq_count, heads, local_len), jnp.float32),
        ),
    )
    mixed = mixed_all.reshape(total_rows, width)
    vector_blank = jnp.zeros((width,), jnp.bfloat16)
    output_init = (jnp.zeros((total_rows, width), jnp.float32), vector_blank, vector_blank) + ()
    w_out = lax.all_gather(output_weight, ("dp", "seq"), axis=0, tiled=True)
    b_out = lax.all_gather(output_bias, ("dp", "seq"), axis=0, tiled=True)
    g_piece = lax.all_gather(second_gain, ("dp", "seq"), axis=0, tiled=True)
    s_piece = lax.all_gather(second_shift, ("dp", "seq"), axis=0, tiled=True)
    branch = place_cols(output_init[0], project(mixed, w_out) + b_out.astype(jnp.float32))
    gain_two = g_piece
    shift_two = s_piece
    stored = output_init[3:]
    folded = (branch, gain_two, shift_two) + stored
    branch = folded[0]
    gain_two = folded[1].astype(jnp.float32)
    shift_two = folded[2].astype(jnp.float32)
    middle = inputs + active * branch
    normed_mid = normalize(middle)
    second_rows = (normed_mid * gain_two + shift_two).astype(jnp.bfloat16)
    expand_init = (jnp.zeros((total_rows, hidden_width), jnp.float32),) + ()
    w_expand = lax.all_gather(expand_weight, ("dp", "seq"), axis=0, tiled=True)
    b_expand = lax.all_gather(expand_bias, ("dp", "seq"), axis=0, tiled=True)
    hidden_pre = place_cols(
        expand_init[0], project(second_rows, w_expand) + b_expand.astype(jnp.float32)
    )
    stored = expand_init[1:]
    expanded = (hidden_pre,) + stored
    hidden_pre = expanded[0]

    def gelu_exact(pre_values):
        return jax.nn.gelu(pre_values, approximate=False)

    activated_full, gelu_back = jax.vjp(gelu_exact, hidden_pre)
    activated = activated_full.astype(jnp.bfloat16)
    shrink_init = (jnp.zeros((total_rows, width), jnp.float32),) + ()
    w_shrink = lax.all_gather(shrink_weight, ("dp", "seq"), axis=0, tiled=True)
    b_shrink = lax.all_gather(shrink_bias, ("dp", "seq"), axis=0, tiled=True)
    shrunk = place_cols(shrink_init[0], project(activated, w_shrink) + b_shrink.astype(jnp.float32))
    stored = shrink_init[1:]
    shrunk_all = (shrunk,) + stored
    shrunk = shrunk_all[0]
    layer_out = (middle + active * shrunk).astype(jnp.bfloat16).reshape(seq_count, local_len, width)
    grad_out = cotangent.reshape(total_rows, width).astype(jnp.float32)
    grad_shrunk = (active * grad_out).astype(jnp.bfloat16)
    grad_units = through(
        grad_shrunk, lax.all_gather(shrink_weight, ("dp", "seq"), axis=0, tiled=True)
    )
    grad_pre = gelu_back(grad_units)[0].astype(jnp.bfloat16)
    grad_second = through(
        grad_pre, lax.all_gather(expand_weight, ("dp", "seq"), axis=0, tiled=True)
    )
    mid_value, mid_back = jax.vjp(normalize, middle)
    grad_middle = grad_out + mid_back(grad_second * gain_two)[0]
    grad_branch = (active * grad_middle).astype(jnp.bfloat16)
    grad_mixed = through(
        grad_branch, lax.all_gather(output_weight, ("dp", "seq"), axis=0, tiled=True)
    )
    grad_mixed_local = grad_mixed.astype(jnp.bfloat16).reshape(seq_count, local_len, width)

    def backward_group(group_index, state):
        grad_query_all, grad_key_all, grad_value_all = state
        start_col = group_index * group_width
        q_part, k_part, v_part, scores = group_parts(start_col)
        g_part = lax.dynamic_slice_in_dim(grad_mixed_local, start_col, group_width, 2).reshape(
            seq_count, local_len, group, HEAD_DIM
        )
        lse_part = lax.dynamic_slice_in_dim(log_total, group_index * group, group, 1)
        soft = jnp.exp(scores - lse_part[..., None])
        grad_probs = jnp.einsum(
            "sqhd,skhd->shqk", g_part, v_part, preferred_element_type=jnp.float32
        )
        value_term = jnp.einsum(
            "shqk,sqhd->skhd", soft.astype(jnp.bfloat16), g_part, preferred_element_type=jnp.float32
        )
        centered = jnp.sum(soft * grad_probs, axis=-1, keepdims=True)
        grad_scores = (soft * (grad_probs - centered)).astype(jnp.bfloat16)
        query_term = (
            jnp.einsum("shqk,skhd->sqhd", grad_scores, k_part, preferred_element_type=jnp.float32)
            * factor
        )
        key_term = (
            jnp.einsum("shqk,sqhd->skhd", grad_scores, q_part, preferred_element_type=jnp.float32)
            * factor
        )
        grad_query_all = lax.dynamic_update_slice_in_dim(
            grad_query_all, query_term.reshape(seq_count, local_len, group_width), start_col, 2
        )
        grad_key_all = lax.dynamic_update_slice_in_dim(
            grad_key_all, key_term.reshape(seq_count, full_len, group_width), start_col, 2
        )
        grad_value_all = lax.dynamic_update_slice_in_dim(
            grad_value_all, value_term.reshape(seq_count, full_len, group_width), start_col, 2
        )
        return (grad_query_all, grad_key_all, grad_value_all)

    grad_query_all, grad_key_all, grad_value_all = lax.fori_loop(
        0,
        group_total,
        backward_group,
        (
            jnp.zeros((seq_count, local_len, width), jnp.float32),
            jnp.zeros((seq_count, full_len, width), jnp.float32),
            jnp.zeros((seq_count, full_len, width), jnp.float32),
        ),
    )
    key_sum, value_sum = (
        lax.psum_scatter(grad_key_all, "seq", scatter_dimension=1, tiled=True),
        lax.psum_scatter(grad_value_all, "seq", scatter_dimension=1, tiled=True),
    )
    grad_query = grad_query_all.astype(jnp.bfloat16).reshape(total_rows, width)
    grad_key = key_sum.astype(jnp.bfloat16).reshape(total_rows, width)
    grad_value = value_sum.astype(jnp.bfloat16).reshape(total_rows, width)
    total = through(grad_query, lax.all_gather(query_weight, ("dp", "seq"), axis=0, tiled=True))
    total = total + through(grad_key, lax.all_gather(key_weight, ("dp", "seq"), axis=0, tiled=True))
    grad_first = total + through(
        grad_value, lax.all_gather(value_weight, ("dp", "seq"), axis=0, tiled=True)
    )
    in_value, in_back = jax.vjp(normalize, inputs)
    tokens_grad = (
        (grad_middle + in_back(grad_first * gain_one)[0])
        .astype(jnp.bfloat16)
        .reshape(seq_count, local_len, width)
    )
    first_scaled = grad_first * normed_in
    second_scaled = grad_second * normed_mid
    vectors = jnp.stack(
        [
            column_total(grad_query),
            column_total(grad_value),
            column_total(grad_branch),
            column_total(grad_shrunk),
            column_total(first_scaled),
            column_total(grad_first),
            column_total(second_scaled),
            column_total(grad_second),
        ],
        axis=1,
    )

    def scattered(grad_cols, inputs):
        return lax.psum_scatter(
            outer_rows(grad_cols, inputs), ("dp", "seq"), scatter_dimension=0, tiled=True
        )

    vector_sums = lax.psum_scatter(vectors, ("dp", "seq"), scatter_dimension=0, tiled=True)
    expand_bias_sums = lax.psum_scatter(
        column_total(grad_pre), ("dp", "seq"), scatter_dimension=0, tiled=True
    )
    shrink_sums = scattered(grad_shrunk, activated)
    grad_pre, second_rows, shrink_sums = lax.optimization_barrier(
        (grad_pre, second_rows, shrink_sums)
    )
    expand_sums = scattered(grad_pre, second_rows)
    grad_branch, grad_query, grad_key, grad_value, expand_sums = lax.optimization_barrier(
        (grad_branch, grad_query, grad_key, grad_value, expand_sums)
    )
    return (
        layer_out,
        tokens_grad,
        vector_sums[:, 4],
        vector_sums[:, 5],
        scattered(grad_query, first_rows),
        vector_sums[:, 0],
        scattered(grad_key, first_rows),
        scattered(grad_value, first_rows),
        vector_sums[:, 1],
        scattered(grad_branch, mixed),
        vector_sums[:, 2],
        vector_sums[:, 6],
        vector_sums[:, 7],
        expand_sums,
        expand_bias_sums,
        shrink_sums,
        vector_sums[:, 3],
    )


def solution(mesh):
    in_specs = (
        P("dp", "seq", None),
        P("dp", "seq"),
        P(("dp", "seq")),
        P(("dp", "seq")),
        P(("dp", "seq"), None),
        P(("dp", "seq")),
        P(("dp", "seq"), None),
        P(("dp", "seq"), None),
        P(("dp", "seq")),
        P(("dp", "seq"), None),
        P(("dp", "seq")),
        P(("dp", "seq")),
        P(("dp", "seq")),
        P(("dp", "seq"), None),
        P(("dp", "seq")),
        P(("dp", "seq"), None),
        P(("dp", "seq")),
        P("dp", "seq", None),
    )
    out_specs = (
        P("dp", "seq", None),
        P("dp", "seq", None),
        P(("dp", "seq")),
        P(("dp", "seq")),
        P(("dp", "seq"), None),
        P(("dp", "seq")),
        P(("dp", "seq"), None),
        P(("dp", "seq"), None),
        P(("dp", "seq")),
        P(("dp", "seq"), None),
        P(("dp", "seq")),
        P(("dp", "seq")),
        P(("dp", "seq")),
        P(("dp", "seq"), None),
        P(("dp", "seq")),
        P(("dp", "seq"), None),
        P(("dp", "seq")),
    )
    def per_device(*arrays):
        tokens, query_weight = arrays[0], arrays[4]
        fits = (
            mesh.shape["dp"] == 8
            and mesh.shape["seq"] == 4
            and tokens.shape[0] == 2
            and query_weight.shape[0] == HEAD_DIM
        )
        return (whole_sequence_device if fits else general_device)(*arrays)

    return jax.shard_map(
        per_device, mesh=mesh, in_specs=in_specs, out_specs=out_specs, check_vma=False
    )
```

```python
import math

import jax
import jax.numpy as jnp
from jax import lax
from jax.experimental import pallas as pl
from jax.experimental.pallas import tpu as pltpu
from jax.sharding import PartitionSpec as P

HEAD_DIM = 64
LAYER = 12


EPS = 1e-05


def normalize(values):
    center = values - jnp.mean(values, axis=-1, keepdims=True)
    spread = jnp.mean(center * center, axis=-1, keepdims=True)
    return center * lax.rsqrt(spread + EPS)


def project(left, weight):
    return lax.dot_general(
        left, weight, (((1,), (1,)), ((), ())), preferred_element_type=jnp.float32
    )


def through(left, weight):
    return jnp.dot(left, weight, preferred_element_type=jnp.float32)


def outer_rows(grad_cols, inputs):
    return lax.dot_general(
        grad_cols, inputs, (((0,), (0,)), ((), ())), preferred_element_type=jnp.float32
    )


def place_cols(buffer, piece):
    return piece.astype(buffer.dtype)


def column_total(matrix):
    return jnp.sum(matrix, axis=0, dtype=jnp.float32)


def swap(values, bit):
    size = lax.axis_size("dp")
    return lax.ppermute(values, "dp", [(i, i ^ bit) for i in range(size)])


CORE, ALONG_X, ALONG_Y = 1, 2, 4


def pick(flag, first, second):
    return jnp.where(flag == 0, first, second)


def ordered(flag, own, other, axis):
    return pick(
        flag, jnp.concatenate([own, other], axis), jnp.concatenate([other, own], axis)
    )


def arrange(pieces, block, sources, targets):
    count = len(pieces)
    steps = len(sources)
    table = jnp.stack([jnp.asarray(target, jnp.int32) for target in targets])

    def kernel(table_ref, *refs):
        step = pl.program_id(0)
        for index in range(count):
            mine = [at for at, source in enumerate(sources) if source[0] == index]

            @pl.when((step >= mine[0]) & (step <= mine[-1]))
            def _():
                refs[count][...] = refs[index][...]

    def place_of(index):
        mine = [at for at, source in enumerate(sources) if source[0] == index]

        def block_of(step, table_ref):
            row, column = sources[mine[0]][1:]
            for at in mine[1:]:
                row = jnp.where(step >= at, sources[at][1], row)
                column = jnp.where(step >= at, sources[at][2], column)
            return row, column

        return block_of

    total = steps * block[0] * block[1]
    return pl.pallas_call(
        kernel,
        grid_spec=pltpu.PrefetchScalarGridSpec(
            num_scalar_prefetch=1,
            grid=(steps,),
            in_specs=[pl.BlockSpec(block, place_of(index)) for index in range(count)],
            out_specs=pl.BlockSpec(block, lambda step, table_ref: (table_ref[step], 0)),
        ),
        out_shape=jax.ShapeDtypeStruct((steps * block[0], block[1]), pieces[0].dtype),
        compiler_params=pltpu.CompilerParams(vmem_limit_bytes=48 << 20),
        cost_estimate=pl.CostEstimate(flops=0, bytes_accessed=4 * total, transcendentals=0),
        name="arrange",
    )(table, *pieces)


def split_kernel(table_ref, first, second, first_out, second_out):
    first_out[...] = first[...]
    second_out[...] = second[...]


def split_columns(core, matrix, block):
    rows, columns = matrix.shape
    count = columns // block // 2
    piece = jax.ShapeDtypeStruct((rows, columns // 2), matrix.dtype)
    return pl.pallas_call(
        split_kernel,
        grid_spec=pltpu.PrefetchScalarGridSpec(
            num_scalar_prefetch=1,
            grid=(count,),
            in_specs=[
                pl.BlockSpec((rows, block), lambda i, core_ref: (0, 2 * i + core_ref[0])),
                pl.BlockSpec((rows, block), lambda i, core_ref: (0, 2 * i + 1 - core_ref[0])),
            ],
            out_specs=[pl.BlockSpec((rows, block), lambda i, core_ref: (0, i))] * 2,
        ),
        out_shape=(piece, piece),
        cost_estimate=pl.CostEstimate(
            flops=0, bytes_accessed=4 * rows * columns, transcendentals=0
        ),
        name="split_columns",
    )(core.reshape(1), matrix, matrix)


def weave_kernel(core_ref, mine, theirs, out):
    block = mine.shape[1]

    @pl.when(core_ref[0] == 0)
    def _():
        out[:, :block] = mine[...]
        out[:, block:] = theirs[...]

    @pl.when(core_ref[0] == 1)
    def _():
        out[:, :block] = theirs[...]
        out[:, block:] = mine[...]


def weave_columns(core, mine, theirs, block):
    rows, columns = mine.shape
    return pl.pallas_call(
        weave_kernel,
        grid_spec=pltpu.PrefetchScalarGridSpec(
            num_scalar_prefetch=1,
            grid=(columns // block,),
            in_specs=[pl.BlockSpec((rows, block), lambda i, core_ref: (0, i))] * 2,
            out_specs=pl.BlockSpec((rows, 2 * block), lambda i, core_ref: (0, i)),
        ),
        out_shape=jax.ShapeDtypeStruct((rows, 2 * columns), mine.dtype),
        cost_estimate=pl.CostEstimate(
            flops=0, bytes_accessed=8 * rows * columns, transcendentals=0
        ),
        name="weave_columns",
    )(core.reshape(1), mine, theirs)


def outer_rows_of(index, lefts, rights, rows, tile=512, table=None):
    count, columns = rights[0].shape
    terms = len(lefts)
    scalars = [jnp.asarray(index, jnp.int32).reshape(1)]
    if table is not None:
        scalars.append(jnp.stack([jnp.asarray(target, jnp.int32) for target in table]))

    def kernel(*refs):
        operands = refs[len(scalars) :]
        total = 0.0
        for left, right in zip(operands[:terms], operands[terms : 2 * terms]):
            total = total + lax.dot_general(
                left[...], right[...], (((0,), (0,)), ((), ())), preferred_element_type=jnp.float32
            )
        total = total.astype(jnp.bfloat16)
        out = operands[-1]
        if table is None:
            out[...] = total
        else:
            for at in range(len(table)):
                start = pl.multiple_of(refs[1][at] * HEAD_DIM, HEAD_DIM)
                out[pl.ds(start, HEAD_DIM), :] = total[at * HEAD_DIM : (at + 1) * HEAD_DIM]

    return pl.pallas_call(
        kernel,
        grid_spec=pltpu.PrefetchScalarGridSpec(
            num_scalar_prefetch=len(scalars),
            grid=(columns // tile,),
            in_specs=[pl.BlockSpec((count, rows), lambda i, ref, *_: (0, ref[0]))] * terms
            + [pl.BlockSpec((count, tile), lambda i, *_: (0, i))] * terms,
            out_specs=pl.BlockSpec((rows, tile), lambda i, *_: (0, i)),
        ),
        out_shape=jax.ShapeDtypeStruct((rows, columns), jnp.bfloat16),
        compiler_params=pltpu.CompilerParams(vmem_limit_bytes=48 << 20),
        cost_estimate=pl.CostEstimate(
            flops=2 * terms * count * rows * columns,
            bytes_accessed=2 * (terms * count * (rows + columns) + rows * columns),
            transcendentals=0,
        ),
        name="outer_rows_of",
    )(*scalars, *lefts, *rights)


def outer_sides(indices, left, right, rows):
    count, columns = right.shape
    pieces = len(indices) // 2
    table = jnp.stack([jnp.asarray(index, jnp.int32) for index in indices])

    def kernel(table_ref, left, right, *outs):
        step = pl.program_id(0)
        total = lax.dot_general(
            left[...], right[...], (((0,), (0,)), ((), ())), preferred_element_type=jnp.float32
        ).astype(jnp.bfloat16)
        for piece, out in enumerate(outs):

            @pl.when(step // 2 == piece)
            def _():
                out[...] = total

    def side_of(piece):
        return lambda step, table_ref: (0, jnp.clip(step - 2 * piece, 0, 1))

    return pl.pallas_call(
        kernel,
        grid_spec=pltpu.PrefetchScalarGridSpec(
            num_scalar_prefetch=1,
            grid=(2 * pieces,),
            in_specs=[
                pl.BlockSpec((count, rows), lambda step, table_ref: (0, table_ref[step])),
                pl.BlockSpec((count, columns), lambda step, table_ref: (0, 0)),
            ],
            out_specs=[pl.BlockSpec((rows, columns), side_of(piece)) for piece in range(pieces)],
        ),
        out_shape=[jax.ShapeDtypeStruct((rows, 2 * columns), jnp.bfloat16)] * pieces,
        compiler_params=pltpu.CompilerParams(vmem_limit_bytes=48 << 20),
        cost_estimate=pl.CostEstimate(
            flops=4 * pieces * count * rows * columns,
            bytes_accessed=4 * count * (pieces * rows + columns),
            transcendentals=0,
        ),
        name="outer_sides",
    )(table, left, right)


def exchange(values):
    half = values.shape[0] // 2
    beside = swap(values, ALONG_X)
    across = swap(values, ALONG_Y)
    upper = swap(beside[:half], ALONG_Y)
    lower = swap(across[half:], ALONG_X)
    return [values, beside, across, upper, lower]


def total_plane(pieces, wait):
    own, beside, across, corner = pieces
    half = own.shape[0] // 2
    upper = swap(corner[:half], ALONG_Y)
    lower = swap(corner[half:], ALONG_X)
    beside = lax.dynamic_update_slice(beside, add_low(beside[:half], upper), (0, 0))
    across = lax.dynamic_update_slice(across, add_low(across[half:], lower), (half, 0))
    got_x = swap(beside, ALONG_X)
    got_y = swap(across, ALONG_Y)
    if wait is not None:
        own = after(own, wait)
    return (
        own.astype(jnp.float32) + got_x.astype(jnp.float32) + got_y.astype(jnp.float32)
    ).astype(jnp.bfloat16)


def add_low(left, right):
    return (left.astype(jnp.float32) + right.astype(jnp.float32)).astype(jnp.bfloat16)


BLOCK = 256


def softmax_block(index, keys_wide, query_wide):
    start = index * BLOCK
    tiles = []
    if index > 0:
        tiles.append(
            lax.dot_general(
                keys_wide[:start],
                query_wide,
                (((1,), (1,)), ((), ())),
                preferred_element_type=jnp.float32,
            )
        )
    last = lax.dot_general(
        keys_wide[start : start + BLOCK],
        query_wide,
        (((1,), (1,)), ((), ())),
        preferred_element_type=jnp.float32,
    )
    key_pos = lax.broadcasted_iota(jnp.int32, last.shape, 0)
    query_pos = lax.broadcasted_iota(jnp.int32, last.shape, 1)
    tiles.append(jnp.where(key_pos <= query_pos, last, jnp.float32(-1e30)))
    peak = jnp.max(tiles[-1], axis=0, keepdims=True)
    if index > 0:
        peak = jnp.maximum(peak, jnp.max(tiles[0], axis=0, keepdims=True))
    tiles = [jnp.exp(tile - peak) for tile in tiles]
    total = sum(jnp.sum(tile, axis=0, keepdims=True) for tile in tiles)
    inverse = 1.0 / total
    return [tile * inverse for tile in tiles]


def widen(head, rows_ref, mask_ref):
    first = 3 * HEAD_DIM * head
    query = rows_ref[:, first : first + HEAD_DIM] * jnp.bfloat16(HEAD_DIM**-0.5)
    keys = rows_ref[:, first + HEAD_DIM : first + 2 * HEAD_DIM]
    values = rows_ref[:, first + 2 * HEAD_DIM : first + 3 * HEAD_DIM]
    even = jnp.full(query.shape, 1.0 / HEAD_DIM, jnp.bfloat16)
    query_wide = jnp.concatenate([query, even], axis=1)
    keys_wide = jnp.concatenate([keys, mask_ref[...]], axis=1)
    return query, keys, values, query_wide, keys_wide


def attend_kernel(rows_ref, mask_ref, out_ref):
    blocks = rows_ref.shape[0] // BLOCK
    results = [[], []]
    for head in range(2):
        _, _, values, query_wide, keys_wide = widen(head, rows_ref, mask_ref)
        for index in range(blocks):
            start, stop = index * BLOCK, (index + 1) * BLOCK
            tiles = softmax_block(index, keys_wide, query_wide[start:stop])
            low = jnp.concatenate([tile.astype(jnp.bfloat16) for tile in tiles], axis=0)
            outcome = lax.dot_general(
                values[:stop], low, (((0,), (0,)), ((), ())), preferred_element_type=jnp.float32
            )
            results[head].append(outcome.T)
    for index in range(blocks):
        both = jnp.concatenate([results[0][index], results[1][index]], axis=1)
        out_ref[index * BLOCK : (index + 1) * BLOCK, :] = both.astype(jnp.bfloat16)


def attend_back_kernel(rows_ref, grad_ref, mask_ref, out_ref, key_sum, value_sum):
    blocks = rows_ref.shape[0] // BLOCK
    columns = []
    for head in range(2):
        query, keys, values, query_wide, keys_wide = widen(head, rows_ref, mask_ref)
        grad = grad_ref[:, head * HEAD_DIM : (head + 1) * HEAD_DIM]
        query_parts = []
        for index in reversed(range(blocks)):
            start, stop = index * BLOCK, (index + 1) * BLOCK
            tiles = softmax_block(index, keys_wide, query_wide[start:stop])
            soft = jnp.concatenate(tiles, axis=0)
            grad_rows = grad[start:stop]
            grad_probs = lax.dot_general(
                values[:stop],
                grad_rows,
                (((1,), (1,)), ((), ())),
                preferred_element_type=jnp.float32,
            )
            weighted = soft * grad_probs
            delta = jnp.sum(weighted, axis=0, keepdims=True)
            grad_scores = (weighted - soft * delta).astype(jnp.bfloat16)
            value_term = jnp.dot(
                soft.astype(jnp.bfloat16), grad_rows, preferred_element_type=jnp.float32
            )
            key_term = jnp.dot(
                grad_scores, query[start:stop], preferred_element_type=jnp.float32
            )
            if index == blocks - 1:
                value_sum[...] = value_term
                key_sum[...] = key_term
            else:
                value_sum[:stop, :] += value_term
                key_sum[:stop, :] += key_term
            outcome = lax.dot_general(
                keys[:stop],
                grad_scores,
                (((0,), (0,)), ((), ())),
                preferred_element_type=jnp.float32,
            )
            query_parts.insert(0, outcome.T * jnp.float32(HEAD_DIM**-0.5))
        columns += [jnp.concatenate(query_parts, axis=0), key_sum[...], value_sum[...]]
    out_ref[...] = jnp.concatenate([part.astype(jnp.bfloat16) for part in columns], axis=1)


def attend(rows, mask):
    count, columns = rows.shape
    pairs = columns // (6 * HEAD_DIM)
    work = pairs * 2 * count * count * HEAD_DIM
    return pl.pallas_call(
        attend_kernel,
        grid=(pairs,),
        in_specs=[
            pl.BlockSpec((count, 6 * HEAD_DIM), lambda i: (0, i)),
            pl.BlockSpec((count, HEAD_DIM), lambda i: (0, 0)),
        ],
        out_specs=pl.BlockSpec((count, 2 * HEAD_DIM), lambda i: (0, i)),
        out_shape=jax.ShapeDtypeStruct((count, pairs * 2 * HEAD_DIM), jnp.bfloat16),
        compiler_params=pltpu.CompilerParams(vmem_limit_bytes=48 << 20),
        cost_estimate=pl.CostEstimate(
            flops=16 * work, bytes_accessed=8 * count * columns, transcendentals=0
        ),
        name="attend",
    )(rows, mask)


def attend_back(rows, grad, mask):
    count, columns = rows.shape
    pairs = columns // (6 * HEAD_DIM)
    work = pairs * 2 * count * count * HEAD_DIM
    return pl.pallas_call(
        attend_back_kernel,
        grid=(pairs,),
        in_specs=[
            pl.BlockSpec((count, 6 * HEAD_DIM), lambda i: (0, i)),
            pl.BlockSpec((count, 2 * HEAD_DIM), lambda i: (0, i)),
            pl.BlockSpec((count, HEAD_DIM), lambda i: (0, 0)),
        ],
        out_specs=pl.BlockSpec((count, 6 * HEAD_DIM), lambda i: (0, i)),
        out_shape=jax.ShapeDtypeStruct((count, columns), jnp.bfloat16),
        scratch_shapes=[pltpu.VMEM((count, HEAD_DIM), jnp.float32)] * 2,
        compiler_params=pltpu.CompilerParams(vmem_limit_bytes=48 << 20),
        cost_estimate=pl.CostEstimate(
            flops=40 * work, bytes_accessed=8 * count * columns, transcendentals=0
        ),
        name="attend_back",
    )(rows, grad, mask)


ROWS = 128


def normal_parts(values):
    center = values - jnp.mean(values, axis=-1, keepdims=True)
    spread_of = jnp.mean(center * center, axis=-1, keepdims=True)
    scale = lax.rsqrt(spread_of + EPS)
    return center * scale, scale


def normal_back(normed, scale, grad):
    mean_grad = jnp.mean(grad, axis=-1, keepdims=True)
    mean_product = jnp.mean(grad * normed, axis=-1, keepdims=True)
    return (grad - mean_grad - normed * mean_product) * scale


def first_kernel(start_ref, tokens, gain, shift, out):
    normed, _ = normal_parts(tokens[...].astype(jnp.float32))
    out[...] = (normed * gain[...] + shift[...]).astype(out.dtype)


def middle_kernel(
    start_ref, tokens, own, got, active, bias, gain, shift, middle_out, rows_out
):
    branch = own[...].astype(jnp.float32) + got[...].astype(jnp.float32) + bias[...]
    middle = tokens[...].astype(jnp.float32) + active[...] * branch
    middle_out[...] = middle
    normed, _ = normal_parts(middle)
    rows_out[...] = (normed * gain[...] + shift[...]).astype(rows_out.dtype)


def add_totals(totals, parts):
    first = pl.program_id(0) == 0
    for index, part in enumerate(parts):
        total = jnp.sum(part, axis=0, keepdims=True)
        totals[index : index + 1, :] = total + jnp.where(
            first, 0.0, totals[index : index + 1, :]
        )


def middle_back_kernel(
    start_ref, cotangent, middle, own, got, peer, active, gain, grad_out, branch_out, totals
):
    grad_second = own[...] + got[...].astype(jnp.float32) + peer[...].astype(jnp.float32)
    normed, scale = normal_parts(middle[...])
    grad_middle = cotangent[...].astype(jnp.float32) + normal_back(
        normed, scale, grad_second * gain[...]
    )
    grad_out[...] = grad_middle
    grad_branch = (active[...] * grad_middle).astype(jnp.bfloat16)
    branch_out[...] = grad_branch
    add_totals(
        totals, (grad_second * normed, grad_second, grad_branch.astype(jnp.float32))
    )


def first_back_kernel(start_ref, tokens, grad_middle, own, got, gain, grad_out, totals):
    grad_first = own[...] + got[...].astype(jnp.float32)
    normed, scale = normal_parts(tokens[...].astype(jnp.float32))
    grad = grad_middle[...] + normal_back(normed, scale, grad_first * gain[...])
    grad_out[...] = grad.astype(grad_out.dtype)
    add_totals(totals, (grad_first * normed, grad_first))


def by_rows(kernel, start, count, arrays, outs, name):
    width = arrays[0][0].shape[1]
    specs = {
        "rows": pl.BlockSpec((ROWS, width), lambda i, start_ref: (i, 0)),
        "from": pl.BlockSpec((ROWS, width), lambda i, start_ref: (start_ref[0] + i, 0)),
        "vector": pl.BlockSpec((1, width), lambda i, start_ref: (0, 0)),
        "totals": pl.BlockSpec((8, width), lambda i, start_ref: (0, 0)),
        "flag": pl.BlockSpec((ROWS, 1), lambda i, start_ref: (i, 0)),
        "flag from": pl.BlockSpec((ROWS, 1), lambda i, start_ref: (start_ref[0] + i, 0)),
    }
    shapes = [
        jax.ShapeDtypeStruct((8 if kind == "totals" else count, width), dtype)
        for kind, dtype in outs
    ]
    moved = sum(
        count * width * array.dtype.itemsize for array, kind in arrays if kind in ("rows", "from")
    ) + sum(math.prod(shape.shape) * shape.dtype.itemsize for shape in shapes)
    return pl.pallas_call(
        kernel,
        grid_spec=pltpu.PrefetchScalarGridSpec(
            num_scalar_prefetch=1,
            grid=(count // ROWS,),
            in_specs=[specs[kind] for _, kind in arrays],
            out_specs=[specs[kind] for kind, _ in outs],
        ),
        out_shape=shapes,
        compiler_params=pltpu.CompilerParams(vmem_limit_bytes=48 << 20),
        cost_estimate=pl.CostEstimate(
            flops=20 * count * width, bytes_accessed=moved, transcendentals=0
        ),
        name=name,
    )(start, *[array for array, _ in arrays])


def after(value, *others):
    return lax.optimization_barrier((value, others))[0]


def whole_sequence_device(
    tokens,
    exit_layer,
    first_gain,
    first_shift,
    query_weight,
    query_bias,
    key_weight,
    value_weight,
    value_bias,
    output_weight,
    output_bias,
    second_gain,
    second_shift,
    expand_weight,
    expand_bias,
    shrink_weight,
    shrink_bias,
    cotangent,
):
    seq_count, local_len, width = tokens.shape
    heads_rows = query_weight.shape[0]
    hidden_rows = expand_weight.shape[0]
    dp_size, seq_size = lax.axis_size("dp"), lax.axis_size("seq")
    dp, depth = lax.axis_index("dp"), lax.axis_index("seq")
    core, place = dp % 2, dp // 2
    along_x, along_y = place % 2, place // 2
    parity = depth % 2
    full_len = local_len * seq_size
    half_len = full_len // 2
    f32, low = jnp.float32, jnp.bfloat16

    def route(flip):
        pairs = []
        for i in range(dp_size):
            for j in range(seq_size):
                target = 2 * (i % 2) + (j % 2 if not flip else 1 - j % 2)
                pairs.append((i * seq_size + j, (i // 2 * 2 + j // 2) * seq_size + target))
        return pairs

    def to_chips(values):
        first = pick(parity, values[0], values[1])
        second = pick(parity, values[1], values[0])
        first = lax.ppermute(first, ("dp", "seq"), route(False))
        second = lax.ppermute(second, ("dp", "seq"), route(True))
        half = ordered(parity, first[None], second[None], 0)
        return ordered(core, half, swap(half, CORE), 0)

    def from_chips(half):
        half = half.reshape(2, local_len, width)
        first = pick(parity, half[0], half[1])
        second = pick(parity, half[1], half[0])
        first = lax.ppermute(first, ("dp", "seq"), [(b, a) for a, b in route(False)])
        second = lax.ppermute(second, ("dp", "seq"), [(b, a) for a, b in route(True)])
        return ordered(parity, first[None], second[None], 0)

    alive = (exit_layer > LAYER).astype(low)
    flag_rows = jnp.broadcast_to(alive[:, None, :], (seq_count, 16, local_len))
    flag_rows = jnp.pad(flag_rows, ((0, 0), (0, 0), (0, width - local_len)))

    devices = dp_size * seq_size
    all_dp = jnp.arange(dp_size, dtype=jnp.int32)[:, None]
    all_seq = jnp.arange(seq_size, dtype=jnp.int32)[None, :]
    relative = ((all_dp ^ dp) * seq_size + (depth - all_seq) % seq_size).reshape(-1)

    def shift_z(values, steps):
        return lax.ppermute(
            values, "seq", [(i, (i + steps) % seq_size) for i in range(seq_size)]
        )

    vectors = jnp.concatenate(
        [
            first_gain,
            first_shift,
            query_bias,
            value_bias,
            output_bias,
            second_gain,
            second_shift,
            shrink_bias,
            expand_bias,
        ]
    )[None]
    for bit in (CORE, ALONG_X, ALONG_Y):
        vectors = jnp.concatenate([vectors, swap(vectors, bit)], 0)
    vectors = jnp.stack(
        [vectors] + [shift_z(vectors, steps) for steps in range(1, seq_size)], 1
    )
    vectors = vectors.reshape(devices, -1)[relative].astype(f32)

    def vector(index):
        return vectors[:, index * heads_rows : (index + 1) * heads_rows].reshape(1, -1)

    def of_core(matrix):
        cut = matrix.reshape(4, 2, seq_size, -1)
        return lax.dynamic_index_in_dim(cut, core, 1, False).reshape(4 * seq_size, -1)

    gain_one, shift_one = vector(0), vector(1)
    bias_query = of_core(vectors[:, 2 * heads_rows : 3 * heads_rows])
    bias_value = of_core(vectors[:, 3 * heads_rows : 4 * heads_rows])
    bias_rows = jnp.stack([bias_query, jnp.zeros_like(bias_query), bias_value], 1).reshape(-1)
    bias_out, gain_two, shift_two, bias_shrink = vector(4), vector(5), vector(6), vector(7)
    def of_quarter(matrix):
        cut = matrix.reshape(2, 4, seq_size, -1)
        return lax.dynamic_index_in_dim(cut, 2 * along_x + core, 1, False)

    bias_expand = of_quarter(vectors[:, 8 * heads_rows :]).reshape(-1)

    def through_z(shard):
        return lax.all_gather(shard, "seq", axis=0, tiled=True)

    places = [place ^ d for d in range(4)]
    sides = [core, 1 - core]
    depth_rows = heads_rows * seq_size
    hidden_block = hidden_rows * seq_size

    z_qkv = through_z(jnp.concatenate([query_weight, key_weight, value_weight], 0))

    mine, theirs = split_columns(core, shrink_weight, hidden_block)
    shard_shrink = jnp.concatenate([mine, swap(theirs, CORE)], 0)
    mine, theirs = split_columns(along_x, shard_shrink, hidden_block)
    shard_shrink = jnp.concatenate([mine, swap(theirs, ALONG_X)], 0)

    z_out = through_z(after(output_weight, z_qkv))
    z_expand = through_z(after(expand_weight, z_out))
    z_shrink = through_z(after(shard_shrink, z_expand))

    arrived = to_chips(after(jnp.concatenate([tokens, flag_rows], axis=1), z_qkv))
    inputs = arrived[:, :local_len].reshape(full_len, width)
    alive = arrived[:, local_len, :local_len].reshape(full_len, 1)
    active = alive.astype(f32)
    mask = jnp.broadcast_to((alive - 1) * jnp.bfloat16(1e30), (full_len, HEAD_DIM))

    pieces_qkv = exchange(after(z_qkv, vectors, shard_shrink))
    mine, theirs = split_columns(core, z_out, depth_rows)
    rows_out = jnp.concatenate([mine, swap(theirs, CORE)], 1)
    pieces_out = exchange(after(rows_out, pieces_qkv))
    across_expand = swap(after(z_expand, pieces_out), ALONG_Y)
    across_shrink = swap(after(z_shrink, across_expand), ALONG_Y)
    cotangent_full = to_chips(after(cotangent, z_expand)).reshape(full_len, width)

    half_qkv = 3 * depth_rows // 2
    w_qkv = arrange(
        pieces_qkv,
        (half_qkv, width),
        [(p, r, 0) for p in range(3) for r in range(2)] + [(3, 0, 0), (4, 0, 0)],
        [2 * places[d] + r for d in range(4) for r in range(2)],
    )
    half_out = depth_rows // 2
    w_out = arrange(
        pieces_out,
        (half_out, width // 2),
        [(p, r, i) for p in range(3) for r in range(2) for i in range(2)]
        + [(p, 0, i) for p in (3, 4) for i in range(2)],
        [2 * (2 * places[d] + sides[i]) + r for d in range(4) for r in range(2) for i in range(2)],
    )
    w_expand = arrange(
        [z_expand, across_expand],
        (hidden_block // 2, width),
        [(p, r, 0) for p in range(2) for r in range(2)],
        [2 * (along_y ^ p) + r for p in range(2) for r in range(2)],
    )
    w_shrink = arrange(
        [z_shrink, across_shrink],
        (heads_rows, 2 * hidden_block),
        [(p, (4 * j + 2 * s + t), 0) for p in range(2) for j in range(seq_size) for s in range(2) for t in range(2)],
        [
            ((2 * (along_y ^ p) + (along_x ^ s)) * 2 + (core ^ t)) * seq_size + j
            for p in range(2)
            for j in range(seq_size)
            for s in range(2)
            for t in range(2)
        ],
    )

    no_start = jnp.zeros((1,), jnp.int32)
    half_start = (core * (half_len // ROWS)).reshape(1)

    def half_rows(matrix, which):
        return lax.dynamic_slice_in_dim(matrix, which * half_len, half_len, 0)

    def own_half(left, weight, dot):
        got = swap(dot(half_rows(left, 1 - core), weight).astype(low), CORE)
        return dot(half_rows(left, core), weight), got

    def of_peer(matrix):
        got = swap(half_rows(matrix, core), ALONG_X)
        return ordered(core, got, swap(got, CORE), 0)

    (first_rows,) = by_rows(
        first_kernel,
        no_start,
        full_len,
        [(inputs, "rows"), (gain_one, "vector"), (shift_one, "vector")],
        [("rows", low)],
        "first_norm",
    )
    qkv = (project(first_rows, w_qkv) + bias_rows).astype(low)
    mixed = attend(qkv, mask)
    branch = project(mixed, w_out).astype(low)
    middle, second_rows = by_rows(
        middle_kernel,
        no_start,
        full_len,
        [
            (inputs, "rows"),
            (branch, "rows"),
            (swap(branch, CORE), "rows"),
            (active, "flag"),
            (bias_out, "vector"),
            (gain_two, "vector"),
            (shift_two, "vector"),
        ],
        [("rows", f32), ("rows", low)],
        "middle_norm",
    )
    second_peer = of_peer(second_rows)
    grad_shrunk = (active * cotangent_full.astype(f32)).astype(low)
    grad_shrunk_peer = of_peer(grad_shrunk)

    def lift(rows):
        hidden_pre = project(rows, w_expand) + bias_expand
        lifted = 0.5 * (1.0 + lax.erf(hidden_pre * (0.5**0.5)))
        bell = jnp.exp(-0.5 * hidden_pre * hidden_pre) * ((0.5 / math.pi) ** 0.5)
        return (hidden_pre * lifted).astype(low), (lifted + hidden_pre * bell).astype(low)

    activated, slope = lift(second_rows)
    activated_peer, slope_peer = lift(second_peer)

    def scatter_z(total):
        return lax.psum_scatter(total, "seq", scatter_dimension=0, tiled=True)

    z_first = [
        (j * 2 + (along_x ^ s)) * 2 + (core ^ t)
        for s in range(2)
        for t in range(2)
        for j in range(seq_size)
    ]
    shrink_parts = [
        outer_rows_of(
            along_y ^ d,
            (grad_shrunk, grad_shrunk_peer),
            (activated, activated_peer),
            4 * depth_rows,
            table=z_first,
        )
        for d in (1, 0)
    ]
    shrink_got = swap(after(shrink_parts[0], across_shrink), ALONG_Y)

    grad_units_peer = through(after(grad_shrunk_peer, shrink_parts[0]), w_shrink)
    grad_pre_peer = (grad_units_peer * slope_peer.astype(f32)).astype(low)
    grad_units = through(after(grad_shrunk, grad_pre_peer), w_shrink)
    grad_pre = (grad_units * slope.astype(f32)).astype(low)

    peer_half, peer_got = own_half(grad_pre_peer, w_expand, through)
    peer_half = (peer_half + peer_got.astype(f32)).astype(low)
    second_from_peer = swap(peer_half, ALONG_X)
    second_half, second_got = own_half(after(grad_pre, peer_half), w_expand, through)
    expand_parts = [
        outer_rows_of(
            along_y ^ d,
            (after(grad_pre, second_half), grad_pre_peer),
            (second_rows, second_peer),
            hidden_block,
        )
        for d in (1, 0)
    ]
    shrink_sum = add_low(shrink_parts[1], after(shrink_got, expand_parts[0]))
    expand_got = swap(after(expand_parts[0], shrink_got), ALONG_Y)

    grad_middle, grad_branch_half, middle_totals = by_rows(
        middle_back_kernel,
        half_start,
        half_len,
        [
            (cotangent_full, "from"),
            (middle, "from"),
            (after(second_half, expand_parts[1]), "rows"),
            (second_got, "rows"),
            (second_from_peer, "rows"),
            (active, "flag from"),
            (gain_two, "vector"),
        ],
        [("rows", f32), ("rows", low), ("totals", f32)],
        "middle_norm_back",
    )
    grad_branch = ordered(core, grad_branch_half, swap(grad_branch_half, CORE), 0)

    grad_mixed = through(grad_branch, w_out).astype(low)
    out_parts = list(outer_sides(
        [2 * places[d] + sides[i] for d in range(4) for i in range(2)],
        after(grad_branch, grad_mixed),
        mixed,
        depth_rows,
    ))
    out_parts[3] = after(out_parts[3], shrink_got)
    grad_qkv = attend_back(qkv, after(grad_mixed, out_parts[0]), mask)
    out_sum = total_plane(out_parts, grad_qkv)
    expand_sum = add_low(expand_parts[1], after(expand_got, grad_qkv))

    qkv_parts = {}
    left = grad_qkv
    for d in (3, 1, 2, 0):
        qkv_parts[d] = outer_rows_of(places[d], (left,), (first_rows,), 3 * depth_rows)
        left = after(left, qkv_parts[d])
    qkv_sum = total_plane([qkv_parts[d] for d in range(4)], None)
    grad_first, grad_first_got = own_half(left, w_qkv, through)
    grad_half, first_totals = by_rows(
        first_back_kernel,
        half_start,
        half_len,
        [
            (inputs, "from"),
            (grad_middle, "rows"),
            (grad_first, "rows"),
            (grad_first_got, "rows"),
            (gain_one, "vector"),
        ],
        [("rows", low), ("totals", f32)],
        "first_norm_back",
    )
    tokens_grad = from_chips(grad_half)

    shrunk_peer, shrunk_peer_got = own_half(after(activated_peer, grad_half), w_shrink, project)
    shrunk_from_peer = swap((shrunk_peer + shrunk_peer_got.astype(f32)).astype(low), ALONG_X)
    shrunk, shrunk_got = own_half(after(activated, shrunk_peer), w_shrink, project)
    shrunk = shrunk + shrunk_got.astype(f32) + shrunk_from_peer.astype(f32) + bias_shrink
    out_half_rows = (half_rows(middle, core) + half_rows(active, core) * shrunk).astype(low)
    layer_out = from_chips(out_half_rows)

    shrink_rows = scatter_z(shrink_sum)
    half = shrink_rows.shape[0] // 2
    shrink_rows = weave_columns(
        along_x, shrink_rows[:half], swap(shrink_rows[half:], ALONG_X), hidden_block
    )
    shrink_weight_grad = weave_columns(
        core, shrink_rows[:heads_rows], swap(shrink_rows[heads_rows:], CORE), hidden_block
    ).astype(f32)
    expand_weight_grad = scatter_z(expand_sum).astype(f32)
    out_rows = weave_columns(
        core, out_sum[:, : width // 2], swap(out_sum[:, width // 2 :], CORE), depth_rows
    )
    output_weight_grad = scatter_z(out_rows).astype(f32)
    qkv_weight_grad = scatter_z(qkv_sum).astype(f32)

    def column_sum(matrix):
        return jnp.sum(matrix.astype(f32), axis=0)

    def all_devices(totals, rows):
        return totals.reshape(devices, rows)

    def core_devices(totals, rows):
        cut = totals.reshape(4, 1, seq_size, rows)
        return ordered(core, cut, jnp.zeros_like(cut), 1).reshape(devices, rows)

    def quarter_devices(totals, rows):
        cut = totals.reshape(2, 1, seq_size, rows)
        none = jnp.zeros_like(cut)
        quarters = [jnp.where(2 * along_x + core == q, cut, none) for q in range(4)]
        return jnp.concatenate(quarters, 1).reshape(devices, rows)

    qkv_sums = column_sum(grad_qkv).reshape(4 * seq_size, 3, heads_rows)
    sums = jnp.concatenate(
        [
            all_devices(first_totals[0], heads_rows),
            all_devices(first_totals[1], heads_rows),
            core_devices(qkv_sums[:, 0], heads_rows),
            core_devices(qkv_sums[:, 2], heads_rows),
            all_devices(middle_totals[2], heads_rows),
            all_devices(middle_totals[0], heads_rows),
            all_devices(middle_totals[1], heads_rows),
            all_devices(0.5 * column_sum(grad_shrunk), heads_rows),
            quarter_devices(column_sum(grad_pre) + column_sum(grad_pre_peer), hidden_rows),
        ],
        axis=1,
    )
    to_relative = ((all_dp ^ dp) * seq_size + (all_seq + depth) % seq_size).reshape(-1)
    sums = sums[to_relative].reshape(dp_size, seq_size, -1)
    for bit in (ALONG_Y, ALONG_X, CORE):
        sums = sums[:bit] + swap(sums[bit:], bit)
    sums = sums[0]
    sums = sums[0] + sum(shift_z(sums[steps], steps) for steps in range(1, seq_size))

    def vector_grad(index):
        return sums[index * heads_rows : (index + 1) * heads_rows]

    return (
        layer_out,
        tokens_grad,
        vector_grad(0),
        vector_grad(1),
        qkv_weight_grad[:heads_rows],
        vector_grad(2),
        qkv_weight_grad[heads_rows : 2 * heads_rows],
        qkv_weight_grad[2 * heads_rows :],
        vector_grad(3),
        output_weight_grad,
        vector_grad(4),
        vector_grad(5),
        vector_grad(6),
        expand_weight_grad,
        sums[8 * heads_rows :],
        shrink_weight_grad,
        vector_grad(7),
    )


def general_device(
    tokens,
    exit_layer,
    first_gain,
    first_shift,
    query_weight,
    query_bias,
    key_weight,
    value_weight,
    value_bias,
    output_weight,
    output_bias,
    second_gain,
    second_shift,
    expand_weight,
    expand_bias,
    shrink_weight,
    shrink_bias,
    cotangent,
):
    seq_count, local_len, width = tokens.shape
    hidden_width = shrink_weight.shape[1]
    total_rows = seq_count * local_len
    heads = width // HEAD_DIM
    inputs = tokens.reshape(total_rows, width).astype(jnp.float32)
    active = (exit_layer > LAYER).astype(jnp.float32).reshape(total_rows, 1)
    gain_one, shift_one = (
        lax.all_gather(first_gain, ("dp", "seq"), axis=0, tiled=True),
        lax.all_gather(first_shift, ("dp", "seq"), axis=0, tiled=True),
    )
    gain_one = gain_one.astype(jnp.float32)
    shift_one = shift_one.astype(jnp.float32)
    normed_in = normalize(inputs)
    first_rows = (normed_in * gain_one + shift_one).astype(jnp.bfloat16)
    blank = jnp.zeros((total_rows, width), jnp.bfloat16)
    attention_init = (blank, blank, blank) + ()
    w_query = lax.all_gather(query_weight, ("dp", "seq"), axis=0, tiled=True)
    b_query = lax.all_gather(query_bias, ("dp", "seq"), axis=0, tiled=True)
    w_key = lax.all_gather(key_weight, ("dp", "seq"), axis=0, tiled=True)
    w_value = lax.all_gather(value_weight, ("dp", "seq"), axis=0, tiled=True)
    b_value = lax.all_gather(value_bias, ("dp", "seq"), axis=0, tiled=True)
    queries = place_cols(
        attention_init[0], project(first_rows, w_query) + b_query.astype(jnp.float32)
    )
    key_rows = place_cols(attention_init[1], project(first_rows, w_key))
    value_rows = place_cols(
        attention_init[2], project(first_rows, w_value) + b_value.astype(jnp.float32)
    )
    stored = attention_init[3:]
    gathered = (queries, key_rows, value_rows) + stored
    queries, key_rows, value_rows = (gathered[0], gathered[1], gathered[2])
    query_local = queries.reshape(seq_count, local_len, width)
    key_local = key_rows.reshape(seq_count, local_len, width)
    value_local = value_rows.reshape(seq_count, local_len, width)
    alive_local = active.reshape(seq_count, local_len)
    key_all, value_all, alive_all = (
        lax.all_gather(key_local, "seq", axis=1, tiled=True),
        lax.all_gather(value_local, "seq", axis=1, tiled=True),
        lax.all_gather(alive_local.astype(jnp.bfloat16), "seq", axis=1, tiled=True),
    )
    full_len = key_all.shape[1]
    offset = lax.axis_index("seq") * local_len
    query_pos = offset + jnp.arange(local_len, dtype=jnp.int32)
    key_pos = jnp.arange(full_len, dtype=jnp.int32)
    causal = key_pos[None, :] <= query_pos[:, None]
    allowed = causal[None, None] & (alive_all.astype(jnp.float32)[:, None, None, :] > 0.5)
    factor = HEAD_DIM ** (-0.5)
    group = min(8, heads)
    group_width = group * HEAD_DIM
    group_total = heads // group

    def group_parts(start_col):
        q_part = lax.dynamic_slice_in_dim(query_local, start_col, group_width, 2).reshape(
            seq_count, local_len, group, HEAD_DIM
        )
        k_part = lax.dynamic_slice_in_dim(key_all, start_col, group_width, 2).reshape(
            seq_count, full_len, group, HEAD_DIM
        )
        v_part = lax.dynamic_slice_in_dim(value_all, start_col, group_width, 2).reshape(
            seq_count, full_len, group, HEAD_DIM
        )
        scores = (
            jnp.einsum("sqhd,skhd->shqk", q_part, k_part, preferred_element_type=jnp.float32)
            * factor
        )
        scores = jnp.where(allowed, scores, jnp.float32(-1e30))
        return (q_part, k_part, v_part, scores)

    def forward_group(group_index, state):
        mixed_all, log_total = state
        start_col = group_index * group_width
        q_part, k_part, v_part, scores = group_parts(start_col)
        row_max = jnp.max(scores, axis=-1, keepdims=True)
        raised = jnp.exp(scores - row_max)
        totals = jnp.sum(raised, axis=-1, keepdims=True)
        weights_low = (raised / totals).astype(jnp.bfloat16)
        outcome = jnp.einsum(
            "shqk,skhd->sqhd", weights_low, v_part, preferred_element_type=jnp.float32
        )
        mixed_all = lax.dynamic_update_slice_in_dim(
            mixed_all,
            outcome.reshape(seq_count, local_len, group_width).astype(jnp.bfloat16),
            start_col,
            2,
        )
        log_total = lax.dynamic_update_slice_in_dim(
            log_total, (row_max + jnp.log(totals))[..., 0], group_index * group, 1
        )
        return (mixed_all, log_total)

    mixed_all, log_total = lax.fori_loop(
        0,
        group_total,
        forward_group,
        (
            jnp.zeros((seq_count, local_len, width), jnp.bfloat16),
            jnp.zeros((seq_count, heads, local_len), jnp.float32),
        ),
    )
    mixed = mixed_all.reshape(total_rows, width)
    vector_blank = jnp.zeros((width,), jnp.bfloat16)
    output_init = (jnp.zeros((total_rows, width), jnp.float32), vector_blank, vector_blank) + ()
    w_out = lax.all_gather(output_weight, ("dp", "seq"), axis=0, tiled=True)
    b_out = lax.all_gather(output_bias, ("dp", "seq"), axis=0, tiled=True)
    g_piece = lax.all_gather(second_gain, ("dp", "seq"), axis=0, tiled=True)
    s_piece = lax.all_gather(second_shift, ("dp", "seq"), axis=0, tiled=True)
    branch = place_cols(output_init[0], project(mixed, w_out) + b_out.astype(jnp.float32))
    gain_two = g_piece
    shift_two = s_piece
    stored = output_init[3:]
    folded = (branch, gain_two, shift_two) + stored
    branch = folded[0]
    gain_two = folded[1].astype(jnp.float32)
    shift_two = folded[2].astype(jnp.float32)
    middle = inputs + active * branch
    normed_mid = normalize(middle)
    second_rows = (normed_mid * gain_two + shift_two).astype(jnp.bfloat16)
    expand_init = (jnp.zeros((total_rows, hidden_width), jnp.float32),) + ()
    w_expand = lax.all_gather(expand_weight, ("dp", "seq"), axis=0, tiled=True)
    b_expand = lax.all_gather(expand_bias, ("dp", "seq"), axis=0, tiled=True)
    hidden_pre = place_cols(
        expand_init[0], project(second_rows, w_expand) + b_expand.astype(jnp.float32)
    )
    stored = expand_init[1:]
    expanded = (hidden_pre,) + stored
    hidden_pre = expanded[0]

    def gelu_exact(pre_values):
        return jax.nn.gelu(pre_values, approximate=False)

    activated_full, gelu_back = jax.vjp(gelu_exact, hidden_pre)
    activated = activated_full.astype(jnp.bfloat16)
    shrink_init = (jnp.zeros((total_rows, width), jnp.float32),) + ()
    w_shrink = lax.all_gather(shrink_weight, ("dp", "seq"), axis=0, tiled=True)
    b_shrink = lax.all_gather(shrink_bias, ("dp", "seq"), axis=0, tiled=True)
    shrunk = place_cols(shrink_init[0], project(activated, w_shrink) + b_shrink.astype(jnp.float32))
    stored = shrink_init[1:]
    shrunk_all = (shrunk,) + stored
    shrunk = shrunk_all[0]
    layer_out = (middle + active * shrunk).astype(jnp.bfloat16).reshape(seq_count, local_len, width)
    grad_out = cotangent.reshape(total_rows, width).astype(jnp.float32)
    grad_shrunk = (active * grad_out).astype(jnp.bfloat16)
    grad_units = through(
        grad_shrunk, lax.all_gather(shrink_weight, ("dp", "seq"), axis=0, tiled=True)
    )
    grad_pre = gelu_back(grad_units)[0].astype(jnp.bfloat16)
    grad_second = through(
        grad_pre, lax.all_gather(expand_weight, ("dp", "seq"), axis=0, tiled=True)
    )
    mid_value, mid_back = jax.vjp(normalize, middle)
    grad_middle = grad_out + mid_back(grad_second * gain_two)[0]
    grad_branch = (active * grad_middle).astype(jnp.bfloat16)
    grad_mixed = through(
        grad_branch, lax.all_gather(output_weight, ("dp", "seq"), axis=0, tiled=True)
    )
    grad_mixed_local = grad_mixed.astype(jnp.bfloat16).reshape(seq_count, local_len, width)

    def backward_group(group_index, state):
        grad_query_all, grad_key_all, grad_value_all = state
        start_col = group_index * group_width
        q_part, k_part, v_part, scores = group_parts(start_col)
        g_part = lax.dynamic_slice_in_dim(grad_mixed_local, start_col, group_width, 2).reshape(
            seq_count, local_len, group, HEAD_DIM
        )
        lse_part = lax.dynamic_slice_in_dim(log_total, group_index * group, group, 1)
        soft = jnp.exp(scores - lse_part[..., None])
        grad_probs = jnp.einsum(
            "sqhd,skhd->shqk", g_part, v_part, preferred_element_type=jnp.float32
        )
        value_term = jnp.einsum(
            "shqk,sqhd->skhd", soft.astype(jnp.bfloat16), g_part, preferred_element_type=jnp.float32
        )
        centered = jnp.sum(soft * grad_probs, axis=-1, keepdims=True)
        grad_scores = (soft * (grad_probs - centered)).astype(jnp.bfloat16)
        query_term = (
            jnp.einsum("shqk,skhd->sqhd", grad_scores, k_part, preferred_element_type=jnp.float32)
            * factor
        )
        key_term = (
            jnp.einsum("shqk,sqhd->skhd", grad_scores, q_part, preferred_element_type=jnp.float32)
            * factor
        )
        grad_query_all = lax.dynamic_update_slice_in_dim(
            grad_query_all, query_term.reshape(seq_count, local_len, group_width), start_col, 2
        )
        grad_key_all = lax.dynamic_update_slice_in_dim(
            grad_key_all, key_term.reshape(seq_count, full_len, group_width), start_col, 2
        )
        grad_value_all = lax.dynamic_update_slice_in_dim(
            grad_value_all, value_term.reshape(seq_count, full_len, group_width), start_col, 2
        )
        return (grad_query_all, grad_key_all, grad_value_all)

    grad_query_all, grad_key_all, grad_value_all = lax.fori_loop(
        0,
        group_total,
        backward_group,
        (
            jnp.zeros((seq_count, local_len, width), jnp.float32),
            jnp.zeros((seq_count, full_len, width), jnp.float32),
            jnp.zeros((seq_count, full_len, width), jnp.float32),
        ),
    )
    key_sum, value_sum = (
        lax.psum_scatter(grad_key_all, "seq", scatter_dimension=1, tiled=True),
        lax.psum_scatter(grad_value_all, "seq", scatter_dimension=1, tiled=True),
    )
    grad_query = grad_query_all.astype(jnp.bfloat16).reshape(total_rows, width)
    grad_key = key_sum.astype(jnp.bfloat16).reshape(total_rows, width)
    grad_value = value_sum.astype(jnp.bfloat16).reshape(total_rows, width)
    total = through(grad_query, lax.all_gather(query_weight, ("dp", "seq"), axis=0, tiled=True))
    total = total + through(grad_key, lax.all_gather(key_weight, ("dp", "seq"), axis=0, tiled=True))
    grad_first = total + through(
        grad_value, lax.all_gather(value_weight, ("dp", "seq"), axis=0, tiled=True)
    )
    in_value, in_back = jax.vjp(normalize, inputs)
    tokens_grad = (
        (grad_middle + in_back(grad_first * gain_one)[0])
        .astype(jnp.bfloat16)
        .reshape(seq_count, local_len, width)
    )
    first_scaled = grad_first * normed_in
    second_scaled = grad_second * normed_mid
    vectors = jnp.stack(
        [
            column_total(grad_query),
            column_total(grad_value),
            column_total(grad_branch),
            column_total(grad_shrunk),
            column_total(first_scaled),
            column_total(grad_first),
            column_total(second_scaled),
            column_total(grad_second),
        ],
        axis=1,
    )

    def scattered(grad_cols, inputs):
        return lax.psum_scatter(
            outer_rows(grad_cols, inputs), ("dp", "seq"), scatter_dimension=0, tiled=True
        )

    vector_sums = lax.psum_scatter(vectors, ("dp", "seq"), scatter_dimension=0, tiled=True)
    expand_bias_sums = lax.psum_scatter(
        column_total(grad_pre), ("dp", "seq"), scatter_dimension=0, tiled=True
    )
    shrink_sums = scattered(grad_shrunk, activated)
    grad_pre, second_rows, shrink_sums = lax.optimization_barrier(
        (grad_pre, second_rows, shrink_sums)
    )
    expand_sums = scattered(grad_pre, second_rows)
    grad_branch, grad_query, grad_key, grad_value, expand_sums = lax.optimization_barrier(
        (grad_branch, grad_query, grad_key, grad_value, expand_sums)
    )
    return (
        layer_out,
        tokens_grad,
        vector_sums[:, 4],
        vector_sums[:, 5],
        scattered(grad_query, first_rows),
        vector_sums[:, 0],
        scattered(grad_key, first_rows),
        scattered(grad_value, first_rows),
        vector_sums[:, 1],
        scattered(grad_branch, mixed),
        vector_sums[:, 2],
        vector_sums[:, 6],
        vector_sums[:, 7],
        expand_sums,
        expand_bias_sums,
        shrink_sums,
        vector_sums[:, 3],
    )


def solution(mesh):
    in_specs = (
        P("dp", "seq", None),
        P("dp", "seq"),
        P(("dp", "seq")),
        P(("dp", "seq")),
        P(("dp", "seq"), None),
        P(("dp", "seq")),
        P(("dp", "seq"), None),
        P(("dp", "seq"), None),
        P(("dp", "seq")),
        P(("dp", "seq"), None),
        P(("dp", "seq")),
        P(("dp", "seq")),
        P(("dp", "seq")),
        P(("dp", "seq"), None),
        P(("dp", "seq")),
        P(("dp", "seq"), None),
        P(("dp", "seq")),
        P("dp", "seq", None),
    )
    out_specs = (
        P("dp", "seq", None),
        P("dp", "seq", None),
        P(("dp", "seq")),
        P(("dp", "seq")),
        P(("dp", "seq"), None),
        P(("dp", "seq")),
        P(("dp", "seq"), None),
        P(("dp", "seq"), None),
        P(("dp", "seq")),
        P(("dp", "seq"), None),
        P(("dp", "seq")),
        P(("dp", "seq")),
        P(("dp", "seq")),
        P(("dp", "seq"), None),
        P(("dp", "seq")),
        P(("dp", "seq"), None),
        P(("dp", "seq")),
    )
    def per_device(*arrays):
        tokens, query_weight = arrays[0], arrays[4]
        fits = (
            mesh.shape["dp"] == 8
            and mesh.shape["seq"] == 4
            and tokens.shape[0] == 2
            and query_weight.shape[0] == HEAD_DIM
        )
        return (whole_sequence_device if fits else general_device)(*arrays)

    return jax.shard_map(
        per_device, mesh=mesh, in_specs=in_specs, out_specs=out_specs, check_vma=False
    )
```

```python
import math

import jax
import jax.numpy as jnp
from jax import lax
from jax.experimental import pallas as pl
from jax.experimental.pallas import tpu as pltpu
from jax.sharding import Mesh, PartitionSpec as P

HEAD_DIM = 64
LAYER = 12


EPS = 1e-05


def normalize(values):
    center = values - jnp.mean(values, axis=-1, keepdims=True)
    spread = jnp.mean(center * center, axis=-1, keepdims=True)
    return center * lax.rsqrt(spread + EPS)


def project(left, weight):
    return lax.dot_general(
        left, weight, (((1,), (1,)), ((), ())), preferred_element_type=jnp.float32
    )


def through(left, weight):
    return jnp.dot(left, weight, preferred_element_type=jnp.float32)


def outer_rows(grad_cols, inputs):
    return lax.dot_general(
        grad_cols, inputs, (((0,), (0,)), ((), ())), preferred_element_type=jnp.float32
    )


def place_cols(buffer, piece):
    return piece.astype(buffer.dtype)


def column_total(matrix):
    return jnp.sum(matrix, axis=0, dtype=jnp.float32)


BRIEF = pl.CostEstimate(flops=1, bytes_accessed=1, transcendentals=0)

CORE, ALONG_X, ALONG_Y = "core", "x", "y"
DEVICES = ("y", "x", "core", "seq")


def swap(values, axis):
    return lax.ppermute(values, axis, [(0, 1), (1, 0)])


def pick(flag, first, second):
    return jnp.where(flag == 0, first, second)


def ordered(flag, own, other, axis):
    return pick(
        flag, jnp.concatenate([own, other], axis), jnp.concatenate([other, own], axis)
    )


def arrange(pieces, block, sources, targets):
    count = len(pieces)
    steps = len(sources)
    table = jnp.stack([jnp.asarray(target, jnp.int32) for target in targets])

    def kernel(table_ref, *refs):
        step = pl.program_id(0)
        for index in range(count):
            mine = [at for at, source in enumerate(sources) if source[0] == index]

            @pl.when((step >= mine[0]) & (step <= mine[-1]))
            def _():
                refs[count][...] = refs[index][...]

    def place_of(index):
        mine = [at for at, source in enumerate(sources) if source[0] == index]

        def block_of(step, table_ref):
            row, column = sources[mine[0]][1:]
            for at in mine[1:]:
                row = jnp.where(step >= at, sources[at][1], row)
                column = jnp.where(step >= at, sources[at][2], column)
            return row, column

        return block_of

    total = steps * block[0] * block[1]
    return pl.pallas_call(
        kernel,
        grid_spec=pltpu.PrefetchScalarGridSpec(
            num_scalar_prefetch=1,
            grid=(steps,),
            in_specs=[pl.BlockSpec(block, place_of(index)) for index in range(count)],
            out_specs=pl.BlockSpec(block, lambda step, table_ref: (table_ref[step], 0)),
        ),
        out_shape=jax.ShapeDtypeStruct((steps * block[0], block[1]), pieces[0].dtype),
        compiler_params=pltpu.CompilerParams(vmem_limit_bytes=48 << 20),
        cost_estimate=BRIEF,
        name="arrange",
    )(table, *pieces)


def split_kernel(table_ref, first, second, first_out, second_out):
    first_out[...] = first[...]
    second_out[...] = second[...]


def split_columns(core, matrix, block):
    rows, columns = matrix.shape
    count = columns // block // 2
    piece = jax.ShapeDtypeStruct((rows, columns // 2), matrix.dtype)
    return pl.pallas_call(
        split_kernel,
        grid_spec=pltpu.PrefetchScalarGridSpec(
            num_scalar_prefetch=1,
            grid=(count,),
            in_specs=[
                pl.BlockSpec((rows, block), lambda i, core_ref: (0, 2 * i + core_ref[0])),
                pl.BlockSpec((rows, block), lambda i, core_ref: (0, 2 * i + 1 - core_ref[0])),
            ],
            out_specs=[pl.BlockSpec((rows, block), lambda i, core_ref: (0, i))] * 2,
        ),
        out_shape=(piece, piece),
        cost_estimate=BRIEF,
        name="split_columns",
    )(core.reshape(1), matrix, matrix)


def weave_kernel(core_ref, mine, theirs, out):
    block = mine.shape[1]

    @pl.when(core_ref[0] == 0)
    def _():
        out[:, :block] = mine[...]
        out[:, block:] = theirs[...]

    @pl.when(core_ref[0] == 1)
    def _():
        out[:, :block] = theirs[...]
        out[:, block:] = mine[...]


def weave_columns(core, mine, theirs, block):
    rows, columns = mine.shape
    return pl.pallas_call(
        weave_kernel,
        grid_spec=pltpu.PrefetchScalarGridSpec(
            num_scalar_prefetch=1,
            grid=(columns // block,),
            in_specs=[pl.BlockSpec((rows, block), lambda i, core_ref: (0, i))] * 2,
            out_specs=pl.BlockSpec((rows, 2 * block), lambda i, core_ref: (0, i)),
        ),
        out_shape=jax.ShapeDtypeStruct((rows, 2 * columns), mine.dtype),
        cost_estimate=BRIEF,
        name="weave_columns",
    )(core.reshape(1), mine, theirs)


def outer_rows_of(lefts, rights, rows, sources, tile=512, runs=None):
    count, columns = rights[0].shape
    terms, blocks = len(lefts), len(sources)
    table = jnp.stack([jnp.asarray(index, jnp.int32) for index in [*sources, *(runs or [])]])

    def kernel(table_ref, *refs):
        total = 0.0
        for left, right in zip(refs[:terms], refs[terms : 2 * terms]):
            total = total + lax.dot_general(
                left[...], right[...], (((0,), (0,)), ((), ())), preferred_element_type=jnp.float32
            )
        total = total.astype(jnp.bfloat16)
        if runs is None:
            refs[-1][...] = total
        else:
            for at in range(len(runs)):
                start = pl.multiple_of(table_ref[blocks + at] * HEAD_DIM, HEAD_DIM)
                refs[-1][pl.ds(start, HEAD_DIM), :] = total[at * HEAD_DIM : (at + 1) * HEAD_DIM]

    return pl.pallas_call(
        kernel,
        grid_spec=pltpu.PrefetchScalarGridSpec(
            num_scalar_prefetch=1,
            grid=(blocks, columns // tile),
            in_specs=[pl.BlockSpec((count, rows), lambda i, j, ref: (0, ref[i]))] * terms
            + [pl.BlockSpec((count, tile), lambda i, j, ref: (0, j))] * terms,
            out_specs=pl.BlockSpec((rows, tile), lambda i, j, ref: (i, j)),
        ),
        out_shape=jax.ShapeDtypeStruct((blocks * rows, columns), jnp.bfloat16),
        compiler_params=pltpu.CompilerParams(vmem_limit_bytes=48 << 20),
        cost_estimate=BRIEF,
        name="outer_rows_of",
    )(table, *lefts, *rights)


def outer_sides(indices, left, right, rows):
    count, columns = right.shape
    pieces = len(indices) // 2
    table = jnp.stack([jnp.asarray(index, jnp.int32) for index in indices])

    def kernel(table_ref, left, right, *outs):
        step = pl.program_id(0)
        total = lax.dot_general(
            left[...], right[...], (((0,), (0,)), ((), ())), preferred_element_type=jnp.float32
        ).astype(jnp.bfloat16)
        for piece, out in enumerate(outs):

            @pl.when(step // 2 == piece)
            def _():
                out[...] = total

    def side_of(piece):
        return lambda step, table_ref: (0, jnp.clip(step - 2 * piece, 0, 1))

    return pl.pallas_call(
        kernel,
        grid_spec=pltpu.PrefetchScalarGridSpec(
            num_scalar_prefetch=1,
            grid=(2 * pieces,),
            in_specs=[
                pl.BlockSpec((count, rows), lambda step, table_ref: (0, table_ref[step])),
                pl.BlockSpec((count, columns), lambda step, table_ref: (0, 0)),
            ],
            out_specs=[pl.BlockSpec((rows, columns), side_of(piece)) for piece in range(pieces)],
        ),
        out_shape=[jax.ShapeDtypeStruct((rows, 2 * columns), jnp.bfloat16)] * pieces,
        compiler_params=pltpu.CompilerParams(vmem_limit_bytes=48 << 20),
        cost_estimate=BRIEF,
        name="outer_sides",
    )(table, left, right)


def regroup(bits, matrix, seq_size):
    rows, columns = matrix.shape
    block = 256

    def kernel(bits_ref, matrix, out):
        for flips in range(8):
            y_flip, x_flip, core_flip = flips // 4, flips // 2 % 2, flips % 2

            @pl.when(4 * bits_ref[0] + 2 * bits_ref[1] + bits_ref[2] == flips)
            def _():
                runs = [
                    (((y ^ y_flip) * 2 + (x ^ x_flip)) * 2 + (side ^ core_flip)) * seq_size + z
                    for z in range(seq_size)
                    for y in range(2)
                    for x in range(2)
                    for side in range(2)
                ]
                out[...] = jnp.concatenate(
                    [matrix[:, run * HEAD_DIM : (run + 1) * HEAD_DIM] for run in runs], axis=1
                )

    return pl.pallas_call(
        kernel,
        grid_spec=pltpu.PrefetchScalarGridSpec(
            num_scalar_prefetch=1,
            grid=(rows // block,),
            in_specs=[pl.BlockSpec((block, columns), lambda i, bits_ref: (i, 0))],
            out_specs=pl.BlockSpec((block, columns), lambda i, bits_ref: (i, 0)),
        ),
        out_shape=jax.ShapeDtypeStruct((rows, columns), matrix.dtype),
        compiler_params=pltpu.CompilerParams(vmem_limit_bytes=48 << 20),
        cost_estimate=BRIEF,
        name="regroup",
    )(bits, matrix)


def regroup_back(bits, mine, got, seq_size, dtype):
    rows, columns = mine.shape
    block = 128

    def kernel(bits_ref, mine, got, out):
        for flips in range(8):
            y_flip, x_flip, core_flip = flips // 4, flips // 2 % 2, flips % 2

            @pl.when(4 * bits_ref[0] + 2 * bits_ref[1] + bits_ref[2] == flips)
            def _():
                runs = [
                    ((z * 2 + (y ^ y_flip)) * 2 + (x ^ x_flip)) * 2 + (side ^ core_flip)
                    for y in range(2)
                    for x in range(2)
                    for side in range(2)
                    for z in range(seq_size)
                ]
                own = [mine[:, run * HEAD_DIM : (run + 1) * HEAD_DIM] for run in runs]
                runs = [run ^ 1 for run in runs]
                other = [got[:, run * HEAD_DIM : (run + 1) * HEAD_DIM] for run in runs]
                out[...] = (
                    jnp.concatenate(own, axis=1)
                    + jnp.concatenate(other, axis=1).astype(jnp.float32)
                ).astype(dtype)

    spec = pl.BlockSpec((block, columns), lambda i, bits_ref: (i, 0))
    return pl.pallas_call(
        kernel,
        grid_spec=pltpu.PrefetchScalarGridSpec(
            num_scalar_prefetch=1,
            grid=(rows // block,),
            in_specs=[spec, spec],
            out_specs=spec,
        ),
        out_shape=jax.ShapeDtypeStruct((rows, columns), dtype),
        compiler_params=pltpu.CompilerParams(vmem_limit_bytes=48 << 20),
        cost_estimate=BRIEF,
        name="regroup_back",
    )(bits, mine, got)


def half_dot(which, left, right, by_columns, dtype, tile=512, places=None):
    lefts = left if places is not None else (left,)
    rows, depth = lefts[0].shape
    columns = right.shape[0] if by_columns else right.shape[1]
    contract = 1 if by_columns else 0
    count = len(lefts)
    table = jnp.stack([which, *(places or [])])

    def kernel(table_ref, *refs):
        total = 0.0
        for index in range(count):
            total = total + lax.dot_general(
                refs[index][...],
                refs[count + index][...],
                (((1,), (contract,)), ((), ())),
                preferred_element_type=jnp.float32,
            )
        refs[-1][...] = total.astype(dtype)

    def right_block(index):
        if by_columns:
            return pl.BlockSpec((tile, depth), lambda i, table_ref: (i, 0))
        if places is None:
            return pl.BlockSpec((depth, tile), lambda i, table_ref: (0, i))
        return pl.BlockSpec((depth, tile), lambda i, table_ref: (table_ref[1 + index], i))

    return pl.pallas_call(
        kernel,
        grid_spec=pltpu.PrefetchScalarGridSpec(
            num_scalar_prefetch=1,
            grid=(columns // tile,),
            in_specs=[
                pl.BlockSpec((rows // 2, depth), lambda i, table_ref: (table_ref[0], 0))
            ]
            * count
            + [right_block(index) for index in range(count)],
            out_specs=pl.BlockSpec((rows // 2, tile), lambda i, table_ref: (0, i)),
        ),
        out_shape=jax.ShapeDtypeStruct((rows // 2, columns), dtype),
        compiler_params=pltpu.CompilerParams(vmem_limit_bytes=48 << 20),
        cost_estimate=BRIEF,
        name="half_dot",
    )(table, *lefts, *[right] * count)


def multiply(lefts, rights, by_columns, tile=512, bias=None, slope=None, lift=False):
    rows = lefts[0].shape[0]
    terms = len(lefts)
    columns = rights[0].shape[0] if by_columns else rights[0].shape[1]
    contract = 1 if by_columns else 0
    extra = [] if bias is None else [bias]
    extra += [] if slope is None else [slope]
    across = pl.BlockSpec((rows, tile), lambda i: (0, i))
    row = pl.BlockSpec((1, tile), lambda i: (0, i))
    wide = jax.ShapeDtypeStruct((rows, columns), jnp.bfloat16)
    outs = [(across, wide)]
    if lift:
        outs.append((across, wide))
    if slope is not None:
        outs.append((row, jax.ShapeDtypeStruct((1, columns), jnp.float32)))

    def kernel(*refs):
        total = 0.0
        for left, right in zip(refs[:terms], refs[terms : 2 * terms]):
            total = total + lax.dot_general(
                left[...],
                right[...],
                (((1,), (contract,)), ((), ())),
                preferred_element_type=jnp.float32,
            )
        rest = refs[2 * terms :]
        if bias is not None:
            total = total + rest[0][...]
        out = rest[len(extra)]
        if lift:
            lifted = 0.5 * (1.0 + lax.erf(total * (0.5**0.5)))
            bell = jnp.exp(-0.5 * total * total) * ((0.5 / math.pi) ** 0.5)
            out[...] = (total * lifted).astype(jnp.bfloat16)
            rest[len(extra) + 1][...] = (lifted + total * bell).astype(jnp.bfloat16)
        elif slope is not None:
            low = (total * rest[len(extra) - 1][...].astype(jnp.float32)).astype(jnp.bfloat16)
            out[...] = low
            rest[len(extra) + 1][...] = jnp.sum(low.astype(jnp.float32), axis=0, keepdims=True)
        else:
            out[...] = total.astype(jnp.bfloat16)

    def right_spec(right):
        if by_columns:
            return pl.BlockSpec((tile, right.shape[1]), lambda i: (i, 0))
        return pl.BlockSpec((right.shape[0], tile), lambda i: (0, i))

    result = pl.pallas_call(
        kernel,
        grid=(columns // tile,),
        in_specs=[pl.BlockSpec(left.shape, lambda i: (0, 0)) for left in lefts]
        + [right_spec(right) for right in rights]
        + ([] if bias is None else [row])
        + ([] if slope is None else [across]),
        out_specs=[spec for spec, _ in outs],
        out_shape=[shape for _, shape in outs],
        compiler_params=pltpu.CompilerParams(vmem_limit_bytes=48 << 20),
        cost_estimate=BRIEF,
        name="multiply",
    )(*lefts, *rights, *extra)
    return result if len(outs) > 1 else result[0]


def add_low(left, right):
    return (left.astype(jnp.float32) + right.astype(jnp.float32)).astype(jnp.bfloat16)


BLOCK = 256


def softmax_block(index, keys_wide, query_wide):
    start = index * BLOCK
    tiles = []
    if index > 0:
        tiles.append(
            lax.dot_general(
                keys_wide[:start],
                query_wide,
                (((1,), (1,)), ((), ())),
                preferred_element_type=jnp.float32,
            )
        )
    last = lax.dot_general(
        keys_wide[start : start + BLOCK],
        query_wide,
        (((1,), (1,)), ((), ())),
        preferred_element_type=jnp.float32,
    )
    key_pos = lax.broadcasted_iota(jnp.int32, last.shape, 0)
    query_pos = lax.broadcasted_iota(jnp.int32, last.shape, 1)
    tiles.append(jnp.where(key_pos <= query_pos, last, jnp.float32(-1e30)))
    peak = jnp.max(tiles[-1], axis=0, keepdims=True)
    if index > 0:
        peak = jnp.maximum(peak, jnp.max(tiles[0], axis=0, keepdims=True))
    tiles = [jnp.exp(tile - peak) for tile in tiles]
    total = sum(jnp.sum(tile, axis=0, keepdims=True) for tile in tiles)
    inverse = 1.0 / total
    return [tile * inverse for tile in tiles]


def widen(head, rows_ref, mask_ref):
    first = 3 * HEAD_DIM * head
    query = rows_ref[:, first : first + HEAD_DIM] * jnp.bfloat16(HEAD_DIM**-0.5)
    keys = rows_ref[:, first + HEAD_DIM : first + 2 * HEAD_DIM]
    values = rows_ref[:, first + 2 * HEAD_DIM : first + 3 * HEAD_DIM]
    even = jnp.full(query.shape, 1.0 / HEAD_DIM, jnp.bfloat16)
    query_wide = jnp.concatenate([query, even], axis=1)
    keys_wide = jnp.concatenate([keys, mask_ref[...]], axis=1)
    return query, keys, values, query_wide, keys_wide


def attend_kernel(rows_ref, mask_ref, out_ref):
    blocks = rows_ref.shape[0] // BLOCK
    results = [[], []]
    for head in range(2):
        _, _, values, query_wide, keys_wide = widen(head, rows_ref, mask_ref)
        for index in range(blocks):
            start, stop = index * BLOCK, (index + 1) * BLOCK
            tiles = softmax_block(index, keys_wide, query_wide[start:stop])
            low = jnp.concatenate([tile.astype(jnp.bfloat16) for tile in tiles], axis=0)
            outcome = lax.dot_general(
                values[:stop], low, (((0,), (0,)), ((), ())), preferred_element_type=jnp.float32
            )
            results[head].append(outcome.T)
    for index in range(blocks):
        both = jnp.concatenate([results[0][index], results[1][index]], axis=1)
        out_ref[index * BLOCK : (index + 1) * BLOCK, :] = both.astype(jnp.bfloat16)


def attend_back_kernel(rows_ref, grad_ref, mask_ref, out_ref, key_sum, value_sum):
    blocks = rows_ref.shape[0] // BLOCK
    columns = []
    for head in range(2):
        query, keys, values, query_wide, keys_wide = widen(head, rows_ref, mask_ref)
        grad = grad_ref[:, head * HEAD_DIM : (head + 1) * HEAD_DIM]
        query_parts = []
        for index in reversed(range(blocks)):
            start, stop = index * BLOCK, (index + 1) * BLOCK
            tiles = softmax_block(index, keys_wide, query_wide[start:stop])
            soft = jnp.concatenate(tiles, axis=0)
            grad_rows = grad[start:stop]
            grad_probs = lax.dot_general(
                values[:stop],
                grad_rows,
                (((1,), (1,)), ((), ())),
                preferred_element_type=jnp.float32,
            )
            weighted = soft * grad_probs
            delta = jnp.sum(weighted, axis=0, keepdims=True)
            grad_scores = (weighted - soft * delta).astype(jnp.bfloat16)
            value_term = jnp.dot(
                soft.astype(jnp.bfloat16), grad_rows, preferred_element_type=jnp.float32
            )
            key_term = jnp.dot(
                grad_scores, query[start:stop], preferred_element_type=jnp.float32
            )
            if index == blocks - 1:
                value_sum[...] = value_term
                key_sum[...] = key_term
            else:
                value_sum[:stop, :] += value_term
                key_sum[:stop, :] += key_term
            outcome = lax.dot_general(
                keys[:stop],
                grad_scores,
                (((0,), (0,)), ((), ())),
                preferred_element_type=jnp.float32,
            )
            query_parts.insert(0, outcome.T * jnp.float32(HEAD_DIM**-0.5))
        columns += [jnp.concatenate(query_parts, axis=0), key_sum[...], value_sum[...]]
    out_ref[...] = jnp.concatenate([part.astype(jnp.bfloat16) for part in columns], axis=1)


def attend(rows, mask):
    count, columns = rows.shape
    pairs = columns // (6 * HEAD_DIM)
    work = pairs * 2 * count * count * HEAD_DIM
    return pl.pallas_call(
        attend_kernel,
        grid=(pairs,),
        in_specs=[
            pl.BlockSpec((count, 6 * HEAD_DIM), lambda i: (0, i)),
            pl.BlockSpec((count, HEAD_DIM), lambda i: (0, 0)),
        ],
        out_specs=pl.BlockSpec((count, 2 * HEAD_DIM), lambda i: (0, i)),
        out_shape=jax.ShapeDtypeStruct((count, pairs * 2 * HEAD_DIM), jnp.bfloat16),
        compiler_params=pltpu.CompilerParams(vmem_limit_bytes=48 << 20),
        cost_estimate=BRIEF,
        name="attend",
    )(rows, mask)


def attend_back(rows, grad, mask, place):
    count, columns = rows.shape
    pairs = columns // (6 * HEAD_DIM) // 4

    def kernel(place_ref, *refs):
        attend_back_kernel(*refs)

    return pl.pallas_call(
        kernel,
        grid_spec=pltpu.PrefetchScalarGridSpec(
            num_scalar_prefetch=1,
            grid=(pairs,),
            in_specs=[
                pl.BlockSpec(
                    (count, 6 * HEAD_DIM), lambda i, place_ref: (0, pairs * place_ref[0] + i)
                ),
                pl.BlockSpec(
                    (count, 2 * HEAD_DIM), lambda i, place_ref: (0, pairs * place_ref[0] + i)
                ),
                pl.BlockSpec((count, HEAD_DIM), lambda i, place_ref: (0, 0)),
            ],
            out_specs=pl.BlockSpec((count, 6 * HEAD_DIM), lambda i, place_ref: (0, i)),
            scratch_shapes=[pltpu.VMEM((count, HEAD_DIM), jnp.float32)] * 2,
        ),
        out_shape=jax.ShapeDtypeStruct((count, columns // 4), jnp.bfloat16),
        compiler_params=pltpu.CompilerParams(vmem_limit_bytes=48 << 20),
        cost_estimate=BRIEF,
        name="attend_back",
    )(place.reshape(1), rows, grad, mask)


ROWS = 128


def normal_parts(values):
    center = values - jnp.mean(values, axis=-1, keepdims=True)
    spread_of = jnp.mean(center * center, axis=-1, keepdims=True)
    scale = lax.rsqrt(spread_of + EPS)
    return center * scale, scale


def normal_back(normed, scale, grad):
    mean_grad = jnp.mean(grad, axis=-1, keepdims=True)
    mean_product = jnp.mean(grad * normed, axis=-1, keepdims=True)
    return (grad - mean_grad - normed * mean_product) * scale


def first_kernel(start_ref, tokens, gain, shift, out):
    normed, _ = normal_parts(tokens[...].astype(jnp.float32))
    out[...] = (normed * gain[...] + shift[...]).astype(out.dtype)


def middle_kernel(
    start_ref, tokens, own, upper, lower, active, bias, gain, shift, middle_out, rows_out
):
    in_upper = pl.program_id(0) < pl.num_programs(0) // 2
    got = jnp.where(in_upper, upper[...], lower[...])
    branch = own[...].astype(jnp.float32) + got.astype(jnp.float32) + bias[...]
    middle = tokens[...].astype(jnp.float32) + active[...] * branch
    middle_out[...] = middle
    normed, _ = normal_parts(middle)
    rows_out[...] = (normed * gain[...] + shift[...]).astype(rows_out.dtype)


def add_totals(totals, parts):
    first = pl.program_id(0) == 0
    for index, part in enumerate(parts):
        total = jnp.sum(part, axis=0, keepdims=True)
        totals[index : index + 1, :] = total + jnp.where(
            first, 0.0, totals[index : index + 1, :]
        )


def middle_back_kernel(
    start_ref,
    cotangent,
    middle,
    own,
    upper,
    lower,
    peer,
    active,
    gain,
    grad_out,
    branch_out,
    totals,
):
    in_upper = pl.program_id(0) < pl.num_programs(0) // 2
    got = jnp.where(in_upper, upper[...], lower[...])
    grad_second = own[...] + got.astype(jnp.float32) + peer[...].astype(jnp.float32)
    normed, scale = normal_parts(middle[...])
    grad_middle = cotangent[...].astype(jnp.float32) + normal_back(
        normed, scale, grad_second * gain[...]
    )
    grad_out[...] = grad_middle
    grad_branch = (active[...] * grad_middle).astype(jnp.bfloat16)
    branch_out[...] = grad_branch
    add_totals(
        totals, (grad_second * normed, grad_second, grad_branch.astype(jnp.float32))
    )


def first_back_kernel(start_ref, tokens, grad_middle, own, got, gain, grad_out, totals):
    grad_first = own[...] + got[...].astype(jnp.float32)
    normed, scale = normal_parts(tokens[...].astype(jnp.float32))
    grad = grad_middle[...] + normal_back(normed, scale, grad_first * gain[...])
    grad_out[...] = grad.astype(grad_out.dtype)
    add_totals(totals, (grad_first * normed, grad_first))


def by_rows(kernel, start, count, arrays, outs, name):
    width = arrays[0][0].shape[1]
    specs = {
        "rows": pl.BlockSpec((ROWS, width), lambda i, start_ref: (i, 0)),
        "from": pl.BlockSpec((ROWS, width), lambda i, start_ref: (start_ref[0] + i, 0)),
        "vector": pl.BlockSpec((1, width), lambda i, start_ref: (0, 0)),
        "totals": pl.BlockSpec((8, width), lambda i, start_ref: (0, 0)),
        "upper": pl.BlockSpec(
            (ROWS, width), lambda i, start_ref: (jnp.minimum(i, count // ROWS // 2 - 1), 0)
        ),
        "lower": pl.BlockSpec(
            (ROWS, width), lambda i, start_ref: (jnp.maximum(i - count // ROWS // 2, 0), 0)
        ),
        "flag": pl.BlockSpec((ROWS, 1), lambda i, start_ref: (i, 0)),
        "flag from": pl.BlockSpec((ROWS, 1), lambda i, start_ref: (start_ref[0] + i, 0)),
    }
    shapes = [
        jax.ShapeDtypeStruct((8 if kind == "totals" else count, width), dtype)
        for kind, dtype in outs
    ]
    moved = sum(
        count * width * array.dtype.itemsize for array, kind in arrays if kind in ("rows", "from")
    ) + sum(math.prod(shape.shape) * shape.dtype.itemsize for shape in shapes)
    return pl.pallas_call(
        kernel,
        grid_spec=pltpu.PrefetchScalarGridSpec(
            num_scalar_prefetch=1,
            grid=(count // ROWS,),
            in_specs=[specs[kind] for _, kind in arrays],
            out_specs=[specs[kind] for kind, _ in outs],
        ),
        out_shape=shapes,
        compiler_params=pltpu.CompilerParams(vmem_limit_bytes=48 << 20),
        cost_estimate=BRIEF,
        name=name,
    )(start, *[array for array, _ in arrays])


def after(value, *others):
    return lax.optimization_barrier((value, others))[0]


MIDDLE_KINDS = ("rows", "rows", "upper", "lower", "flag", "vector", "vector", "vector")
BACK_KINDS = ("from", "from", "rows", "upper", "lower", "rows", "flag from", "vector")


class Line:
    def __init__(self):
        self.last = None

    def __call__(self, function, *arrays):
        if self.last is not None:
            arrays = lax.optimization_barrier((arrays, self.last))[0]
        result = function(*arrays)
        self.last = jax.tree.leaves(result)[0]
        return result


def whole_sequence_device(
    tokens,
    exit_layer,
    first_gain,
    first_shift,
    query_weight,
    query_bias,
    key_weight,
    value_weight,
    value_bias,
    output_weight,
    output_bias,
    second_gain,
    second_shift,
    expand_weight,
    expand_bias,
    shrink_weight,
    shrink_bias,
    cotangent,
):
    seq_count, local_len, width = tokens.shape
    heads_rows = query_weight.shape[0]
    hidden_rows = expand_weight.shape[0]
    seq_size = lax.axis_size("seq")
    dp_size = lax.axis_size(DEVICES) // seq_size
    depth, core = lax.axis_index("seq"), lax.axis_index("core")
    along_x, along_y = lax.axis_index("x"), lax.axis_index("y")
    place = 2 * along_y + along_x
    dp = 2 * place + core
    parity = depth % 2
    full_len = local_len * seq_size
    half_len = full_len // 2
    f32, low = jnp.float32, jnp.bfloat16

    def route(flip):
        pairs = []
        for i in range(dp_size):
            for j in range(seq_size):
                target = 2 * (i % 2) + (j % 2 if not flip else 1 - j % 2)
                pairs.append((i * seq_size + j, (i // 2 * 2 + j // 2) * seq_size + target))
        return pairs

    def send(first, second, back):
        routes = [[(b, a) if back else (a, b) for a, b in route(flip)] for flip in (False, True)]
        return lax.ppermute(first, DEVICES, routes[0]), lax.ppermute(second, DEVICES, routes[1])

    def by_parity(values):
        return pick(parity, values[0], values[1]), pick(parity, values[1], values[0])

    def paired(first, second):
        return ordered(parity, first[None], second[None], 0)

    def by_core(own, other):
        return ordered(core, own, other, 0)

    def half_rows(matrix, which):
        return lax.dynamic_slice_in_dim(matrix, which * half_len, half_len, 0)

    line = Line()
    depth_rows = heads_rows * seq_size
    hidden_block = hidden_rows * seq_size
    places = [place ^ d for d in range(4)]
    sides = [core, 1 - core]
    bits = jnp.stack([along_y, along_x, core])

    def through_z(shard):
        return lax.all_gather(shard, "seq", axis=0, tiled=True)

    devices = dp_size * seq_size
    all_dp = jnp.arange(dp_size, dtype=jnp.int32)[:, None]
    all_seq = jnp.arange(seq_size, dtype=jnp.int32)[None, :]
    relative = ((all_dp ^ dp) * seq_size + (depth - all_seq) % seq_size).reshape(-1)

    def shift_z(values, steps):
        return lax.ppermute(
            values, "seq", [(i, (i + steps) % seq_size) for i in range(seq_size)]
        )

    def stacked(own, other):
        return jnp.concatenate([own, other], 0)

    vectors = [first_gain, first_shift, query_bias, value_bias, output_bias, second_gain]
    vectors += [second_shift, shrink_bias, expand_bias]
    shard_a = line(
        lambda *parts: jnp.concatenate(parts, 0),
        query_weight,
        key_weight,
        value_weight,
        output_weight,
    )
    z_a = through_z(shard_a)
    vectors = line(lambda *parts: jnp.concatenate(parts)[None, None], *vectors)
    shifted = [shift_z(vectors, steps) for steps in range(1, seq_size)]
    alive = (exit_layer > LAYER).astype(low)
    flag_rows = jnp.broadcast_to(alive[:, None, :], (seq_count, 16, local_len))
    flag_rows = jnp.pad(flag_rows, ((0, 0), (0, 0), (0, width - local_len)))
    message = line(
        lambda *arrays: by_parity(jnp.concatenate(arrays, axis=1)), tokens, flag_rows, cotangent
    )
    vectors = line(lambda *parts: jnp.concatenate(parts, 1), vectors, *shifted)
    mine, theirs = line(lambda rows: split_columns(core, rows, hidden_block), shrink_weight)
    theirs = swap(theirs, CORE)
    vectors = line(stacked, vectors, swap(vectors, ALONG_Y))
    shard_shrink = line(stacked, mine, theirs)
    mine, theirs = line(lambda rows: split_columns(along_x, rows, hidden_block), shard_shrink)
    theirs = swap(theirs, ALONG_X)
    vectors = line(stacked, vectors, swap(vectors, ALONG_X))
    shard_shrink = line(stacked, mine, theirs)
    vectors = line(stacked, vectors, swap(vectors, CORE))
    vectors = line(
        lambda rows: rows.reshape(2, 2, 2, seq_size, -1)
        .transpose(2, 1, 0, 3, 4)
        .reshape(devices, -1)[relative]
        .astype(f32),
        vectors,
    )
    shrink_across = swap(shard_shrink, ALONG_Y)

    def vector(index):
        return vectors[:, index * heads_rows : (index + 1) * heads_rows].reshape(1, -1)

    def of_core(matrix):
        cut = matrix.reshape(4, 2, seq_size, -1)
        return lax.dynamic_index_in_dim(cut, core, 1, False).reshape(4 * seq_size, -1)

    def of_quarter(matrix):
        cut = matrix.reshape(2, 4, seq_size, -1)
        return lax.dynamic_index_in_dim(cut, 2 * along_x + core, 1, False)

    gain_one, shift_one = vector(0), vector(1)
    bias_query = of_core(vectors[:, 2 * heads_rows : 3 * heads_rows])
    bias_value = of_core(vectors[:, 3 * heads_rows : 4 * heads_rows])
    bias_rows = jnp.stack([bias_query, jnp.zeros_like(bias_query), bias_value], 1).reshape(1, -1)
    bias_out, gain_two, shift_two, bias_shrink = vector(4), vector(5), vector(6), vector(7)
    bias_expand = of_quarter(vectors[:, 8 * heads_rows :]).reshape(1, -1)

    half_qkv = 3 * depth_rows // 2

    def cut_a(rows):
        cut = rows.reshape(seq_size, -1, width)
        return (
            cut[:, : 3 * heads_rows].reshape(-1, width),
            cut[:, 3 * heads_rows :].reshape(-1, width),
        )

    arrived = send(*(after(part, z_a) for part in message), False)
    z_qkv, z_out = line(cut_a, z_a)
    beside_qkv, across_qkv = swap(z_qkv, ALONG_X), swap(z_qkv, ALONG_Y)
    mine, theirs = line(lambda rows: split_columns(core, rows, depth_rows), z_out)
    rows_out = line(
        lambda own, other: jnp.concatenate([own, other], 1), mine, swap(theirs, CORE)
    )
    upper = line(lambda rows: rows[:half_qkv], beside_qkv)
    lower = line(lambda rows: rows[half_qkv:], across_qkv)
    upper, lower = swap(upper, ALONG_Y), swap(lower, ALONG_X)
    half = line(paired, *arrived)
    z_expand = through_z(after(expand_weight, half))
    joined = line(by_core, half, swap(half, CORE))
    inputs = joined[:, :local_len].reshape(full_len, width)
    alive = joined[:, local_len, :local_len].reshape(full_len, 1)
    cotangent_full = joined[:, local_len + 16 :].reshape(full_len, width)
    active = alive.astype(f32)
    mask = jnp.broadcast_to((alive - 1) * jnp.bfloat16(1e30), (full_len, HEAD_DIM))

    no_start = jnp.zeros((1,), jnp.int32)
    half_start = (core * (half_len // ROWS)).reshape(1)

    grad_shrunk = line(
        lambda flags, grads: (flags * grads.astype(f32)).astype(low), active, cotangent_full
    )
    sent_gs = line(lambda rows: half_rows(rows, core), grad_shrunk)
    gs_got = swap(sent_gs, ALONG_X)
    (first_rows,) = line(
        lambda *arrays: by_rows(
            first_kernel,
            no_start,
            full_len,
            list(zip(arrays, ("rows", "vector", "vector"))),
            [("rows", low)],
            "first_norm",
        ),
        inputs,
        gain_one,
        shift_one,
    )
    w_qkv = line(
        lambda *pieces: arrange(
            pieces,
            (half_qkv, width),
            [(p, r, 0) for p in range(3) for r in range(2)] + [(3, 0, 0), (4, 0, 0)],
            [2 * places[d] + r for d in range(4) for r in range(2)],
        ),
        z_qkv,
        beside_qkv,
        across_qkv,
        upper,
        lower,
    )
    rows_out = after(rows_out, w_qkv)
    out_beside, out_across = swap(rows_out, ALONG_X), swap(rows_out, ALONG_Y)
    across_expand = swap(z_expand, ALONG_Y)

    qkv = line(
        lambda rows, weight: multiply((rows,), (weight,), True, bias=bias_rows), first_rows, w_qkv
    )
    out_corner = swap(line(lambda rows: rows * jnp.bfloat16(1), out_across), ALONG_X)
    mixed = line(attend, qkv, mask)
    w_out = line(
        lambda *pieces: arrange(
            pieces,
            (depth_rows, width // 2),
            [(p, 0, i) for p in range(4) for i in range(2)],
            [2 * places[d] + sides[i] for d in range(4) for i in range(2)],
        ),
        after(rows_out, z_expand),
        out_beside,
        out_across,
        out_corner,
    )
    branch = line(lambda rows, weight: multiply((rows,), (weight,), True), mixed, w_out)
    branch_got = [swap(part, CORE) for part in jnp.split(branch, 2)]
    shard_shrink = line(stacked, shard_shrink, shrink_across)
    w_shrink = through_z(after(shard_shrink, z_expand, branch))
    middle, second_rows = line(
        lambda *arrays: by_rows(
            middle_kernel,
            no_start,
            full_len,
            list(zip(arrays, MIDDLE_KINDS)),
            [("rows", f32), ("rows", low)],
            "middle_norm",
        ),
        inputs,
        branch,
        *branch_got,
        active,
        bias_out,
        gain_two,
        shift_two,
    )
    second_half = line(lambda rows: half_rows(rows, core), second_rows)
    second_got = swap(second_half, ALONG_X)
    gs_own = line(lambda rows: regroup(bits, rows, seq_size), grad_shrunk)
    w_expand = line(
        lambda *pieces: arrange(
            pieces,
            (hidden_block // 2, width),
            [(p, r, 0) for p in range(2) for r in range(2)],
            [2 * (along_y ^ p) + r for p in range(2) for r in range(2)],
        ),
        z_expand,
        across_expand,
    )

    def lift(rows, weight):
        return multiply((rows,), (weight,), True, bias=bias_expand, lift=True)

    activated, slope = line(lift, second_rows, w_expand)
    second_peer = line(by_core, second_got, swap(second_got, CORE))
    activated_peer, slope_peer = line(lift, second_peer, w_expand)

    gs_peer = line(by_core, gs_got, swap(gs_got, CORE))
    gs_peer = line(lambda rows: regroup(bits, rows, seq_size), gs_peer)
    def scatter_z(total):
        return lax.psum_scatter(total, "seq", scatter_dimension=0, tiled=True)

    def units(grads, weight, slopes):
        return multiply((grads,), (weight,), False, slope=slopes)

    def their_half(left, weight, by_columns=False):
        return half_dot(1 - core, left, weight, by_columns, low)

    def my_half(left, weight, by_columns=False):
        return half_dot(core, left, weight, by_columns, f32)

    def add_rounded(left, right):
        return (left.astype(f32) + right.astype(f32)).astype(low)

    shrink_part = line(
        lambda own, peer, rows, rows_peer: outer_rows_of(
            (own, peer), (rows, rows_peer), width // 2, range(2)
        ),
        gs_own,
        gs_peer,
        activated,
        activated_peer,
    )
    shrink_rows = scatter_z(shrink_part)
    grad_pre_peer, peer_sums = line(units, gs_peer, w_shrink, slope_peer)
    theirs = line(their_half, grad_pre_peer, w_expand)
    mine = line(my_half, grad_pre_peer, w_expand)
    peer_half = line(add_rounded, mine, swap(theirs, CORE))
    second_from_peer = swap(peer_half, ALONG_X)
    grad_pre, own_sums = line(units, gs_own, w_shrink, slope)
    theirs = line(their_half, grad_pre, w_expand)
    second_got = [swap(part, CORE) for part in jnp.split(theirs, 2)]
    second_mine = line(my_half, grad_pre, w_expand)
    def expand_part(d):
        return line(
            lambda *arrays: outer_rows_of(arrays[:2], arrays[2:], hidden_block, [along_y ^ d]),
            grad_pre,
            grad_pre_peer,
            second_rows,
            second_peer,
        )

    expand_across = expand_part(1)
    expand_got = swap(expand_across, ALONG_Y)

    grad_middle, grad_branch_half, middle_totals = line(
        lambda *arrays: by_rows(
            middle_back_kernel,
            half_start,
            half_len,
            list(zip(arrays, BACK_KINDS)),
            [("rows", f32), ("rows", low), ("totals", f32)],
            "middle_norm_back",
        ),
        cotangent_full,
        middle,
        second_mine,
        *second_got,
        second_from_peer,
        active,
        gain_two,
    )
    branch_got = swap(grad_branch_half, CORE)

    grad_branch = line(by_core, grad_branch_half, branch_got)
    grad_mixed = line(
        lambda grads, weight: multiply((grads,), (weight,), False, tile=256), grad_branch, w_out
    )
    out_part = line(
        lambda grads, rows: outer_sides(
            [2 * places[d] + sides[i] for d in range(4) for i in range(2)], grads, rows, depth_rows
        ),
        grad_branch,
        mixed,
    )
    out_parts = [out_part[d] for d in range(4)]
    out_corner = swap(out_parts[3], ALONG_X)
    out_got_x = swap(out_parts[1], ALONG_X)

    def attend_piece(d):
        return line(
            lambda rows, grads, flags: attend_back(rows, grads, flags, places[d]),
            qkv,
            grad_mixed,
            mask,
        )

    def qkv_part(d, rows, source):
        return line(
            lambda grads, inputs_low: outer_rows_of((grads,), (inputs_low,), rows, [source]),
            grad_qkv[d],
            first_rows,
        )

    grad_qkv = {3: attend_piece(3)}
    corner_got = swap(qkv_part(3, 2 * half_qkv, 0), ALONG_X)
    grad_qkv[1] = attend_piece(1)
    qkv_x = swap(qkv_part(1, 2 * half_qkv, 0), ALONG_X)
    grad_qkv[2] = attend_piece(2)
    across = qkv_part(2, 2 * half_qkv, 0)
    expand_here = expand_part(0)
    qkv_y = swap(line(add_rounded, across, corner_got), ALONG_Y)
    expand_sum = line(add_rounded, expand_here, expand_got)
    expand_rows = scatter_z(expand_sum)
    grad_qkv[0] = attend_piece(0)
    here = qkv_part(0, 2 * half_qkv, 0)
    grads_qkv = tuple(grad_qkv[d] for d in range(4))

    def first_half(which, dtype):
        return lambda *arrays: half_dot(which, arrays[:4], arrays[4], False, dtype, places=places)

    peer_theirs = line(
        lambda rows, weight: their_half(rows, weight, True), activated_peer, w_shrink
    )
    peer_got = swap(peer_theirs, CORE)
    first_theirs = line(first_half(1 - core, low), *grads_qkv, w_qkv)
    first_got = swap(first_theirs, CORE)
    peer_mine = line(lambda rows, weight: my_half(rows, weight, True), activated_peer, w_shrink)
    first_mine = line(first_half(core, f32), *grads_qkv, w_qkv)
    qkv_sum = line(
        lambda *parts: sum(part.astype(f32) for part in parts).astype(low), here, qkv_x, qkv_y
    )
    qkv_rows = scatter_z(qkv_sum)
    grad_half, first_totals = line(
        lambda *arrays: by_rows(
            first_back_kernel,
            half_start,
            half_len,
            list(zip(arrays, ("from", "rows", "rows", "rows", "vector"))),
            [("rows", low), ("totals", f32)],
            "first_norm_back",
        ),
        inputs,
        grad_middle,
        first_mine,
        first_got,
        gain_one,
    )
    tokens_parts = send(
        *line(lambda rows: by_parity(rows.reshape(2, local_len, width)), grad_half), True
    )

    def column_sum(matrix):
        return jnp.sum(matrix.astype(f32), axis=0)

    def all_devices(totals, rows):
        return totals.reshape(devices, rows)

    def core_devices(totals, rows):
        cut = totals.reshape(4, 1, seq_size, rows)
        return ordered(core, cut, jnp.zeros_like(cut), 1).reshape(devices, rows)

    def quarter_devices(totals, rows):
        cut = totals.reshape(2, 1, seq_size, rows)
        none = jnp.zeros_like(cut)
        quarters = [jnp.where(2 * along_x + core == q, cut, none) for q in range(4)]
        return jnp.concatenate(quarters, 1).reshape(devices, rows)

    def all_sums(first, middle_sums, shrunk_grads, own, peer, *grads):
        qkv_sums = jnp.stack([column_sum(part) for part in grads])[jnp.stack(places)]
        qkv_sums = qkv_sums.reshape(4 * seq_size, 3, heads_rows)
        sums = jnp.concatenate(
            [
                all_devices(first[0], heads_rows),
                all_devices(first[1], heads_rows),
                core_devices(qkv_sums[:, 0], heads_rows),
                core_devices(qkv_sums[:, 2], heads_rows),
                all_devices(middle_sums[2], heads_rows),
                all_devices(middle_sums[0], heads_rows),
                all_devices(middle_sums[1], heads_rows),
                all_devices(0.5 * column_sum(shrunk_grads), heads_rows),
                quarter_devices(own + peer, hidden_rows),
            ],
            axis=1,
        )
        return sums.reshape(dp_size, seq_size, -1)[jnp.arange(dp_size) ^ dp]

    def fold(values, got):
        return values[: got.shape[0]] + got

    sums = line(
        all_sums, first_totals, middle_totals, grad_shrunk, own_sums, peer_sums, *grads_qkv
    )
    out_got_y = swap(line(add_rounded, out_parts[2], out_corner), ALONG_Y)
    sums = line(fold, sums, swap(sums[dp_size // 2 :], ALONG_Y))
    sums = line(fold, sums, swap(sums[dp_size // 4 :], ALONG_X))
    sums = line(fold, sums, swap(sums[dp_size // 8 :], CORE))

    to_peer = line(
        lambda *parts: regroup_back(bits, *parts, seq_size, low), peer_mine, peer_got
    )
    from_peer = swap(to_peer, ALONG_X)
    out_sum = line(
        lambda *parts: sum(part.astype(f32) for part in parts).astype(low),
        out_parts[0],
        out_got_x,
        out_got_y,
    )
    out_got = swap(line(lambda rows: rows[:, width // 2 :], out_sum), CORE)
    theirs = line(lambda rows, weight: their_half(rows, weight, True), activated, w_shrink)
    shrunk_got = swap(theirs, CORE)
    out_rows = line(
        lambda rows, got: weave_columns(core, rows[:, : width // 2], got, depth_rows),
        out_sum,
        out_got,
    )

    def with_vectors(totals, rows):
        totals = totals.reshape(seq_size, 1, -1).astype(low)
        totals = jnp.pad(totals, ((0, 0), (0, 15), (0, width - totals.shape[2])))
        rows = jnp.concatenate([rows.reshape(seq_size, -1, width), totals], 1)
        return rows.reshape(-1, width)

    out_rows = scatter_z(line(with_vectors, sums, out_rows))
    mine = line(lambda rows, weight: my_half(rows, weight, True), activated, w_shrink)
    shrunk = line(lambda *parts: regroup_back(bits, *parts, seq_size, f32), mine, shrunk_got)

    def finish(part, peer, rows, flags, bias):
        total = part + peer.astype(f32) + bias
        out = half_rows(rows, core) + half_rows(flags, core) * total
        return by_parity(out.astype(low).reshape(2, local_len, width))

    out_halves = send(*line(finish, shrunk, from_peer, middle, active, bias_shrink), True)

    half = shrink_rows.shape[0] // 2
    shrink_got = swap(line(lambda rows: rows[half:], shrink_rows), ALONG_Y)
    expand_weight_grad = line(lambda rows: rows.astype(f32), expand_rows)
    tokens_grad = line(paired, *tokens_parts)
    shrink_rows = line(lambda rows, got: add_rounded(rows[:half], got), shrink_rows, shrink_got)
    half = half // 2
    shrink_got = swap(line(lambda rows: rows[half:], shrink_rows), ALONG_X)
    qkv_weight_grad = line(lambda rows: rows.astype(f32), qkv_rows)
    shrink_rows = line(
        lambda rows, got: weave_columns(along_x, rows[:half], got, hidden_block),
        shrink_rows,
        shrink_got,
    )
    shrink_got = swap(line(lambda rows: rows[heads_rows:], shrink_rows), CORE)
    shrink_weight_grad = line(
        lambda rows, got: weave_columns(core, rows[:heads_rows], got, hidden_block).astype(f32),
        shrink_rows,
        shrink_got,
    )
    output_weight_grad, sums = line(
        lambda rows: (
            rows[:heads_rows].astype(f32),
            rows[heads_rows, : 8 * heads_rows + hidden_rows].astype(f32),
        ),
        out_rows,
    )
    layer_out = line(paired, *out_halves)

    def vector_grad(index):
        return sums[index * heads_rows : (index + 1) * heads_rows]

    return (
        layer_out,
        tokens_grad,
        vector_grad(0),
        vector_grad(1),
        qkv_weight_grad[:heads_rows],
        vector_grad(2),
        qkv_weight_grad[heads_rows : 2 * heads_rows],
        qkv_weight_grad[2 * heads_rows :],
        vector_grad(3),
        output_weight_grad,
        vector_grad(4),
        vector_grad(5),
        vector_grad(6),
        expand_weight_grad,
        sums[8 * heads_rows :],
        shrink_weight_grad,
        vector_grad(7),
    )


def general_device(
    tokens,
    exit_layer,
    first_gain,
    first_shift,
    query_weight,
    query_bias,
    key_weight,
    value_weight,
    value_bias,
    output_weight,
    output_bias,
    second_gain,
    second_shift,
    expand_weight,
    expand_bias,
    shrink_weight,
    shrink_bias,
    cotangent,
):
    seq_count, local_len, width = tokens.shape
    hidden_width = shrink_weight.shape[1]
    total_rows = seq_count * local_len
    heads = width // HEAD_DIM
    inputs = tokens.reshape(total_rows, width).astype(jnp.float32)
    active = (exit_layer > LAYER).astype(jnp.float32).reshape(total_rows, 1)
    gain_one, shift_one = (
        lax.all_gather(first_gain, ("dp", "seq"), axis=0, tiled=True),
        lax.all_gather(first_shift, ("dp", "seq"), axis=0, tiled=True),
    )
    gain_one = gain_one.astype(jnp.float32)
    shift_one = shift_one.astype(jnp.float32)
    normed_in = normalize(inputs)
    first_rows = (normed_in * gain_one + shift_one).astype(jnp.bfloat16)
    blank = jnp.zeros((total_rows, width), jnp.bfloat16)
    attention_init = (blank, blank, blank) + ()
    w_query = lax.all_gather(query_weight, ("dp", "seq"), axis=0, tiled=True)
    b_query = lax.all_gather(query_bias, ("dp", "seq"), axis=0, tiled=True)
    w_key = lax.all_gather(key_weight, ("dp", "seq"), axis=0, tiled=True)
    w_value = lax.all_gather(value_weight, ("dp", "seq"), axis=0, tiled=True)
    b_value = lax.all_gather(value_bias, ("dp", "seq"), axis=0, tiled=True)
    queries = place_cols(
        attention_init[0], project(first_rows, w_query) + b_query.astype(jnp.float32)
    )
    key_rows = place_cols(attention_init[1], project(first_rows, w_key))
    value_rows = place_cols(
        attention_init[2], project(first_rows, w_value) + b_value.astype(jnp.float32)
    )
    stored = attention_init[3:]
    gathered = (queries, key_rows, value_rows) + stored
    queries, key_rows, value_rows = (gathered[0], gathered[1], gathered[2])
    query_local = queries.reshape(seq_count, local_len, width)
    key_local = key_rows.reshape(seq_count, local_len, width)
    value_local = value_rows.reshape(seq_count, local_len, width)
    alive_local = active.reshape(seq_count, local_len)
    key_all, value_all, alive_all = (
        lax.all_gather(key_local, "seq", axis=1, tiled=True),
        lax.all_gather(value_local, "seq", axis=1, tiled=True),
        lax.all_gather(alive_local.astype(jnp.bfloat16), "seq", axis=1, tiled=True),
    )
    full_len = key_all.shape[1]
    offset = lax.axis_index("seq") * local_len
    query_pos = offset + jnp.arange(local_len, dtype=jnp.int32)
    key_pos = jnp.arange(full_len, dtype=jnp.int32)
    causal = key_pos[None, :] <= query_pos[:, None]
    allowed = causal[None, None] & (alive_all.astype(jnp.float32)[:, None, None, :] > 0.5)
    factor = HEAD_DIM ** (-0.5)
    group = min(8, heads)
    group_width = group * HEAD_DIM
    group_total = heads // group

    def group_parts(start_col):
        q_part = lax.dynamic_slice_in_dim(query_local, start_col, group_width, 2).reshape(
            seq_count, local_len, group, HEAD_DIM
        )
        k_part = lax.dynamic_slice_in_dim(key_all, start_col, group_width, 2).reshape(
            seq_count, full_len, group, HEAD_DIM
        )
        v_part = lax.dynamic_slice_in_dim(value_all, start_col, group_width, 2).reshape(
            seq_count, full_len, group, HEAD_DIM
        )
        scores = (
            jnp.einsum("sqhd,skhd->shqk", q_part, k_part, preferred_element_type=jnp.float32)
            * factor
        )
        scores = jnp.where(allowed, scores, jnp.float32(-1e30))
        return (q_part, k_part, v_part, scores)

    def forward_group(group_index, state):
        mixed_all, log_total = state
        start_col = group_index * group_width
        q_part, k_part, v_part, scores = group_parts(start_col)
        row_max = jnp.max(scores, axis=-1, keepdims=True)
        raised = jnp.exp(scores - row_max)
        totals = jnp.sum(raised, axis=-1, keepdims=True)
        weights_low = (raised / totals).astype(jnp.bfloat16)
        outcome = jnp.einsum(
            "shqk,skhd->sqhd", weights_low, v_part, preferred_element_type=jnp.float32
        )
        mixed_all = lax.dynamic_update_slice_in_dim(
            mixed_all,
            outcome.reshape(seq_count, local_len, group_width).astype(jnp.bfloat16),
            start_col,
            2,
        )
        log_total = lax.dynamic_update_slice_in_dim(
            log_total, (row_max + jnp.log(totals))[..., 0], group_index * group, 1
        )
        return (mixed_all, log_total)

    mixed_all, log_total = lax.fori_loop(
        0,
        group_total,
        forward_group,
        (
            jnp.zeros((seq_count, local_len, width), jnp.bfloat16),
            jnp.zeros((seq_count, heads, local_len), jnp.float32),
        ),
    )
    mixed = mixed_all.reshape(total_rows, width)
    vector_blank = jnp.zeros((width,), jnp.bfloat16)
    output_init = (jnp.zeros((total_rows, width), jnp.float32), vector_blank, vector_blank) + ()
    w_out = lax.all_gather(output_weight, ("dp", "seq"), axis=0, tiled=True)
    b_out = lax.all_gather(output_bias, ("dp", "seq"), axis=0, tiled=True)
    g_piece = lax.all_gather(second_gain, ("dp", "seq"), axis=0, tiled=True)
    s_piece = lax.all_gather(second_shift, ("dp", "seq"), axis=0, tiled=True)
    branch = place_cols(output_init[0], project(mixed, w_out) + b_out.astype(jnp.float32))
    gain_two = g_piece
    shift_two = s_piece
    stored = output_init[3:]
    folded = (branch, gain_two, shift_two) + stored
    branch = folded[0]
    gain_two = folded[1].astype(jnp.float32)
    shift_two = folded[2].astype(jnp.float32)
    middle = inputs + active * branch
    normed_mid = normalize(middle)
    second_rows = (normed_mid * gain_two + shift_two).astype(jnp.bfloat16)
    expand_init = (jnp.zeros((total_rows, hidden_width), jnp.float32),) + ()
    w_expand = lax.all_gather(expand_weight, ("dp", "seq"), axis=0, tiled=True)
    b_expand = lax.all_gather(expand_bias, ("dp", "seq"), axis=0, tiled=True)
    hidden_pre = place_cols(
        expand_init[0], project(second_rows, w_expand) + b_expand.astype(jnp.float32)
    )
    stored = expand_init[1:]
    expanded = (hidden_pre,) + stored
    hidden_pre = expanded[0]

    def gelu_exact(pre_values):
        return jax.nn.gelu(pre_values, approximate=False)

    activated_full, gelu_back = jax.vjp(gelu_exact, hidden_pre)
    activated = activated_full.astype(jnp.bfloat16)
    shrink_init = (jnp.zeros((total_rows, width), jnp.float32),) + ()
    w_shrink = lax.all_gather(shrink_weight, ("dp", "seq"), axis=0, tiled=True)
    b_shrink = lax.all_gather(shrink_bias, ("dp", "seq"), axis=0, tiled=True)
    shrunk = place_cols(shrink_init[0], project(activated, w_shrink) + b_shrink.astype(jnp.float32))
    stored = shrink_init[1:]
    shrunk_all = (shrunk,) + stored
    shrunk = shrunk_all[0]
    layer_out = (middle + active * shrunk).astype(jnp.bfloat16).reshape(seq_count, local_len, width)
    grad_out = cotangent.reshape(total_rows, width).astype(jnp.float32)
    grad_shrunk = (active * grad_out).astype(jnp.bfloat16)
    grad_units = through(
        grad_shrunk, lax.all_gather(shrink_weight, ("dp", "seq"), axis=0, tiled=True)
    )
    grad_pre = gelu_back(grad_units)[0].astype(jnp.bfloat16)
    grad_second = through(
        grad_pre, lax.all_gather(expand_weight, ("dp", "seq"), axis=0, tiled=True)
    )
    mid_value, mid_back = jax.vjp(normalize, middle)
    grad_middle = grad_out + mid_back(grad_second * gain_two)[0]
    grad_branch = (active * grad_middle).astype(jnp.bfloat16)
    grad_mixed = through(
        grad_branch, lax.all_gather(output_weight, ("dp", "seq"), axis=0, tiled=True)
    )
    grad_mixed_local = grad_mixed.astype(jnp.bfloat16).reshape(seq_count, local_len, width)

    def backward_group(group_index, state):
        grad_query_all, grad_key_all, grad_value_all = state
        start_col = group_index * group_width
        q_part, k_part, v_part, scores = group_parts(start_col)
        g_part = lax.dynamic_slice_in_dim(grad_mixed_local, start_col, group_width, 2).reshape(
            seq_count, local_len, group, HEAD_DIM
        )
        lse_part = lax.dynamic_slice_in_dim(log_total, group_index * group, group, 1)
        soft = jnp.exp(scores - lse_part[..., None])
        grad_probs = jnp.einsum(
            "sqhd,skhd->shqk", g_part, v_part, preferred_element_type=jnp.float32
        )
        value_term = jnp.einsum(
            "shqk,sqhd->skhd", soft.astype(jnp.bfloat16), g_part, preferred_element_type=jnp.float32
        )
        centered = jnp.sum(soft * grad_probs, axis=-1, keepdims=True)
        grad_scores = (soft * (grad_probs - centered)).astype(jnp.bfloat16)
        query_term = (
            jnp.einsum("shqk,skhd->sqhd", grad_scores, k_part, preferred_element_type=jnp.float32)
            * factor
        )
        key_term = (
            jnp.einsum("shqk,sqhd->skhd", grad_scores, q_part, preferred_element_type=jnp.float32)
            * factor
        )
        grad_query_all = lax.dynamic_update_slice_in_dim(
            grad_query_all, query_term.reshape(seq_count, local_len, group_width), start_col, 2
        )
        grad_key_all = lax.dynamic_update_slice_in_dim(
            grad_key_all, key_term.reshape(seq_count, full_len, group_width), start_col, 2
        )
        grad_value_all = lax.dynamic_update_slice_in_dim(
            grad_value_all, value_term.reshape(seq_count, full_len, group_width), start_col, 2
        )
        return (grad_query_all, grad_key_all, grad_value_all)

    grad_query_all, grad_key_all, grad_value_all = lax.fori_loop(
        0,
        group_total,
        backward_group,
        (
            jnp.zeros((seq_count, local_len, width), jnp.float32),
            jnp.zeros((seq_count, full_len, width), jnp.float32),
            jnp.zeros((seq_count, full_len, width), jnp.float32),
        ),
    )
    key_sum, value_sum = (
        lax.psum_scatter(grad_key_all, "seq", scatter_dimension=1, tiled=True),
        lax.psum_scatter(grad_value_all, "seq", scatter_dimension=1, tiled=True),
    )
    grad_query = grad_query_all.astype(jnp.bfloat16).reshape(total_rows, width)
    grad_key = key_sum.astype(jnp.bfloat16).reshape(total_rows, width)
    grad_value = value_sum.astype(jnp.bfloat16).reshape(total_rows, width)
    total = through(grad_query, lax.all_gather(query_weight, ("dp", "seq"), axis=0, tiled=True))
    total = total + through(grad_key, lax.all_gather(key_weight, ("dp", "seq"), axis=0, tiled=True))
    grad_first = total + through(
        grad_value, lax.all_gather(value_weight, ("dp", "seq"), axis=0, tiled=True)
    )
    in_value, in_back = jax.vjp(normalize, inputs)
    tokens_grad = (
        (grad_middle + in_back(grad_first * gain_one)[0])
        .astype(jnp.bfloat16)
        .reshape(seq_count, local_len, width)
    )
    first_scaled = grad_first * normed_in
    second_scaled = grad_second * normed_mid
    vectors = jnp.stack(
        [
            column_total(grad_query),
            column_total(grad_value),
            column_total(grad_branch),
            column_total(grad_shrunk),
            column_total(first_scaled),
            column_total(grad_first),
            column_total(second_scaled),
            column_total(grad_second),
        ],
        axis=1,
    )

    def scattered(grad_cols, inputs):
        return lax.psum_scatter(
            outer_rows(grad_cols, inputs), ("dp", "seq"), scatter_dimension=0, tiled=True
        )

    vector_sums = lax.psum_scatter(vectors, ("dp", "seq"), scatter_dimension=0, tiled=True)
    expand_bias_sums = lax.psum_scatter(
        column_total(grad_pre), ("dp", "seq"), scatter_dimension=0, tiled=True
    )
    shrink_sums = scattered(grad_shrunk, activated)
    grad_pre, second_rows, shrink_sums = lax.optimization_barrier(
        (grad_pre, second_rows, shrink_sums)
    )
    expand_sums = scattered(grad_pre, second_rows)
    grad_branch, grad_query, grad_key, grad_value, expand_sums = lax.optimization_barrier(
        (grad_branch, grad_query, grad_key, grad_value, expand_sums)
    )
    return (
        layer_out,
        tokens_grad,
        vector_sums[:, 4],
        vector_sums[:, 5],
        scattered(grad_query, first_rows),
        vector_sums[:, 0],
        scattered(grad_key, first_rows),
        scattered(grad_value, first_rows),
        vector_sums[:, 1],
        scattered(grad_branch, mixed),
        vector_sums[:, 2],
        vector_sums[:, 6],
        vector_sums[:, 7],
        expand_sums,
        expand_bias_sums,
        shrink_sums,
        vector_sums[:, 3],
    )


def solution(mesh):
    chips = mesh.shape["dp"] // 2
    if chips == 4 and mesh.shape["seq"] == 4:
        names = ("y", "x", "core", "seq")
        mesh = Mesh(mesh.devices.reshape(2, 2, 2, 4), names)
        dp, rows, per_device = names[:3], names, whole_sequence_device
    else:
        dp, rows, per_device = "dp", ("dp", "seq"), general_device
    in_specs = (
        P(dp, "seq", None),
        P(dp, "seq"),
        P(rows),
        P(rows),
        P(rows, None),
        P(rows),
        P(rows, None),
        P(rows, None),
        P(rows),
        P(rows, None),
        P(rows),
        P(rows),
        P(rows),
        P(rows, None),
        P(rows),
        P(rows, None),
        P(rows),
        P(dp, "seq", None),
    )
    out_specs = (
        P(dp, "seq", None),
        P(dp, "seq", None),
        P(rows),
        P(rows),
        P(rows, None),
        P(rows),
        P(rows, None),
        P(rows, None),
        P(rows),
        P(rows, None),
        P(rows),
        P(rows),
        P(rows),
        P(rows, None),
        P(rows),
        P(rows, None),
        P(rows),
    )
    return jax.shard_map(
        per_device, mesh=mesh, in_specs=in_specs, out_specs=out_specs, check_vma=False
    )
```

```python
import math

import jax
import jax.numpy as jnp
from jax import lax
from jax.experimental import pallas as pl
from jax.experimental.pallas import tpu as pltpu
from jax.sharding import Mesh, PartitionSpec as P

HEAD_DIM = 64
LAYER = 12


EPS = 1e-05


def normalize(values):
    center = values - jnp.mean(values, axis=-1, keepdims=True)
    spread = jnp.mean(center * center, axis=-1, keepdims=True)
    return center * lax.rsqrt(spread + EPS)


def project(left, weight):
    return lax.dot_general(
        left, weight, (((1,), (1,)), ((), ())), preferred_element_type=jnp.float32
    )


def through(left, weight):
    return jnp.dot(left, weight, preferred_element_type=jnp.float32)


def outer_rows(grad_cols, inputs):
    return lax.dot_general(
        grad_cols, inputs, (((0,), (0,)), ((), ())), preferred_element_type=jnp.float32
    )


def place_cols(buffer, piece):
    return piece.astype(buffer.dtype)


def column_total(matrix):
    return jnp.sum(matrix, axis=0, dtype=jnp.float32)


BRIEF = pl.CostEstimate(flops=1, bytes_accessed=1, transcendentals=0)

CORE, ALONG_X, ALONG_Y = "core", "x", "y"
DEVICES = ("y", "x", "core", "seq")


def swap(values, axis):
    return lax.ppermute(values, axis, [(0, 1), (1, 0)])


def pick(flag, first, second):
    return jnp.where(flag == 0, first, second)


def ordered(flag, own, other, axis):
    return pick(
        flag, jnp.concatenate([own, other], axis), jnp.concatenate([other, own], axis)
    )


def arrange(pieces, block, sources, targets):
    count = len(pieces)
    steps = len(sources)
    table = jnp.stack([jnp.asarray(target, jnp.int32) for target in targets])

    def kernel(table_ref, *refs):
        step = pl.program_id(0)
        for index in range(count):
            mine = [at for at, source in enumerate(sources) if source[0] == index]

            @pl.when((step >= mine[0]) & (step <= mine[-1]))
            def _():
                refs[count][...] = refs[index][...]

    def place_of(index):
        mine = [at for at, source in enumerate(sources) if source[0] == index]

        def block_of(step, table_ref):
            row, column = sources[mine[0]][1:]
            for at in mine[1:]:
                row = jnp.where(step >= at, sources[at][1], row)
                column = jnp.where(step >= at, sources[at][2], column)
            return row, column

        return block_of

    total = steps * block[0] * block[1]
    return pl.pallas_call(
        kernel,
        grid_spec=pltpu.PrefetchScalarGridSpec(
            num_scalar_prefetch=1,
            grid=(steps,),
            in_specs=[pl.BlockSpec(block, place_of(index)) for index in range(count)],
            out_specs=pl.BlockSpec(block, lambda step, table_ref: (table_ref[step], 0)),
        ),
        out_shape=jax.ShapeDtypeStruct((steps * block[0], block[1]), pieces[0].dtype),
        compiler_params=pltpu.CompilerParams(vmem_limit_bytes=48 << 20),
        cost_estimate=BRIEF,
        name="arrange",
    )(table, *pieces)


def split_kernel(table_ref, first, second, first_out, second_out):
    first_out[...] = first[...]
    second_out[...] = second[...]


def split_columns(core, matrix, block):
    rows, columns = matrix.shape
    count = columns // block // 2
    piece = jax.ShapeDtypeStruct((rows, columns // 2), matrix.dtype)
    return pl.pallas_call(
        split_kernel,
        grid_spec=pltpu.PrefetchScalarGridSpec(
            num_scalar_prefetch=1,
            grid=(count,),
            in_specs=[
                pl.BlockSpec((rows, block), lambda i, core_ref: (0, 2 * i + core_ref[0])),
                pl.BlockSpec((rows, block), lambda i, core_ref: (0, 2 * i + 1 - core_ref[0])),
            ],
            out_specs=[pl.BlockSpec((rows, block), lambda i, core_ref: (0, i))] * 2,
        ),
        out_shape=(piece, piece),
        cost_estimate=BRIEF,
        name="split_columns",
    )(core.reshape(1), matrix, matrix)


def weave_kernel(core_ref, mine, theirs, out):
    block = mine.shape[1]

    @pl.when(core_ref[0] == 0)
    def _():
        out[:, :block] = mine[...]
        out[:, block:] = theirs[...]

    @pl.when(core_ref[0] == 1)
    def _():
        out[:, :block] = theirs[...]
        out[:, block:] = mine[...]


def weave_columns(core, mine, theirs, block):
    rows, columns = mine.shape
    return pl.pallas_call(
        weave_kernel,
        grid_spec=pltpu.PrefetchScalarGridSpec(
            num_scalar_prefetch=1,
            grid=(columns // block,),
            in_specs=[pl.BlockSpec((rows, block), lambda i, core_ref: (0, i))] * 2,
            out_specs=pl.BlockSpec((rows, 2 * block), lambda i, core_ref: (0, i)),
        ),
        out_shape=jax.ShapeDtypeStruct((rows, 2 * columns), mine.dtype),
        cost_estimate=BRIEF,
        name="weave_columns",
    )(core.reshape(1), mine, theirs)


def outer_rows_of(lefts, rights, rows, sources, tile=512, runs=None):
    count, columns = rights[0].shape
    terms, blocks = len(lefts), len(sources)
    table = jnp.stack([jnp.asarray(index, jnp.int32) for index in [*sources, *(runs or [])]])

    def kernel(table_ref, *refs):
        total = 0.0
        for left, right in zip(refs[:terms], refs[terms : 2 * terms]):
            total = total + lax.dot_general(
                left[...], right[...], (((0,), (0,)), ((), ())), preferred_element_type=jnp.float32
            )
        total = total.astype(jnp.bfloat16)
        if runs is None:
            refs[-1][...] = total
        else:
            for at in range(len(runs)):
                start = pl.multiple_of(table_ref[blocks + at] * HEAD_DIM, HEAD_DIM)
                refs[-1][pl.ds(start, HEAD_DIM), :] = total[at * HEAD_DIM : (at + 1) * HEAD_DIM]

    return pl.pallas_call(
        kernel,
        grid_spec=pltpu.PrefetchScalarGridSpec(
            num_scalar_prefetch=1,
            grid=(blocks, columns // tile),
            in_specs=[pl.BlockSpec((count, rows), lambda i, j, ref: (0, ref[i]))] * terms
            + [pl.BlockSpec((count, tile), lambda i, j, ref: (0, j))] * terms,
            out_specs=pl.BlockSpec((rows, tile), lambda i, j, ref: (i, j)),
        ),
        out_shape=jax.ShapeDtypeStruct((blocks * rows, columns), jnp.bfloat16),
        compiler_params=pltpu.CompilerParams(vmem_limit_bytes=48 << 20),
        cost_estimate=BRIEF,
        name="outer_rows_of",
    )(table, *lefts, *rights)


def outer_sides(indices, left, right, rows):
    count, columns = right.shape
    pieces = len(indices) // 2
    table = jnp.stack([jnp.asarray(index, jnp.int32) for index in indices])

    def kernel(table_ref, left, right, *outs):
        step = pl.program_id(0)
        total = lax.dot_general(
            left[...], right[...], (((0,), (0,)), ((), ())), preferred_element_type=jnp.float32
        ).astype(jnp.bfloat16)
        for piece, out in enumerate(outs):

            @pl.when(step // 2 == piece)
            def _():
                out[...] = total

    def side_of(piece):
        return lambda step, table_ref: (0, jnp.clip(step - 2 * piece, 0, 1))

    return pl.pallas_call(
        kernel,
        grid_spec=pltpu.PrefetchScalarGridSpec(
            num_scalar_prefetch=1,
            grid=(2 * pieces,),
            in_specs=[
                pl.BlockSpec((count, rows), lambda step, table_ref: (0, table_ref[step])),
                pl.BlockSpec((count, columns), lambda step, table_ref: (0, 0)),
            ],
            out_specs=[pl.BlockSpec((rows, columns), side_of(piece)) for piece in range(pieces)],
        ),
        out_shape=[jax.ShapeDtypeStruct((rows, 2 * columns), jnp.bfloat16)] * pieces,
        compiler_params=pltpu.CompilerParams(vmem_limit_bytes=48 << 20),
        cost_estimate=BRIEF,
        name="outer_sides",
    )(table, left, right)


def regroup(bits, matrix, seq_size):
    rows, columns = matrix.shape
    block = 256

    def kernel(bits_ref, matrix, out):
        for flips in range(8):
            y_flip, x_flip, core_flip = flips // 4, flips // 2 % 2, flips % 2

            @pl.when(4 * bits_ref[0] + 2 * bits_ref[1] + bits_ref[2] == flips)
            def _():
                runs = [
                    (((y ^ y_flip) * 2 + (x ^ x_flip)) * 2 + (side ^ core_flip)) * seq_size + z
                    for z in range(seq_size)
                    for y in range(2)
                    for x in range(2)
                    for side in range(2)
                ]
                out[...] = jnp.concatenate(
                    [matrix[:, run * HEAD_DIM : (run + 1) * HEAD_DIM] for run in runs], axis=1
                )

    return pl.pallas_call(
        kernel,
        grid_spec=pltpu.PrefetchScalarGridSpec(
            num_scalar_prefetch=1,
            grid=(rows // block,),
            in_specs=[pl.BlockSpec((block, columns), lambda i, bits_ref: (i, 0))],
            out_specs=pl.BlockSpec((block, columns), lambda i, bits_ref: (i, 0)),
        ),
        out_shape=jax.ShapeDtypeStruct((rows, columns), matrix.dtype),
        compiler_params=pltpu.CompilerParams(vmem_limit_bytes=48 << 20),
        cost_estimate=BRIEF,
        name="regroup",
    )(bits, matrix)


def regroup_back(bits, mine, got, seq_size, dtype):
    rows, columns = mine.shape
    block = 128

    def kernel(bits_ref, mine, got, out):
        for flips in range(8):
            y_flip, x_flip, core_flip = flips // 4, flips // 2 % 2, flips % 2

            @pl.when(4 * bits_ref[0] + 2 * bits_ref[1] + bits_ref[2] == flips)
            def _():
                runs = [
                    ((z * 2 + (y ^ y_flip)) * 2 + (x ^ x_flip)) * 2 + (side ^ core_flip)
                    for y in range(2)
                    for x in range(2)
                    for side in range(2)
                    for z in range(seq_size)
                ]
                own = [mine[:, run * HEAD_DIM : (run + 1) * HEAD_DIM] for run in runs]
                runs = [run ^ 1 for run in runs]
                other = [got[:, run * HEAD_DIM : (run + 1) * HEAD_DIM] for run in runs]
                out[...] = (
                    jnp.concatenate(own, axis=1)
                    + jnp.concatenate(other, axis=1).astype(jnp.float32)
                ).astype(dtype)

    spec = pl.BlockSpec((block, columns), lambda i, bits_ref: (i, 0))
    return pl.pallas_call(
        kernel,
        grid_spec=pltpu.PrefetchScalarGridSpec(
            num_scalar_prefetch=1,
            grid=(rows // block,),
            in_specs=[spec, spec],
            out_specs=spec,
        ),
        out_shape=jax.ShapeDtypeStruct((rows, columns), dtype),
        compiler_params=pltpu.CompilerParams(vmem_limit_bytes=48 << 20),
        cost_estimate=BRIEF,
        name="regroup_back",
    )(bits, mine, got)


def half_dot(which, left, right, by_columns, dtype, tile=512, places=None):
    lefts = left if places is not None else (left,)
    rows, depth = lefts[0].shape
    columns = right.shape[0] if by_columns else right.shape[1]
    contract = 1 if by_columns else 0
    count = len(lefts)
    table = jnp.stack([which, *(places or [])])

    def kernel(table_ref, *refs):
        total = 0.0
        for index in range(count):
            total = total + lax.dot_general(
                refs[index][...],
                refs[count + index][...],
                (((1,), (contract,)), ((), ())),
                preferred_element_type=jnp.float32,
            )
        refs[-1][...] = total.astype(dtype)

    def right_block(index):
        if by_columns:
            return pl.BlockSpec((tile, depth), lambda i, table_ref: (i, 0))
        if places is None:
            return pl.BlockSpec((depth, tile), lambda i, table_ref: (0, i))
        return pl.BlockSpec((depth, tile), lambda i, table_ref: (table_ref[1 + index], i))

    return pl.pallas_call(
        kernel,
        grid_spec=pltpu.PrefetchScalarGridSpec(
            num_scalar_prefetch=1,
            grid=(columns // tile,),
            in_specs=[
                pl.BlockSpec((rows // 2, depth), lambda i, table_ref: (table_ref[0], 0))
            ]
            * count
            + [right_block(index) for index in range(count)],
            out_specs=pl.BlockSpec((rows // 2, tile), lambda i, table_ref: (0, i)),
        ),
        out_shape=jax.ShapeDtypeStruct((rows // 2, columns), dtype),
        compiler_params=pltpu.CompilerParams(vmem_limit_bytes=48 << 20),
        cost_estimate=BRIEF,
        name="half_dot",
    )(table, *lefts, *[right] * count)


def multiply(
    lefts, rights, by_columns, tile=512, bias=None, slope=None, lift=False, halves=False
):
    rows = lefts[0].shape[0]
    terms = len(lefts)
    columns = rights[0].shape[0] if by_columns else rights[0].shape[1]
    contract = 1 if by_columns else 0
    extra = [] if bias is None else [bias]
    extra += [] if slope is None else [slope]
    across = pl.BlockSpec((rows, tile), lambda i: (0, i))
    row = pl.BlockSpec((1, tile), lambda i: (0, i))
    wide = jax.ShapeDtypeStruct((rows, columns), jnp.bfloat16)
    outs = [(across, wide)]
    if halves:
        part = pl.BlockSpec((rows // 2, tile), lambda i: (0, i))
        outs = [(part, jax.ShapeDtypeStruct((rows // 2, columns), jnp.bfloat16))] * 2
    if lift:
        outs.append((across, wide))
    if slope is not None:
        outs.append((row, jax.ShapeDtypeStruct((1, columns), jnp.float32)))

    def kernel(*refs):
        total = 0.0
        for left, right in zip(refs[:terms], refs[terms : 2 * terms]):
            total = total + lax.dot_general(
                left[...],
                right[...],
                (((1,), (contract,)), ((), ())),
                preferred_element_type=jnp.float32,
            )
        rest = refs[2 * terms :]
        if bias is not None:
            total = total + rest[0][...]
        out = rest[len(extra)]
        if lift:
            lifted = 0.5 * (1.0 + lax.erf(total * (0.5**0.5)))
            bell = jnp.exp(-0.5 * total * total) * ((0.5 / math.pi) ** 0.5)
            out[...] = (total * lifted).astype(jnp.bfloat16)
            rest[len(extra) + 1][...] = (lifted + total * bell).astype(jnp.bfloat16)
        elif slope is not None:
            low = (total * rest[len(extra) - 1][...].astype(jnp.float32)).astype(jnp.bfloat16)
            out[...] = low
            rest[len(extra) + 1][...] = jnp.sum(low.astype(jnp.float32), axis=0, keepdims=True)
        elif halves:
            out[...] = total[: rows // 2].astype(jnp.bfloat16)
            rest[len(extra) + 1][...] = total[rows // 2 :].astype(jnp.bfloat16)
        else:
            out[...] = total.astype(jnp.bfloat16)

    def right_spec(right):
        if by_columns:
            return pl.BlockSpec((tile, right.shape[1]), lambda i: (i, 0))
        return pl.BlockSpec((right.shape[0], tile), lambda i: (0, i))

    result = pl.pallas_call(
        kernel,
        grid=(columns // tile,),
        in_specs=[pl.BlockSpec(left.shape, lambda i: (0, 0)) for left in lefts]
        + [right_spec(right) for right in rights]
        + ([] if bias is None else [row])
        + ([] if slope is None else [across]),
        out_specs=[spec for spec, _ in outs],
        out_shape=[shape for _, shape in outs],
        compiler_params=pltpu.CompilerParams(vmem_limit_bytes=48 << 20),
        cost_estimate=BRIEF,
        name="multiply",
    )(*lefts, *rights, *extra)
    return result if len(outs) > 1 else result[0]


def add_low(left, right):
    return (left.astype(jnp.float32) + right.astype(jnp.float32)).astype(jnp.bfloat16)


BLOCK = 256


def softmax_block(index, keys_wide, query_wide):
    start = index * BLOCK
    tiles = []
    if index > 0:
        tiles.append(
            lax.dot_general(
                keys_wide[:start],
                query_wide,
                (((1,), (1,)), ((), ())),
                preferred_element_type=jnp.float32,
            )
        )
    last = lax.dot_general(
        keys_wide[start : start + BLOCK],
        query_wide,
        (((1,), (1,)), ((), ())),
        preferred_element_type=jnp.float32,
    )
    key_pos = lax.broadcasted_iota(jnp.int32, last.shape, 0)
    query_pos = lax.broadcasted_iota(jnp.int32, last.shape, 1)
    tiles.append(jnp.where(key_pos <= query_pos, last, jnp.float32(-1e30)))
    peak = jnp.max(tiles[-1], axis=0, keepdims=True)
    if index > 0:
        peak = jnp.maximum(peak, jnp.max(tiles[0], axis=0, keepdims=True))
    tiles = [jnp.exp(tile - peak) for tile in tiles]
    total = sum(jnp.sum(tile, axis=0, keepdims=True) for tile in tiles)
    inverse = 1.0 / total
    return [tile * inverse for tile in tiles]


def widen(head, rows_ref, mask_ref):
    first = 3 * HEAD_DIM * head
    query = rows_ref[:, first : first + HEAD_DIM] * jnp.bfloat16(HEAD_DIM**-0.5)
    keys = rows_ref[:, first + HEAD_DIM : first + 2 * HEAD_DIM]
    values = rows_ref[:, first + 2 * HEAD_DIM : first + 3 * HEAD_DIM]
    even = jnp.full(query.shape, 1.0 / HEAD_DIM, jnp.bfloat16)
    query_wide = jnp.concatenate([query, even], axis=1)
    keys_wide = jnp.concatenate([keys, mask_ref[...]], axis=1)
    return query, keys, values, query_wide, keys_wide


def attend_kernel(rows_ref, mask_ref, out_ref):
    blocks = rows_ref.shape[0] // BLOCK
    results = [[], []]
    for head in range(2):
        _, _, values, query_wide, keys_wide = widen(head, rows_ref, mask_ref)
        for index in range(blocks):
            start, stop = index * BLOCK, (index + 1) * BLOCK
            tiles = softmax_block(index, keys_wide, query_wide[start:stop])
            low = jnp.concatenate([tile.astype(jnp.bfloat16) for tile in tiles], axis=0)
            outcome = lax.dot_general(
                values[:stop], low, (((0,), (0,)), ((), ())), preferred_element_type=jnp.float32
            )
            results[head].append(outcome.T)
    for index in range(blocks):
        both = jnp.concatenate([results[0][index], results[1][index]], axis=1)
        out_ref[index * BLOCK : (index + 1) * BLOCK, :] = both.astype(jnp.bfloat16)


def attend_back_kernel(rows_ref, grad_ref, mask_ref, out_ref, key_sum, value_sum):
    blocks = rows_ref.shape[0] // BLOCK
    columns = []
    for head in range(2):
        query, keys, values, query_wide, keys_wide = widen(head, rows_ref, mask_ref)
        grad = grad_ref[:, head * HEAD_DIM : (head + 1) * HEAD_DIM]
        query_parts = []
        for index in reversed(range(blocks)):
            start, stop = index * BLOCK, (index + 1) * BLOCK
            tiles = softmax_block(index, keys_wide, query_wide[start:stop])
            soft = jnp.concatenate(tiles, axis=0)
            grad_rows = grad[start:stop]
            grad_probs = lax.dot_general(
                values[:stop],
                grad_rows,
                (((1,), (1,)), ((), ())),
                preferred_element_type=jnp.float32,
            )
            weighted = soft * grad_probs
            delta = jnp.sum(weighted, axis=0, keepdims=True)
            grad_scores = (weighted - soft * delta).astype(jnp.bfloat16)
            value_term = jnp.dot(
                soft.astype(jnp.bfloat16), grad_rows, preferred_element_type=jnp.float32
            )
            key_term = jnp.dot(
                grad_scores, query[start:stop], preferred_element_type=jnp.float32
            )
            if index == blocks - 1:
                value_sum[...] = value_term
                key_sum[...] = key_term
            else:
                value_sum[:stop, :] += value_term
                key_sum[:stop, :] += key_term
            outcome = lax.dot_general(
                keys[:stop],
                grad_scores,
                (((0,), (0,)), ((), ())),
                preferred_element_type=jnp.float32,
            )
            query_parts.insert(0, outcome.T * jnp.float32(HEAD_DIM**-0.5))
        columns += [jnp.concatenate(query_parts, axis=0), key_sum[...], value_sum[...]]
    out_ref[...] = jnp.concatenate([part.astype(jnp.bfloat16) for part in columns], axis=1)


def attend(rows, mask):
    count, columns = rows.shape
    pairs = columns // (6 * HEAD_DIM)
    work = pairs * 2 * count * count * HEAD_DIM
    return pl.pallas_call(
        attend_kernel,
        grid=(pairs,),
        in_specs=[
            pl.BlockSpec((count, 6 * HEAD_DIM), lambda i: (0, i)),
            pl.BlockSpec((count, HEAD_DIM), lambda i: (0, 0)),
        ],
        out_specs=pl.BlockSpec((count, 2 * HEAD_DIM), lambda i: (0, i)),
        out_shape=jax.ShapeDtypeStruct((count, pairs * 2 * HEAD_DIM), jnp.bfloat16),
        compiler_params=pltpu.CompilerParams(vmem_limit_bytes=48 << 20),
        cost_estimate=BRIEF,
        name="attend",
    )(rows, mask)


def attend_back(rows, grad, mask, place):
    count, columns = rows.shape
    pairs = columns // (6 * HEAD_DIM) // 4

    def kernel(place_ref, *refs):
        attend_back_kernel(*refs)

    return pl.pallas_call(
        kernel,
        grid_spec=pltpu.PrefetchScalarGridSpec(
            num_scalar_prefetch=1,
            grid=(pairs,),
            in_specs=[
                pl.BlockSpec(
                    (count, 6 * HEAD_DIM), lambda i, place_ref: (0, pairs * place_ref[0] + i)
                ),
                pl.BlockSpec(
                    (count, 2 * HEAD_DIM), lambda i, place_ref: (0, pairs * place_ref[0] + i)
                ),
                pl.BlockSpec((count, HEAD_DIM), lambda i, place_ref: (0, 0)),
            ],
            out_specs=pl.BlockSpec((count, 6 * HEAD_DIM), lambda i, place_ref: (0, i)),
            scratch_shapes=[pltpu.VMEM((count, HEAD_DIM), jnp.float32)] * 2,
        ),
        out_shape=jax.ShapeDtypeStruct((count, columns // 4), jnp.bfloat16),
        compiler_params=pltpu.CompilerParams(vmem_limit_bytes=48 << 20),
        cost_estimate=BRIEF,
        name="attend_back",
    )(place.reshape(1), rows, grad, mask)


ROWS = 128


def normal_parts(values):
    center = values - jnp.mean(values, axis=-1, keepdims=True)
    spread_of = jnp.mean(center * center, axis=-1, keepdims=True)
    scale = lax.rsqrt(spread_of + EPS)
    return center * scale, scale


def normal_back(normed, scale, grad):
    mean_grad = jnp.mean(grad, axis=-1, keepdims=True)
    mean_product = jnp.mean(grad * normed, axis=-1, keepdims=True)
    return (grad - mean_grad - normed * mean_product) * scale


def first_kernel(start_ref, tokens, gain, shift, out):
    normed, _ = normal_parts(tokens[...].astype(jnp.float32))
    out[...] = (normed * gain[...] + shift[...]).astype(out.dtype)


def middle_kernel(
    start_ref,
    tokens,
    own_upper,
    own_lower,
    upper,
    lower,
    active,
    bias,
    gain,
    shift,
    middle_out,
    rows_out,
):
    in_upper = pl.program_id(0) < pl.num_programs(0) // 2
    own = jnp.where(in_upper, own_upper[...], own_lower[...])
    got = jnp.where(in_upper, upper[...], lower[...])
    branch = own.astype(jnp.float32) + got.astype(jnp.float32) + bias[...]
    middle = tokens[...].astype(jnp.float32) + active[...] * branch
    middle_out[...] = middle
    normed, _ = normal_parts(middle)
    rows_out[...] = (normed * gain[...] + shift[...]).astype(rows_out.dtype)


def add_totals(totals, parts):
    first = pl.program_id(0) == 0
    for index, part in enumerate(parts):
        total = jnp.sum(part, axis=0, keepdims=True)
        totals[index : index + 1, :] = total + jnp.where(
            first, 0.0, totals[index : index + 1, :]
        )


def middle_back_kernel(
    start_ref,
    cotangent,
    middle,
    own,
    upper,
    lower,
    peer,
    active,
    gain,
    grad_out,
    branch_out,
    totals,
):
    in_upper = pl.program_id(0) < pl.num_programs(0) // 2
    got = jnp.where(in_upper, upper[...], lower[...])
    grad_second = own[...] + got.astype(jnp.float32) + peer[...].astype(jnp.float32)
    normed, scale = normal_parts(middle[...])
    grad_middle = cotangent[...].astype(jnp.float32) + normal_back(
        normed, scale, grad_second * gain[...]
    )
    grad_out[...] = grad_middle
    grad_branch = (active[...] * grad_middle).astype(jnp.bfloat16)
    branch_out[...] = grad_branch
    add_totals(
        totals, (grad_second * normed, grad_second, grad_branch.astype(jnp.float32))
    )


def first_back_kernel(start_ref, tokens, grad_middle, own, got, gain, grad_out, totals):
    grad_first = own[...] + got[...].astype(jnp.float32)
    normed, scale = normal_parts(tokens[...].astype(jnp.float32))
    grad = grad_middle[...] + normal_back(normed, scale, grad_first * gain[...])
    grad_out[...] = grad.astype(grad_out.dtype)
    add_totals(totals, (grad_first * normed, grad_first))


def by_rows(kernel, start, count, arrays, outs, name):
    width = arrays[0][0].shape[1]
    specs = {
        "rows": pl.BlockSpec((ROWS, width), lambda i, start_ref: (i, 0)),
        "from": pl.BlockSpec((ROWS, width), lambda i, start_ref: (start_ref[0] + i, 0)),
        "vector": pl.BlockSpec((1, width), lambda i, start_ref: (0, 0)),
        "totals": pl.BlockSpec((8, width), lambda i, start_ref: (0, 0)),
        "upper": pl.BlockSpec(
            (ROWS, width), lambda i, start_ref: (jnp.minimum(i, count // ROWS // 2 - 1), 0)
        ),
        "lower": pl.BlockSpec(
            (ROWS, width), lambda i, start_ref: (jnp.maximum(i - count // ROWS // 2, 0), 0)
        ),
        "flag": pl.BlockSpec((ROWS, 1), lambda i, start_ref: (i, 0)),
        "flag from": pl.BlockSpec((ROWS, 1), lambda i, start_ref: (start_ref[0] + i, 0)),
    }
    shapes = [
        jax.ShapeDtypeStruct((8 if kind == "totals" else count, width), dtype)
        for kind, dtype in outs
    ]
    moved = sum(
        count * width * array.dtype.itemsize for array, kind in arrays if kind in ("rows", "from")
    ) + sum(math.prod(shape.shape) * shape.dtype.itemsize for shape in shapes)
    return pl.pallas_call(
        kernel,
        grid_spec=pltpu.PrefetchScalarGridSpec(
            num_scalar_prefetch=1,
            grid=(count // ROWS,),
            in_specs=[specs[kind] for _, kind in arrays],
            out_specs=[specs[kind] for kind, _ in outs],
        ),
        out_shape=shapes,
        compiler_params=pltpu.CompilerParams(vmem_limit_bytes=48 << 20),
        cost_estimate=BRIEF,
        name=name,
    )(start, *[array for array, _ in arrays])


def after(value, *others):
    return lax.optimization_barrier((value, others))[0]


MIDDLE_KINDS = ("rows", "upper", "lower", "upper", "lower", "flag", "vector", "vector", "vector")
BACK_KINDS = ("from", "from", "rows", "upper", "lower", "rows", "flag from", "vector")


class Line:
    def __init__(self):
        self.last = None

    def __call__(self, function, *arrays):
        if self.last is not None:
            arrays = lax.optimization_barrier((arrays, self.last))[0]
        result = function(*arrays)
        self.last = jax.tree.leaves(result)[0]
        return result


def whole_sequence_device(
    tokens,
    exit_layer,
    first_gain,
    first_shift,
    query_weight,
    query_bias,
    key_weight,
    value_weight,
    value_bias,
    output_weight,
    output_bias,
    second_gain,
    second_shift,
    expand_weight,
    expand_bias,
    shrink_weight,
    shrink_bias,
    cotangent,
):
    seq_count, local_len, width = tokens.shape
    heads_rows = query_weight.shape[0]
    hidden_rows = expand_weight.shape[0]
    seq_size = lax.axis_size("seq")
    dp_size = lax.axis_size(DEVICES) // seq_size
    depth, core = lax.axis_index("seq"), lax.axis_index("core")
    along_x, along_y = lax.axis_index("x"), lax.axis_index("y")
    place = 2 * along_y + along_x
    dp = 2 * place + core
    parity = depth % 2
    full_len = local_len * seq_size
    half_len = full_len // 2
    f32, low = jnp.float32, jnp.bfloat16

    def route(flip):
        pairs = []
        for i in range(dp_size):
            for j in range(seq_size):
                target = 2 * (i % 2) + (j % 2 if not flip else 1 - j % 2)
                pairs.append((i * seq_size + j, (i // 2 * 2 + j // 2) * seq_size + target))
        return pairs

    def send(first, second, back):
        routes = [[(b, a) if back else (a, b) for a, b in route(flip)] for flip in (False, True)]
        return lax.ppermute(first, DEVICES, routes[0]), lax.ppermute(second, DEVICES, routes[1])

    def by_parity(values):
        return pick(parity, values[0], values[1]), pick(parity, values[1], values[0])

    def paired(first, second):
        return ordered(parity, first[None], second[None], 0)

    def by_core(own, other):
        return ordered(core, own, other, 0)

    def half_rows(matrix, which):
        return lax.dynamic_slice_in_dim(matrix, which * half_len, half_len, 0)

    line = Line()
    depth_rows = heads_rows * seq_size
    hidden_block = hidden_rows * seq_size
    places = [place ^ d for d in range(4)]
    sides = [core, 1 - core]
    bits = jnp.stack([along_y, along_x, core])

    def through_z(shard):
        return lax.all_gather(shard, "seq", axis=0, tiled=True)

    devices = dp_size * seq_size
    all_dp = jnp.arange(dp_size, dtype=jnp.int32)[:, None]
    all_seq = jnp.arange(seq_size, dtype=jnp.int32)[None, :]
    relative = ((all_dp ^ dp) * seq_size + (depth - all_seq) % seq_size).reshape(-1)

    def shift_z(values, steps):
        return lax.ppermute(
            values, "seq", [(i, (i + steps) % seq_size) for i in range(seq_size)]
        )

    def stacked(own, other):
        return jnp.concatenate([own, other], 0)

    vectors = [first_gain, first_shift, query_bias, value_bias, output_bias, second_gain]
    vectors += [second_shift, shrink_bias, expand_bias]
    shard_qkv = line(
        lambda *parts: jnp.concatenate(parts, 0), query_weight, key_weight, value_weight
    )
    z_qkv = through_z(shard_qkv)
    vectors = line(lambda *parts: jnp.concatenate(parts)[None, None], *vectors)
    shifted = [shift_z(vectors, steps) for steps in range(1, seq_size)]
    alive = (exit_layer > LAYER).astype(low)
    flag_rows = jnp.broadcast_to(alive[:, None, :], (seq_count, 16, local_len))
    flag_rows = jnp.pad(flag_rows, ((0, 0), (0, 0), (0, width - local_len)))
    message = line(
        lambda *arrays: by_parity(jnp.concatenate(arrays, axis=1)), tokens, flag_rows, cotangent
    )
    vectors = line(lambda *parts: jnp.concatenate(parts, 1), vectors, *shifted)
    mine, theirs = line(lambda rows: split_columns(core, rows, hidden_block), shrink_weight)
    theirs = swap(theirs, CORE)
    vectors = line(stacked, vectors, swap(vectors, ALONG_Y))
    shard_shrink = line(stacked, mine, theirs)
    mine, theirs = line(lambda rows: split_columns(along_x, rows, hidden_block), shard_shrink)
    theirs = swap(theirs, ALONG_X)
    vectors = line(stacked, vectors, swap(vectors, ALONG_X))
    shard_shrink = line(stacked, mine, theirs)
    vectors = line(stacked, vectors, swap(vectors, CORE))
    vectors = line(
        lambda rows: rows.reshape(2, 2, 2, seq_size, -1)
        .transpose(2, 1, 0, 3, 4)
        .reshape(devices, -1)[relative]
        .astype(f32),
        vectors,
    )
    shrink_across = swap(shard_shrink, ALONG_Y)

    def vector(index):
        return vectors[:, index * heads_rows : (index + 1) * heads_rows].reshape(1, -1)

    def of_core(matrix):
        cut = matrix.reshape(4, 2, seq_size, -1)
        return lax.dynamic_index_in_dim(cut, core, 1, False).reshape(4 * seq_size, -1)

    def of_quarter(matrix):
        cut = matrix.reshape(2, 4, seq_size, -1)
        return lax.dynamic_index_in_dim(cut, 2 * along_x + core, 1, False)

    gain_one, shift_one = vector(0), vector(1)
    bias_query = of_core(vectors[:, 2 * heads_rows : 3 * heads_rows])
    bias_value = of_core(vectors[:, 3 * heads_rows : 4 * heads_rows])
    bias_rows = jnp.stack([bias_query, jnp.zeros_like(bias_query), bias_value], 1).reshape(1, -1)
    bias_out, gain_two, shift_two, bias_shrink = vector(4), vector(5), vector(6), vector(7)
    bias_expand = of_quarter(vectors[:, 8 * heads_rows :]).reshape(1, -1)

    half_qkv = 3 * depth_rows // 2

    z_qkv = after(z_qkv, vectors, shard_shrink)
    beside_qkv, across_qkv = swap(z_qkv, ALONG_X), swap(z_qkv, ALONG_Y)
    z_out = through_z(after(output_weight, z_qkv))
    arrived = send(*(after(part, z_out) for part in message), False)
    mine, theirs = line(lambda rows: split_columns(core, rows, depth_rows), z_out)
    rows_out = line(
        lambda own, other: jnp.concatenate([own, other], 1), mine, swap(theirs, CORE)
    )
    upper = line(lambda rows: rows[:half_qkv], beside_qkv)
    lower = line(lambda rows: rows[half_qkv:], across_qkv)
    upper, lower = swap(upper, ALONG_Y), swap(lower, ALONG_X)
    z_expand = through_z(after(expand_weight, *arrived))
    w_qkv = line(
        lambda *pieces: arrange(
            pieces,
            (half_qkv, width),
            [(p, r, 0) for p in range(3) for r in range(2)] + [(3, 0, 0), (4, 0, 0)],
            [2 * places[d] + r for d in range(4) for r in range(2)],
        ),
        z_qkv,
        beside_qkv,
        across_qkv,
        upper,
        lower,
    )
    half = line(paired, *arrived)
    joined = line(by_core, half, swap(half, CORE))
    inputs = joined[:, :local_len].reshape(full_len, width)
    alive = joined[:, local_len, :local_len].reshape(full_len, 1)
    cotangent_full = joined[:, local_len + 16 :].reshape(full_len, width)
    active = alive.astype(f32)
    mask = jnp.broadcast_to((alive - 1) * jnp.bfloat16(1e30), (full_len, HEAD_DIM))

    no_start = jnp.zeros((1,), jnp.int32)
    half_start = (core * (half_len // ROWS)).reshape(1)

    (first_rows,) = line(
        lambda *arrays: by_rows(
            first_kernel,
            no_start,
            full_len,
            list(zip(arrays, ("rows", "vector", "vector"))),
            [("rows", low)],
            "first_norm",
        ),
        inputs,
        gain_one,
        shift_one,
    )
    rows_out = after(rows_out, w_qkv)
    out_beside, out_across = swap(rows_out, ALONG_X), swap(rows_out, ALONG_Y)
    across_expand = swap(z_expand, ALONG_Y)

    qkv = line(
        lambda rows, weight: multiply((rows,), (weight,), True, bias=bias_rows), first_rows, w_qkv
    )
    out_corner = swap(line(lambda rows: rows * jnp.bfloat16(1), out_across), ALONG_X)
    grad_shrunk = line(
        lambda flags, grads: (flags * grads.astype(f32)).astype(low), active, cotangent_full
    )
    sent_gs = line(lambda rows: half_rows(rows, core), grad_shrunk)
    gs_got = swap(sent_gs, ALONG_X)
    mixed = line(attend, qkv, mask)
    w_out = line(
        lambda *pieces: arrange(
            pieces,
            (depth_rows, width // 2),
            [(p, 0, i) for p in range(4) for i in range(2)],
            [2 * places[d] + sides[i] for d in range(4) for i in range(2)],
        ),
        after(rows_out, z_expand),
        out_beside,
        out_across,
        out_corner,
    )
    branch = line(
        lambda rows, weight: multiply((rows,), (weight,), True, halves=True), mixed, w_out
    )
    branch_got = [swap(part, CORE) for part in branch]
    shard_shrink = line(stacked, shard_shrink, shrink_across)
    w_shrink = through_z(after(shard_shrink, z_expand, branch))
    middle, second_rows = line(
        lambda *arrays: by_rows(
            middle_kernel,
            no_start,
            full_len,
            list(zip(arrays, MIDDLE_KINDS)),
            [("rows", f32), ("rows", low)],
            "middle_norm",
        ),
        inputs,
        *branch,
        *branch_got,
        active,
        bias_out,
        gain_two,
        shift_two,
    )
    second_half = line(lambda rows: half_rows(rows, core), second_rows)
    second_got = swap(second_half, ALONG_X)
    gs_own = line(lambda rows: regroup(bits, rows, seq_size), grad_shrunk)
    w_expand = line(
        lambda *pieces: arrange(
            pieces,
            (hidden_block // 2, width),
            [(p, r, 0) for p in range(2) for r in range(2)],
            [2 * (along_y ^ p) + r for p in range(2) for r in range(2)],
        ),
        z_expand,
        across_expand,
    )

    def lift(rows, weight):
        return multiply((rows,), (weight,), True, bias=bias_expand, lift=True)

    activated, slope = line(lift, second_rows, w_expand)
    second_peer = line(by_core, second_got, swap(second_got, CORE))
    activated_peer, slope_peer = line(lift, second_peer, w_expand)

    gs_peer = line(by_core, gs_got, swap(after(gs_got, activated), CORE))
    gs_peer = line(lambda rows: regroup(bits, rows, seq_size), gs_peer)
    def scatter_z(total):
        return lax.psum_scatter(total, "seq", scatter_dimension=0, tiled=True)

    def units(grads, weight, slopes):
        return multiply((grads,), (weight,), False, slope=slopes)

    def their_half(left, weight, by_columns=False):
        return half_dot(1 - core, left, weight, by_columns, low)

    def my_half(left, weight, by_columns=False):
        return half_dot(core, left, weight, by_columns, f32)

    def add_rounded(left, right):
        return (left.astype(f32) + right.astype(f32)).astype(low)

    shrink_part = line(
        lambda own, peer, rows, rows_peer: outer_rows_of(
            (own, peer), (rows, rows_peer), width // 2, range(2)
        ),
        gs_own,
        gs_peer,
        activated,
        activated_peer,
    )
    shrink_rows = scatter_z(shrink_part)
    grad_pre_peer, peer_sums = line(units, gs_peer, w_shrink, slope_peer)
    theirs = line(their_half, grad_pre_peer, w_expand)
    mine = line(my_half, grad_pre_peer, w_expand)
    peer_half = line(add_rounded, mine, swap(theirs, CORE))
    second_from_peer = swap(peer_half, ALONG_X)
    grad_pre, own_sums = line(units, gs_own, w_shrink, slope)
    theirs = line(their_half, grad_pre, w_expand)
    second_got = [swap(part, CORE) for part in jnp.split(theirs, 2)]
    second_mine = line(my_half, grad_pre, w_expand)
    def expand_part(d):
        return line(
            lambda *arrays: outer_rows_of(arrays[:2], arrays[2:], hidden_block, [along_y ^ d]),
            grad_pre,
            grad_pre_peer,
            second_rows,
            second_peer,
        )

    expand_across = expand_part(1)
    expand_got = swap(expand_across, ALONG_Y)

    grad_middle, grad_branch_half, middle_totals = line(
        lambda *arrays: by_rows(
            middle_back_kernel,
            half_start,
            half_len,
            list(zip(arrays, BACK_KINDS)),
            [("rows", f32), ("rows", low), ("totals", f32)],
            "middle_norm_back",
        ),
        cotangent_full,
        middle,
        second_mine,
        *second_got,
        second_from_peer,
        active,
        gain_two,
    )
    branch_got = swap(grad_branch_half, CORE)

    grad_branch = line(by_core, grad_branch_half, branch_got)
    grad_mixed = line(
        lambda grads, weight: multiply((grads,), (weight,), False, tile=256), grad_branch, w_out
    )
    out_part = line(
        lambda grads, rows: outer_sides(
            [2 * places[d] + sides[i] for d in range(4) for i in range(2)], grads, rows, depth_rows
        ),
        grad_branch,
        mixed,
    )
    out_parts = [out_part[d] for d in range(4)]
    out_corner = swap(out_parts[3], ALONG_X)
    out_got_x = swap(out_parts[1], ALONG_X)

    def attend_piece(d):
        return line(
            lambda rows, grads, flags: attend_back(rows, grads, flags, places[d]),
            qkv,
            grad_mixed,
            mask,
        )

    def qkv_part(d, rows, source):
        return line(
            lambda grads, inputs_low: outer_rows_of((grads,), (inputs_low,), rows, [source]),
            grad_qkv[d],
            first_rows,
        )

    grad_qkv = {3: attend_piece(3)}
    corner_got = swap(after(qkv_part(3, 2 * half_qkv, 0), out_corner), ALONG_X)
    grad_qkv[1] = attend_piece(1)
    out_got_y = swap(line(add_rounded, out_parts[2], out_corner), ALONG_Y)
    qkv_x = swap(qkv_part(1, 2 * half_qkv, 0), ALONG_X)
    grad_qkv[2] = attend_piece(2)
    across = qkv_part(2, 2 * half_qkv, 0)
    expand_here = expand_part(0)
    grad_qkv[0] = attend_piece(0)
    qkv_y = swap(line(add_rounded, across, corner_got), ALONG_Y)
    expand_sum = line(add_rounded, expand_here, expand_got)
    expand_rows = scatter_z(expand_sum)
    here = qkv_part(0, 2 * half_qkv, 0)
    grads_qkv = tuple(grad_qkv[d] for d in range(4))

    def first_half(which, dtype):
        return lambda *arrays: half_dot(which, arrays[:4], arrays[4], False, dtype, places=places)

    peer_theirs = line(lambda rows, weight: their_half(rows, weight, True), activated_peer, w_shrink)
    peer_got = swap(peer_theirs, CORE)
    first_theirs = line(first_half(1 - core, low), *grads_qkv, w_qkv)
    first_got = swap(first_theirs, CORE)
    peer_mine = line(lambda rows, weight: my_half(rows, weight, True), activated_peer, w_shrink)
    first_mine = line(first_half(core, f32), *grads_qkv, w_qkv)
    to_peer = line(
        lambda *parts: regroup_back(bits, *parts, seq_size, low), peer_mine, peer_got
    )
    from_peer = swap(to_peer, ALONG_X)
    half = shrink_rows.shape[0] // 2
    shrink_got = swap(line(lambda rows: rows[half:], shrink_rows), ALONG_Y)
    qkv_sum = line(
        lambda *parts: sum(part.astype(f32) for part in parts).astype(low), here, qkv_x, qkv_y
    )
    qkv_rows = scatter_z(qkv_sum)
    grad_half, first_totals = line(
        lambda *arrays: by_rows(
            first_back_kernel,
            half_start,
            half_len,
            list(zip(arrays, ("from", "rows", "rows", "rows", "vector"))),
            [("rows", low), ("totals", f32)],
            "first_norm_back",
        ),
        inputs,
        grad_middle,
        first_mine,
        first_got,
        gain_one,
    )
    tokens_parts = send(
        *line(lambda rows: by_parity(rows.reshape(2, local_len, width)), grad_half), True
    )

    def beside_own(peer, rows, flags, bias):
        return half_rows(rows, core) + half_rows(flags, core) * (peer.astype(f32) + bias)

    rest = line(beside_own, from_peer, middle, active, bias_shrink)

    def column_sum(matrix):
        return jnp.sum(matrix.astype(f32), axis=0)

    def all_devices(totals, rows):
        return totals.reshape(devices, rows)

    def core_devices(totals, rows):
        cut = totals.reshape(4, 1, seq_size, rows)
        return ordered(core, cut, jnp.zeros_like(cut), 1).reshape(devices, rows)

    def quarter_devices(totals, rows):
        cut = totals.reshape(2, 1, seq_size, rows)
        none = jnp.zeros_like(cut)
        quarters = [jnp.where(2 * along_x + core == q, cut, none) for q in range(4)]
        return jnp.concatenate(quarters, 1).reshape(devices, rows)

    def all_sums(first, middle_sums, shrunk_grads, own, peer, *grads):
        qkv_sums = jnp.stack([column_sum(part) for part in grads])[jnp.stack(places)]
        qkv_sums = qkv_sums.reshape(4 * seq_size, 3, heads_rows)
        sums = jnp.concatenate(
            [
                all_devices(first[0], heads_rows),
                all_devices(first[1], heads_rows),
                core_devices(qkv_sums[:, 0], heads_rows),
                core_devices(qkv_sums[:, 2], heads_rows),
                all_devices(middle_sums[2], heads_rows),
                all_devices(middle_sums[0], heads_rows),
                all_devices(middle_sums[1], heads_rows),
                all_devices(0.5 * column_sum(shrunk_grads), heads_rows),
                quarter_devices(own + peer, hidden_rows),
            ],
            axis=1,
        )
        return sums.reshape(dp_size, seq_size, -1)[jnp.arange(dp_size) ^ dp]

    def fold(values, got):
        return values[: got.shape[0]] + got

    sums = line(
        all_sums, first_totals, middle_totals, grad_shrunk, own_sums, peer_sums, *grads_qkv
    )
    theirs = line(lambda rows, weight: their_half(rows, weight, True), activated, w_shrink)
    shrunk_got = swap(theirs, CORE)
    sums = line(fold, sums, swap(sums[dp_size // 2 :], ALONG_Y))
    mine = line(lambda rows, weight: my_half(rows, weight, True), activated, w_shrink)
    sums = line(fold, sums, swap(sums[dp_size // 4 :], ALONG_X))
    shrunk = line(lambda *parts: regroup_back(bits, *parts, seq_size, f32), mine, shrunk_got)

    def finish(part, other, flags):
        out = other + half_rows(flags, core) * part
        return by_parity(out.astype(low).reshape(2, local_len, width))

    out_halves = send(*line(finish, shrunk, rest, active), True)
    sums = line(fold, sums, swap(sums[dp_size // 8 :], CORE))
    out_sum = line(
        lambda *parts: sum(part.astype(f32) for part in parts).astype(low),
        out_parts[0],
        out_got_x,
        out_got_y,
    )
    out_got = swap(line(lambda rows: rows[:, width // 2 :], out_sum), CORE)
    tokens_grad = line(paired, *tokens_parts)
    out_rows = line(
        lambda rows, got: weave_columns(core, rows[:, : width // 2], got, depth_rows),
        out_sum,
        out_got,
    )

    def with_vectors(totals, rows):
        totals = totals.reshape(seq_size, 1, -1).astype(low)
        totals = jnp.pad(totals, ((0, 0), (0, 15), (0, width - totals.shape[2])))
        rows = jnp.concatenate([rows.reshape(seq_size, -1, width), totals], 1)
        return rows.reshape(-1, width)

    out_rows = scatter_z(line(with_vectors, sums, out_rows))

    shrink_rows = line(lambda rows, got: add_rounded(rows[:half], got), shrink_rows, shrink_got)
    half = half // 2
    shrink_got = swap(line(lambda rows: rows[half:], shrink_rows), ALONG_X)
    expand_weight_grad = line(lambda rows: rows.astype(f32), expand_rows)
    qkv_weight_grad = line(lambda rows: rows.astype(f32), qkv_rows)
    shrink_rows = line(
        lambda rows, got: weave_columns(along_x, rows[:half], got, hidden_block),
        shrink_rows,
        shrink_got,
    )
    shrink_got = swap(line(lambda rows: rows[heads_rows:], shrink_rows), CORE)
    layer_out = line(paired, *out_halves)
    shrink_weight_grad = line(
        lambda rows, got: weave_columns(core, rows[:heads_rows], got, hidden_block).astype(f32),
        shrink_rows,
        shrink_got,
    )
    output_weight_grad, sums = line(
        lambda rows: (
            rows[:heads_rows].astype(f32),
            rows[heads_rows, : 8 * heads_rows + hidden_rows].astype(f32),
        ),
        out_rows,
    )

    def vector_grad(index):
        return sums[index * heads_rows : (index + 1) * heads_rows]

    return (
        layer_out,
        tokens_grad,
        vector_grad(0),
        vector_grad(1),
        qkv_weight_grad[:heads_rows],
        vector_grad(2),
        qkv_weight_grad[heads_rows : 2 * heads_rows],
        qkv_weight_grad[2 * heads_rows :],
        vector_grad(3),
        output_weight_grad,
        vector_grad(4),
        vector_grad(5),
        vector_grad(6),
        expand_weight_grad,
        sums[8 * heads_rows :],
        shrink_weight_grad,
        vector_grad(7),
    )


def general_device(
    tokens,
    exit_layer,
    first_gain,
    first_shift,
    query_weight,
    query_bias,
    key_weight,
    value_weight,
    value_bias,
    output_weight,
    output_bias,
    second_gain,
    second_shift,
    expand_weight,
    expand_bias,
    shrink_weight,
    shrink_bias,
    cotangent,
):
    seq_count, local_len, width = tokens.shape
    hidden_width = shrink_weight.shape[1]
    total_rows = seq_count * local_len
    heads = width // HEAD_DIM
    inputs = tokens.reshape(total_rows, width).astype(jnp.float32)
    active = (exit_layer > LAYER).astype(jnp.float32).reshape(total_rows, 1)
    gain_one, shift_one = (
        lax.all_gather(first_gain, ("dp", "seq"), axis=0, tiled=True),
        lax.all_gather(first_shift, ("dp", "seq"), axis=0, tiled=True),
    )
    gain_one = gain_one.astype(jnp.float32)
    shift_one = shift_one.astype(jnp.float32)
    normed_in = normalize(inputs)
    first_rows = (normed_in * gain_one + shift_one).astype(jnp.bfloat16)
    blank = jnp.zeros((total_rows, width), jnp.bfloat16)
    attention_init = (blank, blank, blank) + ()
    w_query = lax.all_gather(query_weight, ("dp", "seq"), axis=0, tiled=True)
    b_query = lax.all_gather(query_bias, ("dp", "seq"), axis=0, tiled=True)
    w_key = lax.all_gather(key_weight, ("dp", "seq"), axis=0, tiled=True)
    w_value = lax.all_gather(value_weight, ("dp", "seq"), axis=0, tiled=True)
    b_value = lax.all_gather(value_bias, ("dp", "seq"), axis=0, tiled=True)
    queries = place_cols(
        attention_init[0], project(first_rows, w_query) + b_query.astype(jnp.float32)
    )
    key_rows = place_cols(attention_init[1], project(first_rows, w_key))
    value_rows = place_cols(
        attention_init[2], project(first_rows, w_value) + b_value.astype(jnp.float32)
    )
    stored = attention_init[3:]
    gathered = (queries, key_rows, value_rows) + stored
    queries, key_rows, value_rows = (gathered[0], gathered[1], gathered[2])
    query_local = queries.reshape(seq_count, local_len, width)
    key_local = key_rows.reshape(seq_count, local_len, width)
    value_local = value_rows.reshape(seq_count, local_len, width)
    alive_local = active.reshape(seq_count, local_len)
    key_all, value_all, alive_all = (
        lax.all_gather(key_local, "seq", axis=1, tiled=True),
        lax.all_gather(value_local, "seq", axis=1, tiled=True),
        lax.all_gather(alive_local.astype(jnp.bfloat16), "seq", axis=1, tiled=True),
    )
    full_len = key_all.shape[1]
    offset = lax.axis_index("seq") * local_len
    query_pos = offset + jnp.arange(local_len, dtype=jnp.int32)
    key_pos = jnp.arange(full_len, dtype=jnp.int32)
    causal = key_pos[None, :] <= query_pos[:, None]
    allowed = causal[None, None] & (alive_all.astype(jnp.float32)[:, None, None, :] > 0.5)
    factor = HEAD_DIM ** (-0.5)
    group = min(8, heads)
    group_width = group * HEAD_DIM
    group_total = heads // group

    def group_parts(start_col):
        q_part = lax.dynamic_slice_in_dim(query_local, start_col, group_width, 2).reshape(
            seq_count, local_len, group, HEAD_DIM
        )
        k_part = lax.dynamic_slice_in_dim(key_all, start_col, group_width, 2).reshape(
            seq_count, full_len, group, HEAD_DIM
        )
        v_part = lax.dynamic_slice_in_dim(value_all, start_col, group_width, 2).reshape(
            seq_count, full_len, group, HEAD_DIM
        )
        scores = (
            jnp.einsum("sqhd,skhd->shqk", q_part, k_part, preferred_element_type=jnp.float32)
            * factor
        )
        scores = jnp.where(allowed, scores, jnp.float32(-1e30))
        return (q_part, k_part, v_part, scores)

    def forward_group(group_index, state):
        mixed_all, log_total = state
        start_col = group_index * group_width
        q_part, k_part, v_part, scores = group_parts(start_col)
        row_max = jnp.max(scores, axis=-1, keepdims=True)
        raised = jnp.exp(scores - row_max)
        totals = jnp.sum(raised, axis=-1, keepdims=True)
        weights_low = (raised / totals).astype(jnp.bfloat16)
        outcome = jnp.einsum(
            "shqk,skhd->sqhd", weights_low, v_part, preferred_element_type=jnp.float32
        )
        mixed_all = lax.dynamic_update_slice_in_dim(
            mixed_all,
            outcome.reshape(seq_count, local_len, group_width).astype(jnp.bfloat16),
            start_col,
            2,
        )
        log_total = lax.dynamic_update_slice_in_dim(
            log_total, (row_max + jnp.log(totals))[..., 0], group_index * group, 1
        )
        return (mixed_all, log_total)

    mixed_all, log_total = lax.fori_loop(
        0,
        group_total,
        forward_group,
        (
            jnp.zeros((seq_count, local_len, width), jnp.bfloat16),
            jnp.zeros((seq_count, heads, local_len), jnp.float32),
        ),
    )
    mixed = mixed_all.reshape(total_rows, width)
    vector_blank = jnp.zeros((width,), jnp.bfloat16)
    output_init = (jnp.zeros((total_rows, width), jnp.float32), vector_blank, vector_blank) + ()
    w_out = lax.all_gather(output_weight, ("dp", "seq"), axis=0, tiled=True)
    b_out = lax.all_gather(output_bias, ("dp", "seq"), axis=0, tiled=True)
    g_piece = lax.all_gather(second_gain, ("dp", "seq"), axis=0, tiled=True)
    s_piece = lax.all_gather(second_shift, ("dp", "seq"), axis=0, tiled=True)
    branch = place_cols(output_init[0], project(mixed, w_out) + b_out.astype(jnp.float32))
    gain_two = g_piece
    shift_two = s_piece
    stored = output_init[3:]
    folded = (branch, gain_two, shift_two) + stored
    branch = folded[0]
    gain_two = folded[1].astype(jnp.float32)
    shift_two = folded[2].astype(jnp.float32)
    middle = inputs + active * branch
    normed_mid = normalize(middle)
    second_rows = (normed_mid * gain_two + shift_two).astype(jnp.bfloat16)
    expand_init = (jnp.zeros((total_rows, hidden_width), jnp.float32),) + ()
    w_expand = lax.all_gather(expand_weight, ("dp", "seq"), axis=0, tiled=True)
    b_expand = lax.all_gather(expand_bias, ("dp", "seq"), axis=0, tiled=True)
    hidden_pre = place_cols(
        expand_init[0], project(second_rows, w_expand) + b_expand.astype(jnp.float32)
    )
    stored = expand_init[1:]
    expanded = (hidden_pre,) + stored
    hidden_pre = expanded[0]

    def gelu_exact(pre_values):
        return jax.nn.gelu(pre_values, approximate=False)

    activated_full, gelu_back = jax.vjp(gelu_exact, hidden_pre)
    activated = activated_full.astype(jnp.bfloat16)
    shrink_init = (jnp.zeros((total_rows, width), jnp.float32),) + ()
    w_shrink = lax.all_gather(shrink_weight, ("dp", "seq"), axis=0, tiled=True)
    b_shrink = lax.all_gather(shrink_bias, ("dp", "seq"), axis=0, tiled=True)
    shrunk = place_cols(shrink_init[0], project(activated, w_shrink) + b_shrink.astype(jnp.float32))
    stored = shrink_init[1:]
    shrunk_all = (shrunk,) + stored
    shrunk = shrunk_all[0]
    layer_out = (middle + active * shrunk).astype(jnp.bfloat16).reshape(seq_count, local_len, width)
    grad_out = cotangent.reshape(total_rows, width).astype(jnp.float32)
    grad_shrunk = (active * grad_out).astype(jnp.bfloat16)
    grad_units = through(
        grad_shrunk, lax.all_gather(shrink_weight, ("dp", "seq"), axis=0, tiled=True)
    )
    grad_pre = gelu_back(grad_units)[0].astype(jnp.bfloat16)
    grad_second = through(
        grad_pre, lax.all_gather(expand_weight, ("dp", "seq"), axis=0, tiled=True)
    )
    mid_value, mid_back = jax.vjp(normalize, middle)
    grad_middle = grad_out + mid_back(grad_second * gain_two)[0]
    grad_branch = (active * grad_middle).astype(jnp.bfloat16)
    grad_mixed = through(
        grad_branch, lax.all_gather(output_weight, ("dp", "seq"), axis=0, tiled=True)
    )
    grad_mixed_local = grad_mixed.astype(jnp.bfloat16).reshape(seq_count, local_len, width)

    def backward_group(group_index, state):
        grad_query_all, grad_key_all, grad_value_all = state
        start_col = group_index * group_width
        q_part, k_part, v_part, scores = group_parts(start_col)
        g_part = lax.dynamic_slice_in_dim(grad_mixed_local, start_col, group_width, 2).reshape(
            seq_count, local_len, group, HEAD_DIM
        )
        lse_part = lax.dynamic_slice_in_dim(log_total, group_index * group, group, 1)
        soft = jnp.exp(scores - lse_part[..., None])
        grad_probs = jnp.einsum(
            "sqhd,skhd->shqk", g_part, v_part, preferred_element_type=jnp.float32
        )
        value_term = jnp.einsum(
            "shqk,sqhd->skhd", soft.astype(jnp.bfloat16), g_part, preferred_element_type=jnp.float32
        )
        centered = jnp.sum(soft * grad_probs, axis=-1, keepdims=True)
        grad_scores = (soft * (grad_probs - centered)).astype(jnp.bfloat16)
        query_term = (
            jnp.einsum("shqk,skhd->sqhd", grad_scores, k_part, preferred_element_type=jnp.float32)
            * factor
        )
        key_term = (
            jnp.einsum("shqk,sqhd->skhd", grad_scores, q_part, preferred_element_type=jnp.float32)
            * factor
        )
        grad_query_all = lax.dynamic_update_slice_in_dim(
            grad_query_all, query_term.reshape(seq_count, local_len, group_width), start_col, 2
        )
        grad_key_all = lax.dynamic_update_slice_in_dim(
            grad_key_all, key_term.reshape(seq_count, full_len, group_width), start_col, 2
        )
        grad_value_all = lax.dynamic_update_slice_in_dim(
            grad_value_all, value_term.reshape(seq_count, full_len, group_width), start_col, 2
        )
        return (grad_query_all, grad_key_all, grad_value_all)

    grad_query_all, grad_key_all, grad_value_all = lax.fori_loop(
        0,
        group_total,
        backward_group,
        (
            jnp.zeros((seq_count, local_len, width), jnp.float32),
            jnp.zeros((seq_count, full_len, width), jnp.float32),
            jnp.zeros((seq_count, full_len, width), jnp.float32),
        ),
    )
    key_sum, value_sum = (
        lax.psum_scatter(grad_key_all, "seq", scatter_dimension=1, tiled=True),
        lax.psum_scatter(grad_value_all, "seq", scatter_dimension=1, tiled=True),
    )
    grad_query = grad_query_all.astype(jnp.bfloat16).reshape(total_rows, width)
    grad_key = key_sum.astype(jnp.bfloat16).reshape(total_rows, width)
    grad_value = value_sum.astype(jnp.bfloat16).reshape(total_rows, width)
    total = through(grad_query, lax.all_gather(query_weight, ("dp", "seq"), axis=0, tiled=True))
    total = total + through(grad_key, lax.all_gather(key_weight, ("dp", "seq"), axis=0, tiled=True))
    grad_first = total + through(
        grad_value, lax.all_gather(value_weight, ("dp", "seq"), axis=0, tiled=True)
    )
    in_value, in_back = jax.vjp(normalize, inputs)
    tokens_grad = (
        (grad_middle + in_back(grad_first * gain_one)[0])
        .astype(jnp.bfloat16)
        .reshape(seq_count, local_len, width)
    )
    first_scaled = grad_first * normed_in
    second_scaled = grad_second * normed_mid
    vectors = jnp.stack(
        [
            column_total(grad_query),
            column_total(grad_value),
            column_total(grad_branch),
            column_total(grad_shrunk),
            column_total(first_scaled),
            column_total(grad_first),
            column_total(second_scaled),
            column_total(grad_second),
        ],
        axis=1,
    )

    def scattered(grad_cols, inputs):
        return lax.psum_scatter(
            outer_rows(grad_cols, inputs), ("dp", "seq"), scatter_dimension=0, tiled=True
        )

    vector_sums = lax.psum_scatter(vectors, ("dp", "seq"), scatter_dimension=0, tiled=True)
    expand_bias_sums = lax.psum_scatter(
        column_total(grad_pre), ("dp", "seq"), scatter_dimension=0, tiled=True
    )
    shrink_sums = scattered(grad_shrunk, activated)
    grad_pre, second_rows, shrink_sums = lax.optimization_barrier(
        (grad_pre, second_rows, shrink_sums)
    )
    expand_sums = scattered(grad_pre, second_rows)
    grad_branch, grad_query, grad_key, grad_value, expand_sums = lax.optimization_barrier(
        (grad_branch, grad_query, grad_key, grad_value, expand_sums)
    )
    return (
        layer_out,
        tokens_grad,
        vector_sums[:, 4],
        vector_sums[:, 5],
        scattered(grad_query, first_rows),
        vector_sums[:, 0],
        scattered(grad_key, first_rows),
        scattered(grad_value, first_rows),
        vector_sums[:, 1],
        scattered(grad_branch, mixed),
        vector_sums[:, 2],
        vector_sums[:, 6],
        vector_sums[:, 7],
        expand_sums,
        expand_bias_sums,
        shrink_sums,
        vector_sums[:, 3],
    )


def solution(mesh):
    chips = mesh.shape["dp"] // 2
    if chips == 4 and mesh.shape["seq"] == 4:
        names = ("y", "x", "core", "seq")
        mesh = Mesh(mesh.devices.reshape(2, 2, 2, 4), names)
        dp, rows, per_device = names[:3], names, whole_sequence_device
    else:
        dp, rows, per_device = "dp", ("dp", "seq"), general_device
    in_specs = (
        P(dp, "seq", None),
        P(dp, "seq"),
        P(rows),
        P(rows),
        P(rows, None),
        P(rows),
        P(rows, None),
        P(rows, None),
        P(rows),
        P(rows, None),
        P(rows),
        P(rows),
        P(rows),
        P(rows, None),
        P(rows),
        P(rows, None),
        P(rows),
        P(dp, "seq", None),
    )
    out_specs = (
        P(dp, "seq", None),
        P(dp, "seq", None),
        P(rows),
        P(rows),
        P(rows, None),
        P(rows),
        P(rows, None),
        P(rows, None),
        P(rows),
        P(rows, None),
        P(rows),
        P(rows),
        P(rows),
        P(rows, None),
        P(rows),
        P(rows, None),
        P(rows),
    )
    return jax.shard_map(
        per_device, mesh=mesh, in_specs=in_specs, out_specs=out_specs, check_vma=False
    )
```

```python
import math

import jax
import jax.numpy as jnp
from jax import lax
from jax.experimental import pallas as pl
from jax.experimental.pallas import tpu as pltpu
from jax.sharding import Mesh, PartitionSpec as P

HEAD_DIM = 64
LAYER = 12


EPS = 1e-05


def normalize(values):
    center = values - jnp.mean(values, axis=-1, keepdims=True)
    spread = jnp.mean(center * center, axis=-1, keepdims=True)
    return center * lax.rsqrt(spread + EPS)


def project(left, weight):
    return lax.dot_general(
        left, weight, (((1,), (1,)), ((), ())), preferred_element_type=jnp.float32
    )


def through(left, weight):
    return jnp.dot(left, weight, preferred_element_type=jnp.float32)


def outer_rows(grad_cols, inputs):
    return lax.dot_general(
        grad_cols, inputs, (((0,), (0,)), ((), ())), preferred_element_type=jnp.float32
    )


def place_cols(buffer, piece):
    return piece.astype(buffer.dtype)


def column_total(matrix):
    return jnp.sum(matrix, axis=0, dtype=jnp.float32)


BRIEF = pl.CostEstimate(flops=1, bytes_accessed=1, transcendentals=0)

CORE, ALONG_X, ALONG_Y = "core", "x", "y"
DEVICES = ("y", "x", "core", "seq")


def swap(values, axis):
    return lax.ppermute(values, axis, [(0, 1), (1, 0)])


def pick(flag, first, second):
    return jnp.where(flag == 0, first, second)


def ordered(flag, own, other, axis):
    return pick(
        flag, jnp.concatenate([own, other], axis), jnp.concatenate([other, own], axis)
    )


def arrange(pieces, block, sources, targets):
    count = len(pieces)
    steps = len(sources)
    table = jnp.stack([jnp.asarray(target, jnp.int32) for target in targets])

    def kernel(table_ref, *refs):
        step = pl.program_id(0)
        for index in range(count):
            mine = [at for at, source in enumerate(sources) if source[0] == index]

            @pl.when((step >= mine[0]) & (step <= mine[-1]))
            def _():
                refs[count][...] = refs[index][...]

    def place_of(index):
        mine = [at for at, source in enumerate(sources) if source[0] == index]

        def block_of(step, table_ref):
            row, column = sources[mine[0]][1:]
            for at in mine[1:]:
                row = jnp.where(step >= at, sources[at][1], row)
                column = jnp.where(step >= at, sources[at][2], column)
            return row, column

        return block_of

    total = steps * block[0] * block[1]
    return pl.pallas_call(
        kernel,
        grid_spec=pltpu.PrefetchScalarGridSpec(
            num_scalar_prefetch=1,
            grid=(steps,),
            in_specs=[pl.BlockSpec(block, place_of(index)) for index in range(count)],
            out_specs=pl.BlockSpec(block, lambda step, table_ref: (table_ref[step], 0)),
        ),
        out_shape=jax.ShapeDtypeStruct((steps * block[0], block[1]), pieces[0].dtype),
        compiler_params=pltpu.CompilerParams(vmem_limit_bytes=28 << 20),
        cost_estimate=BRIEF,
        name="arrange",
    )(table, *pieces)


def split_kernel(table_ref, first, second, first_out, second_out):
    first_out[...] = first[...]
    second_out[...] = second[...]


def split_columns(core, matrix, block):
    rows, columns = matrix.shape
    count = columns // block // 2
    piece = jax.ShapeDtypeStruct((rows, columns // 2), matrix.dtype)
    return pl.pallas_call(
        split_kernel,
        grid_spec=pltpu.PrefetchScalarGridSpec(
            num_scalar_prefetch=1,
            grid=(count,),
            in_specs=[
                pl.BlockSpec((rows, block), lambda i, core_ref: (0, 2 * i + core_ref[0])),
                pl.BlockSpec((rows, block), lambda i, core_ref: (0, 2 * i + 1 - core_ref[0])),
            ],
            out_specs=[pl.BlockSpec((rows, block), lambda i, core_ref: (0, i))] * 2,
        ),
        out_shape=(piece, piece),
        compiler_params=pltpu.CompilerParams(vmem_limit_bytes=28 << 20),
        cost_estimate=BRIEF,
        name="split_columns",
    )(core.reshape(1), matrix, matrix)


def weave_kernel(core_ref, mine, theirs, out):
    block = mine.shape[1]

    @pl.when(core_ref[0] == 0)
    def _():
        out[:, :block] = mine[...]
        out[:, block:] = theirs[...]

    @pl.when(core_ref[0] == 1)
    def _():
        out[:, :block] = theirs[...]
        out[:, block:] = mine[...]


def weave_columns(core, mine, theirs, block):
    rows, columns = mine.shape
    return pl.pallas_call(
        weave_kernel,
        grid_spec=pltpu.PrefetchScalarGridSpec(
            num_scalar_prefetch=1,
            grid=(columns // block,),
            in_specs=[pl.BlockSpec((rows, block), lambda i, core_ref: (0, i))] * 2,
            out_specs=pl.BlockSpec((rows, 2 * block), lambda i, core_ref: (0, i)),
        ),
        out_shape=jax.ShapeDtypeStruct((rows, 2 * columns), mine.dtype),
        compiler_params=pltpu.CompilerParams(vmem_limit_bytes=28 << 20),
        cost_estimate=BRIEF,
        name="weave_columns",
    )(core.reshape(1), mine, theirs)


def outer_rows_of(lefts, rights, rows, sources, tile=512, runs=None):
    count, columns = rights[0].shape
    terms, blocks = len(lefts), len(sources)
    table = jnp.stack([jnp.asarray(index, jnp.int32) for index in [*sources, *(runs or [])]])

    def kernel(table_ref, *refs):
        total = 0.0
        for left, right in zip(refs[:terms], refs[terms : 2 * terms]):
            total = total + lax.dot_general(
                left[...], right[...], (((0,), (0,)), ((), ())), preferred_element_type=jnp.float32
            )
        total = total.astype(jnp.bfloat16)
        if runs is None:
            refs[-1][...] = total
        else:
            for at in range(len(runs)):
                start = pl.multiple_of(table_ref[blocks + at] * HEAD_DIM, HEAD_DIM)
                refs[-1][pl.ds(start, HEAD_DIM), :] = total[at * HEAD_DIM : (at + 1) * HEAD_DIM]

    return pl.pallas_call(
        kernel,
        grid_spec=pltpu.PrefetchScalarGridSpec(
            num_scalar_prefetch=1,
            grid=(blocks, columns // tile),
            in_specs=[pl.BlockSpec((count, rows), lambda i, j, ref: (0, ref[i]))] * terms
            + [pl.BlockSpec((count, tile), lambda i, j, ref: (0, j))] * terms,
            out_specs=pl.BlockSpec((rows, tile), lambda i, j, ref: (i, j)),
        ),
        out_shape=jax.ShapeDtypeStruct((blocks * rows, columns), jnp.bfloat16),
        compiler_params=pltpu.CompilerParams(vmem_limit_bytes=28 << 20),
        cost_estimate=BRIEF,
        name="outer_rows_of",
    )(table, *lefts, *rights)


def outer_sides(indices, left, right, rows):
    count, columns = right.shape
    pieces = len(indices) // 2
    table = jnp.stack([jnp.asarray(index, jnp.int32) for index in indices])

    def kernel(table_ref, left, right, *outs):
        step = pl.program_id(0)
        total = lax.dot_general(
            left[...], right[...], (((0,), (0,)), ((), ())), preferred_element_type=jnp.float32
        ).astype(jnp.bfloat16)
        for piece, out in enumerate(outs):

            @pl.when(step // 2 == piece)
            def _():
                out[...] = total

    def side_of(piece):
        return lambda step, table_ref: (0, jnp.clip(step - 2 * piece, 0, 1))

    return pl.pallas_call(
        kernel,
        grid_spec=pltpu.PrefetchScalarGridSpec(
            num_scalar_prefetch=1,
            grid=(2 * pieces,),
            in_specs=[
                pl.BlockSpec((count, rows), lambda step, table_ref: (0, table_ref[step])),
                pl.BlockSpec((count, columns), lambda step, table_ref: (0, 0)),
            ],
            out_specs=[pl.BlockSpec((rows, columns), side_of(piece)) for piece in range(pieces)],
        ),
        out_shape=[jax.ShapeDtypeStruct((rows, 2 * columns), jnp.bfloat16)] * pieces,
        compiler_params=pltpu.CompilerParams(vmem_limit_bytes=28 << 20),
        cost_estimate=BRIEF,
        name="outer_sides",
    )(table, left, right)


def regroup(bits, matrix, seq_size):
    rows, columns = matrix.shape
    block = 256

    def kernel(bits_ref, matrix, out):
        for flips in range(8):
            y_flip, x_flip, core_flip = flips // 4, flips // 2 % 2, flips % 2

            @pl.when(4 * bits_ref[0] + 2 * bits_ref[1] + bits_ref[2] == flips)
            def _():
                runs = [
                    (((y ^ y_flip) * 2 + (x ^ x_flip)) * 2 + (side ^ core_flip)) * seq_size + z
                    for z in range(seq_size)
                    for y in range(2)
                    for x in range(2)
                    for side in range(2)
                ]
                out[...] = jnp.concatenate(
                    [matrix[:, run * HEAD_DIM : (run + 1) * HEAD_DIM] for run in runs], axis=1
                )

    return pl.pallas_call(
        kernel,
        grid_spec=pltpu.PrefetchScalarGridSpec(
            num_scalar_prefetch=1,
            grid=(rows // block,),
            in_specs=[pl.BlockSpec((block, columns), lambda i, bits_ref: (i, 0))],
            out_specs=pl.BlockSpec((block, columns), lambda i, bits_ref: (i, 0)),
        ),
        out_shape=jax.ShapeDtypeStruct((rows, columns), matrix.dtype),
        compiler_params=pltpu.CompilerParams(vmem_limit_bytes=28 << 20),
        cost_estimate=BRIEF,
        name="regroup",
    )(bits, matrix)


def regroup_back(bits, mine, got, seq_size, dtype):
    rows, columns = mine.shape
    block = 128

    def kernel(bits_ref, mine, got, out):
        for flips in range(8):
            y_flip, x_flip, core_flip = flips // 4, flips // 2 % 2, flips % 2

            @pl.when(4 * bits_ref[0] + 2 * bits_ref[1] + bits_ref[2] == flips)
            def _():
                runs = [
                    ((z * 2 + (y ^ y_flip)) * 2 + (x ^ x_flip)) * 2 + (side ^ core_flip)
                    for y in range(2)
                    for x in range(2)
                    for side in range(2)
                    for z in range(seq_size)
                ]
                own = [mine[:, run * HEAD_DIM : (run + 1) * HEAD_DIM] for run in runs]
                runs = [run ^ 1 for run in runs]
                other = [got[:, run * HEAD_DIM : (run + 1) * HEAD_DIM] for run in runs]
                out[...] = (
                    jnp.concatenate(own, axis=1)
                    + jnp.concatenate(other, axis=1).astype(jnp.float32)
                ).astype(dtype)

    spec = pl.BlockSpec((block, columns), lambda i, bits_ref: (i, 0))
    return pl.pallas_call(
        kernel,
        grid_spec=pltpu.PrefetchScalarGridSpec(
            num_scalar_prefetch=1,
            grid=(rows // block,),
            in_specs=[spec, spec],
            out_specs=spec,
        ),
        out_shape=jax.ShapeDtypeStruct((rows, columns), dtype),
        compiler_params=pltpu.CompilerParams(vmem_limit_bytes=28 << 20),
        cost_estimate=BRIEF,
        name="regroup_back",
    )(bits, mine, got)


def half_dot(which, left, right, by_columns, dtype, tile=512, places=None):
    lefts = left if places is not None else (left,)
    rows, depth = lefts[0].shape
    columns = right.shape[0] if by_columns else right.shape[1]
    contract = 1 if by_columns else 0
    count = len(lefts)
    table = jnp.stack([which, *(places or [])])

    def kernel(table_ref, *refs):
        total = 0.0
        for index in range(count):
            total = total + lax.dot_general(
                refs[index][...],
                refs[count + index][...],
                (((1,), (contract,)), ((), ())),
                preferred_element_type=jnp.float32,
            )
        refs[-1][...] = total.astype(dtype)

    def right_block(index):
        if by_columns:
            return pl.BlockSpec((tile, depth), lambda i, table_ref: (i, 0))
        if places is None:
            return pl.BlockSpec((depth, tile), lambda i, table_ref: (0, i))
        return pl.BlockSpec((depth, tile), lambda i, table_ref: (table_ref[1 + index], i))

    return pl.pallas_call(
        kernel,
        grid_spec=pltpu.PrefetchScalarGridSpec(
            num_scalar_prefetch=1,
            grid=(columns // tile,),
            in_specs=[
                pl.BlockSpec((rows // 2, depth), lambda i, table_ref: (table_ref[0], 0))
            ]
            * count
            + [right_block(index) for index in range(count)],
            out_specs=pl.BlockSpec((rows // 2, tile), lambda i, table_ref: (0, i)),
        ),
        out_shape=jax.ShapeDtypeStruct((rows // 2, columns), dtype),
        compiler_params=pltpu.CompilerParams(vmem_limit_bytes=28 << 20),
        cost_estimate=BRIEF,
        name="half_dot",
    )(table, *lefts, *[right] * count)


def multiply(
    lefts, rights, by_columns, tile=512, bias=None, slope=None, lift=False, halves=False
):
    rows = lefts[0].shape[0]
    terms = len(lefts)
    columns = rights[0].shape[0] if by_columns else rights[0].shape[1]
    contract = 1 if by_columns else 0
    extra = [] if bias is None else [bias]
    extra += [] if slope is None else [slope]
    across = pl.BlockSpec((rows, tile), lambda i: (0, i))
    row = pl.BlockSpec((1, tile), lambda i: (0, i))
    wide = jax.ShapeDtypeStruct((rows, columns), jnp.bfloat16)
    outs = [(across, wide)]
    if halves:
        part = pl.BlockSpec((rows // 2, tile), lambda i: (0, i))
        outs = [(part, jax.ShapeDtypeStruct((rows // 2, columns), jnp.bfloat16))] * 2
    if lift:
        outs.append((across, wide))
    if slope is not None:
        outs.append((row, jax.ShapeDtypeStruct((1, columns), jnp.float32)))

    def kernel(*refs):
        total = 0.0
        for left, right in zip(refs[:terms], refs[terms : 2 * terms]):
            total = total + lax.dot_general(
                left[...],
                right[...],
                (((1,), (contract,)), ((), ())),
                preferred_element_type=jnp.float32,
            )
        rest = refs[2 * terms :]
        if bias is not None:
            total = total + rest[0][...]
        out = rest[len(extra)]
        if lift:
            lifted = 0.5 * (1.0 + lax.erf(total * (0.5**0.5)))
            bell = jnp.exp(-0.5 * total * total) * ((0.5 / math.pi) ** 0.5)
            out[...] = (total * lifted).astype(jnp.bfloat16)
            rest[len(extra) + 1][...] = (lifted + total * bell).astype(jnp.bfloat16)
        elif slope is not None:
            low = (total * rest[len(extra) - 1][...].astype(jnp.float32)).astype(jnp.bfloat16)
            out[...] = low
            rest[len(extra) + 1][...] = jnp.sum(low.astype(jnp.float32), axis=0, keepdims=True)
        elif halves:
            out[...] = total[: rows // 2].astype(jnp.bfloat16)
            rest[len(extra) + 1][...] = total[rows // 2 :].astype(jnp.bfloat16)
        else:
            out[...] = total.astype(jnp.bfloat16)

    def right_spec(right):
        if by_columns:
            return pl.BlockSpec((tile, right.shape[1]), lambda i: (i, 0))
        return pl.BlockSpec((right.shape[0], tile), lambda i: (0, i))

    result = pl.pallas_call(
        kernel,
        grid=(columns // tile,),
        in_specs=[pl.BlockSpec(left.shape, lambda i: (0, 0)) for left in lefts]
        + [right_spec(right) for right in rights]
        + ([] if bias is None else [row])
        + ([] if slope is None else [across]),
        out_specs=[spec for spec, _ in outs],
        out_shape=[shape for _, shape in outs],
        compiler_params=pltpu.CompilerParams(vmem_limit_bytes=28 << 20),
        cost_estimate=BRIEF,
        name="multiply",
    )(*lefts, *rights, *extra)
    return result if len(outs) > 1 else result[0]


def add_low(left, right):
    return (left.astype(jnp.float32) + right.astype(jnp.float32)).astype(jnp.bfloat16)


BLOCK = 256


def softmax_block(index, keys_wide, query_wide):
    start = index * BLOCK
    tiles = []
    if index > 0:
        tiles.append(
            lax.dot_general(
                keys_wide[:start],
                query_wide,
                (((1,), (1,)), ((), ())),
                preferred_element_type=jnp.float32,
            )
        )
    last = lax.dot_general(
        keys_wide[start : start + BLOCK],
        query_wide,
        (((1,), (1,)), ((), ())),
        preferred_element_type=jnp.float32,
    )
    key_pos = lax.broadcasted_iota(jnp.int32, last.shape, 0)
    query_pos = lax.broadcasted_iota(jnp.int32, last.shape, 1)
    tiles.append(jnp.where(key_pos <= query_pos, last, jnp.float32(-1e30)))
    peak = jnp.max(tiles[-1], axis=0, keepdims=True)
    if index > 0:
        peak = jnp.maximum(peak, jnp.max(tiles[0], axis=0, keepdims=True))
    tiles = [jnp.exp(tile - peak) for tile in tiles]
    total = sum(jnp.sum(tile, axis=0, keepdims=True) for tile in tiles)
    inverse = 1.0 / total
    return [tile * inverse for tile in tiles]


def widen(head, rows_ref, mask_ref):
    first = 3 * HEAD_DIM * head
    query = rows_ref[:, first : first + HEAD_DIM] * jnp.bfloat16(HEAD_DIM**-0.5)
    keys = rows_ref[:, first + HEAD_DIM : first + 2 * HEAD_DIM]
    values = rows_ref[:, first + 2 * HEAD_DIM : first + 3 * HEAD_DIM]
    even = jnp.full(query.shape, 1.0 / HEAD_DIM, jnp.bfloat16)
    query_wide = jnp.concatenate([query, even], axis=1)
    keys_wide = jnp.concatenate([keys, mask_ref[...]], axis=1)
    return query, keys, values, query_wide, keys_wide


def attend_kernel(rows_ref, mask_ref, out_ref):
    blocks = rows_ref.shape[0] // BLOCK
    results = [[], []]
    for head in range(2):
        _, _, values, query_wide, keys_wide = widen(head, rows_ref, mask_ref)
        for index in range(blocks):
            start, stop = index * BLOCK, (index + 1) * BLOCK
            tiles = softmax_block(index, keys_wide, query_wide[start:stop])
            low = jnp.concatenate([tile.astype(jnp.bfloat16) for tile in tiles], axis=0)
            outcome = lax.dot_general(
                values[:stop], low, (((0,), (0,)), ((), ())), preferred_element_type=jnp.float32
            )
            results[head].append(outcome.T)
    for index in range(blocks):
        both = jnp.concatenate([results[0][index], results[1][index]], axis=1)
        out_ref[index * BLOCK : (index + 1) * BLOCK, :] = both.astype(jnp.bfloat16)


def attend_back_kernel(rows_ref, grad_ref, mask_ref, out_ref, key_sum, value_sum):
    blocks = rows_ref.shape[0] // BLOCK
    columns = []
    for head in range(2):
        query, keys, values, query_wide, keys_wide = widen(head, rows_ref, mask_ref)
        grad = grad_ref[:, head * HEAD_DIM : (head + 1) * HEAD_DIM]
        query_parts = []
        for index in reversed(range(blocks)):
            start, stop = index * BLOCK, (index + 1) * BLOCK
            tiles = softmax_block(index, keys_wide, query_wide[start:stop])
            soft = jnp.concatenate(tiles, axis=0)
            grad_rows = grad[start:stop]
            grad_probs = lax.dot_general(
                values[:stop],
                grad_rows,
                (((1,), (1,)), ((), ())),
                preferred_element_type=jnp.float32,
            )
            weighted = soft * grad_probs
            delta = jnp.sum(weighted, axis=0, keepdims=True)
            grad_scores = (weighted - soft * delta).astype(jnp.bfloat16)
            value_term = jnp.dot(
                soft.astype(jnp.bfloat16), grad_rows, preferred_element_type=jnp.float32
            )
            key_term = jnp.dot(
                grad_scores, query[start:stop], preferred_element_type=jnp.float32
            )
            if index == blocks - 1:
                value_sum[...] = value_term
                key_sum[...] = key_term
            else:
                value_sum[:stop, :] += value_term
                key_sum[:stop, :] += key_term
            outcome = lax.dot_general(
                keys[:stop],
                grad_scores,
                (((0,), (0,)), ((), ())),
                preferred_element_type=jnp.float32,
            )
            query_parts.insert(0, outcome.T * jnp.float32(HEAD_DIM**-0.5))
        columns += [jnp.concatenate(query_parts, axis=0), key_sum[...], value_sum[...]]
    out_ref[...] = jnp.concatenate([part.astype(jnp.bfloat16) for part in columns], axis=1)


def attend(rows, mask):
    count, columns = rows.shape
    pairs = columns // (6 * HEAD_DIM)
    work = pairs * 2 * count * count * HEAD_DIM
    return pl.pallas_call(
        attend_kernel,
        grid=(pairs,),
        in_specs=[
            pl.BlockSpec((count, 6 * HEAD_DIM), lambda i: (0, i)),
            pl.BlockSpec((count, HEAD_DIM), lambda i: (0, 0)),
        ],
        out_specs=pl.BlockSpec((count, 2 * HEAD_DIM), lambda i: (0, i)),
        out_shape=jax.ShapeDtypeStruct((count, pairs * 2 * HEAD_DIM), jnp.bfloat16),
        compiler_params=pltpu.CompilerParams(vmem_limit_bytes=28 << 20),
        cost_estimate=BRIEF,
        name="attend",
    )(rows, mask)


def attend_back(rows, grad, mask, place):
    count, columns = rows.shape
    pairs = columns // (6 * HEAD_DIM) // 4

    def kernel(place_ref, *refs):
        attend_back_kernel(*refs)

    return pl.pallas_call(
        kernel,
        grid_spec=pltpu.PrefetchScalarGridSpec(
            num_scalar_prefetch=1,
            grid=(pairs,),
            in_specs=[
                pl.BlockSpec(
                    (count, 6 * HEAD_DIM), lambda i, place_ref: (0, pairs * place_ref[0] + i)
                ),
                pl.BlockSpec(
                    (count, 2 * HEAD_DIM), lambda i, place_ref: (0, pairs * place_ref[0] + i)
                ),
                pl.BlockSpec((count, HEAD_DIM), lambda i, place_ref: (0, 0)),
            ],
            out_specs=pl.BlockSpec((count, 6 * HEAD_DIM), lambda i, place_ref: (0, i)),
            scratch_shapes=[pltpu.VMEM((count, HEAD_DIM), jnp.float32)] * 2,
        ),
        out_shape=jax.ShapeDtypeStruct((count, columns // 4), jnp.bfloat16),
        compiler_params=pltpu.CompilerParams(vmem_limit_bytes=28 << 20),
        cost_estimate=BRIEF,
        name="attend_back",
    )(place.reshape(1), rows, grad, mask)


ROWS = 128


def normal_parts(values):
    center = values - jnp.mean(values, axis=-1, keepdims=True)
    spread_of = jnp.mean(center * center, axis=-1, keepdims=True)
    scale = lax.rsqrt(spread_of + EPS)
    return center * scale, scale


def normal_back(normed, scale, grad):
    mean_grad = jnp.mean(grad, axis=-1, keepdims=True)
    mean_product = jnp.mean(grad * normed, axis=-1, keepdims=True)
    return (grad - mean_grad - normed * mean_product) * scale


def first_kernel(start_ref, tokens, gain, shift, out):
    normed, _ = normal_parts(tokens[...].astype(jnp.float32))
    out[...] = (normed * gain[...] + shift[...]).astype(out.dtype)


def middle_kernel(
    start_ref,
    tokens,
    own_upper,
    own_lower,
    upper,
    lower,
    active,
    bias,
    gain,
    shift,
    middle_out,
    rows_out,
):
    in_upper = pl.program_id(0) < pl.num_programs(0) // 2
    own = jnp.where(in_upper, own_upper[...], own_lower[...])
    got = jnp.where(in_upper, upper[...], lower[...])
    branch = own.astype(jnp.float32) + got.astype(jnp.float32) + bias[...]
    middle = tokens[...].astype(jnp.float32) + active[...] * branch
    middle_out[...] = middle
    normed, _ = normal_parts(middle)
    rows_out[...] = (normed * gain[...] + shift[...]).astype(rows_out.dtype)


def add_totals(totals, parts):
    first = pl.program_id(0) == 0
    for index, part in enumerate(parts):
        total = jnp.sum(part, axis=0, keepdims=True)
        totals[index : index + 1, :] = total + jnp.where(
            first, 0.0, totals[index : index + 1, :]
        )


def middle_back_kernel(
    start_ref,
    cotangent,
    middle,
    own,
    upper,
    lower,
    peer,
    active,
    gain,
    grad_out,
    branch_out,
    totals,
):
    in_upper = pl.program_id(0) < pl.num_programs(0) // 2
    got = jnp.where(in_upper, upper[...], lower[...])
    grad_second = own[...] + got.astype(jnp.float32) + peer[...].astype(jnp.float32)
    normed, scale = normal_parts(middle[...])
    grad_middle = cotangent[...].astype(jnp.float32) + normal_back(
        normed, scale, grad_second * gain[...]
    )
    grad_out[...] = grad_middle
    grad_branch = (active[...] * grad_middle).astype(jnp.bfloat16)
    branch_out[...] = grad_branch
    add_totals(
        totals, (grad_second * normed, grad_second, grad_branch.astype(jnp.float32))
    )


def first_back_kernel(start_ref, tokens, grad_middle, own, got, gain, grad_out, totals):
    grad_first = own[...] + got[...].astype(jnp.float32)
    normed, scale = normal_parts(tokens[...].astype(jnp.float32))
    grad = grad_middle[...] + normal_back(normed, scale, grad_first * gain[...])
    grad_out[...] = grad.astype(grad_out.dtype)
    add_totals(totals, (grad_first * normed, grad_first))


def by_rows(kernel, start, count, arrays, outs, name):
    width = arrays[0][0].shape[1]
    specs = {
        "rows": pl.BlockSpec((ROWS, width), lambda i, start_ref: (i, 0)),
        "from": pl.BlockSpec((ROWS, width), lambda i, start_ref: (start_ref[0] + i, 0)),
        "vector": pl.BlockSpec((1, width), lambda i, start_ref: (0, 0)),
        "totals": pl.BlockSpec((8, width), lambda i, start_ref: (0, 0)),
        "upper": pl.BlockSpec(
            (ROWS, width), lambda i, start_ref: (jnp.minimum(i, count // ROWS // 2 - 1), 0)
        ),
        "lower": pl.BlockSpec(
            (ROWS, width), lambda i, start_ref: (jnp.maximum(i - count // ROWS // 2, 0), 0)
        ),
        "flag": pl.BlockSpec((ROWS, 1), lambda i, start_ref: (i, 0)),
        "flag from": pl.BlockSpec((ROWS, 1), lambda i, start_ref: (start_ref[0] + i, 0)),
    }
    shapes = [
        jax.ShapeDtypeStruct((8 if kind == "totals" else count, width), dtype)
        for kind, dtype in outs
    ]
    moved = sum(
        count * width * array.dtype.itemsize for array, kind in arrays if kind in ("rows", "from")
    ) + sum(math.prod(shape.shape) * shape.dtype.itemsize for shape in shapes)
    return pl.pallas_call(
        kernel,
        grid_spec=pltpu.PrefetchScalarGridSpec(
            num_scalar_prefetch=1,
            grid=(count // ROWS,),
            in_specs=[specs[kind] for _, kind in arrays],
            out_specs=[specs[kind] for kind, _ in outs],
        ),
        out_shape=shapes,
        compiler_params=pltpu.CompilerParams(vmem_limit_bytes=28 << 20),
        cost_estimate=BRIEF,
        name=name,
    )(start, *[array for array, _ in arrays])


def after(value, *others):
    return lax.optimization_barrier((value, others))[0]


MIDDLE_KINDS = ("rows", "upper", "lower", "upper", "lower", "flag", "vector", "vector", "vector")
BACK_KINDS = ("from", "from", "rows", "upper", "lower", "rows", "flag from", "vector")


class Line:
    def __init__(self):
        self.last = None

    def __call__(self, function, *arrays):
        if self.last is not None:
            arrays = lax.optimization_barrier((arrays, self.last))[0]
        result = function(*arrays)
        self.last = jax.tree.leaves(result)[0]
        return result


def whole_sequence_device(
    tokens,
    exit_layer,
    first_gain,
    first_shift,
    query_weight,
    query_bias,
    key_weight,
    value_weight,
    value_bias,
    output_weight,
    output_bias,
    second_gain,
    second_shift,
    expand_weight,
    expand_bias,
    shrink_weight,
    shrink_bias,
    cotangent,
):
    seq_count, local_len, width = tokens.shape
    heads_rows = query_weight.shape[0]
    hidden_rows = expand_weight.shape[0]
    seq_size = lax.axis_size("seq")
    dp_size = lax.axis_size(DEVICES) // seq_size
    depth, core = lax.axis_index("seq"), lax.axis_index("core")
    along_x, along_y = lax.axis_index("x"), lax.axis_index("y")
    place = 2 * along_y + along_x
    dp = 2 * place + core
    parity = depth % 2
    full_len = local_len * seq_size
    half_len = full_len // 2
    f32, low = jnp.float32, jnp.bfloat16

    def route(flip):
        pairs = []
        for i in range(dp_size):
            for j in range(seq_size):
                target = 2 * (i % 2) + (j % 2 if not flip else 1 - j % 2)
                pairs.append((i * seq_size + j, (i // 2 * 2 + j // 2) * seq_size + target))
        return pairs

    def send(first, second, back):
        routes = [[(b, a) if back else (a, b) for a, b in route(flip)] for flip in (False, True)]
        return lax.ppermute(first, DEVICES, routes[0]), lax.ppermute(second, DEVICES, routes[1])

    def by_parity(values):
        return pick(parity, values[0], values[1]), pick(parity, values[1], values[0])

    def paired(first, second):
        return ordered(parity, first[None], second[None], 0)

    def by_core(own, other):
        return ordered(core, own, other, 0)

    def half_rows(matrix, which):
        return lax.dynamic_slice_in_dim(matrix, which * half_len, half_len, 0)

    line = Line()
    depth_rows = heads_rows * seq_size
    hidden_block = hidden_rows * seq_size
    places = [place ^ d for d in range(4)]
    sides = [core, 1 - core]
    bits = jnp.stack([along_y, along_x, core])

    def through_z(shard):
        return lax.all_gather(shard, "seq", axis=0, tiled=True)

    devices = dp_size * seq_size
    all_dp = jnp.arange(dp_size, dtype=jnp.int32)[:, None]
    all_seq = jnp.arange(seq_size, dtype=jnp.int32)[None, :]
    relative = ((all_dp ^ dp) * seq_size + (depth - all_seq) % seq_size).reshape(-1)

    def shift_z(values, steps):
        return lax.ppermute(
            values, "seq", [(i, (i + steps) % seq_size) for i in range(seq_size)]
        )

    def stacked(own, other):
        return jnp.concatenate([own, other], 0)

    vectors = [first_gain, first_shift, query_bias, value_bias, output_bias, second_gain]
    vectors += [second_shift, shrink_bias, expand_bias]
    shard_qkv = line(
        lambda *parts: jnp.concatenate(parts, 0), query_weight, key_weight, value_weight
    )
    z_qkv = through_z(shard_qkv)
    vectors = line(lambda *parts: jnp.concatenate(parts)[None, None], *vectors)
    shifted = [shift_z(vectors, steps) for steps in range(1, seq_size)]
    alive = (exit_layer > LAYER).astype(low)
    flag_rows = jnp.broadcast_to(alive[:, None, :], (seq_count, 16, local_len))
    flag_rows = jnp.pad(flag_rows, ((0, 0), (0, 0), (0, width - local_len)))
    message = line(
        lambda *arrays: by_parity(jnp.concatenate(arrays, axis=1)), tokens, flag_rows, cotangent
    )
    vectors = line(lambda *parts: jnp.concatenate(parts, 1), vectors, *shifted)
    mine, theirs = line(lambda rows: split_columns(core, rows, hidden_block), shrink_weight)
    theirs = swap(theirs, CORE)
    vectors = line(stacked, vectors, swap(vectors, ALONG_Y))
    shard_shrink = line(stacked, mine, theirs)
    mine, theirs = line(lambda rows: split_columns(along_x, rows, hidden_block), shard_shrink)
    theirs = swap(theirs, ALONG_X)
    vectors = line(stacked, vectors, swap(vectors, ALONG_X))
    shard_shrink = line(stacked, mine, theirs)
    vectors = line(stacked, vectors, swap(vectors, CORE))
    vectors = line(
        lambda rows: rows.reshape(2, 2, 2, seq_size, -1)
        .transpose(2, 1, 0, 3, 4)
        .reshape(devices, -1)[relative]
        .astype(f32),
        vectors,
    )
    shrink_across = swap(shard_shrink, ALONG_Y)

    def vector(index):
        return vectors[:, index * heads_rows : (index + 1) * heads_rows].reshape(1, -1)

    def of_core(matrix):
        cut = matrix.reshape(4, 2, seq_size, -1)
        return lax.dynamic_index_in_dim(cut, core, 1, False).reshape(4 * seq_size, -1)

    def of_quarter(matrix):
        cut = matrix.reshape(2, 4, seq_size, -1)
        return lax.dynamic_index_in_dim(cut, 2 * along_x + core, 1, False)

    gain_one, shift_one = vector(0), vector(1)
    bias_query = of_core(vectors[:, 2 * heads_rows : 3 * heads_rows])
    bias_value = of_core(vectors[:, 3 * heads_rows : 4 * heads_rows])
    bias_rows = jnp.stack([bias_query, jnp.zeros_like(bias_query), bias_value], 1).reshape(1, -1)
    bias_out, gain_two, shift_two, bias_shrink = vector(4), vector(5), vector(6), vector(7)
    bias_expand = of_quarter(vectors[:, 8 * heads_rows :]).reshape(1, -1)

    half_qkv = 3 * depth_rows // 2

    z_qkv = after(z_qkv, vectors, shard_shrink)
    beside_qkv, across_qkv = swap(z_qkv, ALONG_X), swap(z_qkv, ALONG_Y)
    z_out = through_z(after(output_weight, z_qkv))
    arrived = send(*(after(part, z_out) for part in message), False)
    mine, theirs = line(lambda rows: split_columns(core, rows, depth_rows), z_out)
    rows_out = line(
        lambda own, other: jnp.concatenate([own, other], 1), mine, swap(theirs, CORE)
    )
    upper = line(lambda rows: rows[:half_qkv], beside_qkv)
    lower = line(lambda rows: rows[half_qkv:], across_qkv)
    upper, lower = swap(upper, ALONG_Y), swap(lower, ALONG_X)
    z_expand = through_z(after(expand_weight, *arrived))
    w_qkv = line(
        lambda *pieces: arrange(
            pieces,
            (half_qkv, width),
            [(p, r, 0) for p in range(3) for r in range(2)] + [(3, 0, 0), (4, 0, 0)],
            [2 * places[d] + r for d in range(4) for r in range(2)],
        ),
        z_qkv,
        beside_qkv,
        across_qkv,
        upper,
        lower,
    )
    half = line(paired, *arrived)
    joined = line(by_core, half, swap(half, CORE))
    inputs = joined[:, :local_len].reshape(full_len, width)
    alive = joined[:, local_len, :local_len].reshape(full_len, 1)
    cotangent_full = joined[:, local_len + 16 :].reshape(full_len, width)
    active = alive.astype(f32)
    mask = jnp.broadcast_to((alive - 1) * jnp.bfloat16(1e30), (full_len, HEAD_DIM))

    no_start = jnp.zeros((1,), jnp.int32)
    half_start = (core * (half_len // ROWS)).reshape(1)

    (first_rows,) = line(
        lambda *arrays: by_rows(
            first_kernel,
            no_start,
            full_len,
            list(zip(arrays, ("rows", "vector", "vector"))),
            [("rows", low)],
            "first_norm",
        ),
        inputs,
        gain_one,
        shift_one,
    )
    rows_out = after(rows_out, w_qkv)
    out_beside, out_across = swap(rows_out, ALONG_X), swap(rows_out, ALONG_Y)
    across_expand = swap(z_expand, ALONG_Y)

    qkv = line(
        lambda rows, weight: multiply((rows,), (weight,), True, bias=bias_rows), first_rows, w_qkv
    )
    out_corner = swap(line(lambda rows: rows * jnp.bfloat16(1), out_across), ALONG_X)
    grad_shrunk = line(
        lambda flags, grads: (flags * grads.astype(f32)).astype(low), active, cotangent_full
    )
    sent_gs = line(lambda rows: half_rows(rows, core), grad_shrunk)
    gs_got = swap(sent_gs, ALONG_X)
    mixed = line(attend, qkv, mask)
    w_out = line(
        lambda *pieces: arrange(
            pieces,
            (depth_rows, width // 2),
            [(p, 0, i) for p in range(4) for i in range(2)],
            [2 * places[d] + sides[i] for d in range(4) for i in range(2)],
        ),
        after(rows_out, z_expand),
        out_beside,
        out_across,
        out_corner,
    )
    branch = line(
        lambda rows, weight: multiply((rows,), (weight,), True, halves=True), mixed, w_out
    )
    branch_got = [swap(part, CORE) for part in branch]
    shard_shrink = line(stacked, shard_shrink, shrink_across)
    w_shrink = through_z(after(shard_shrink, z_expand, branch))
    middle, second_rows = line(
        lambda *arrays: by_rows(
            middle_kernel,
            no_start,
            full_len,
            list(zip(arrays, MIDDLE_KINDS)),
            [("rows", f32), ("rows", low)],
            "middle_norm",
        ),
        inputs,
        *branch,
        *branch_got,
        active,
        bias_out,
        gain_two,
        shift_two,
    )
    second_half = line(lambda rows: half_rows(rows, core), second_rows)
    second_got = swap(second_half, ALONG_X)
    gs_own = line(lambda rows: regroup(bits, rows, seq_size), grad_shrunk)
    w_expand = line(
        lambda *pieces: arrange(
            pieces,
            (hidden_block // 2, width),
            [(p, r, 0) for p in range(2) for r in range(2)],
            [2 * (along_y ^ p) + r for p in range(2) for r in range(2)],
        ),
        z_expand,
        across_expand,
    )

    def lift(rows, weight):
        return multiply((rows,), (weight,), True, bias=bias_expand, lift=True)

    activated, slope = line(lift, second_rows, w_expand)
    second_peer = line(by_core, second_got, swap(second_got, CORE))
    activated_peer, slope_peer = line(lift, second_peer, w_expand)

    gs_peer = line(by_core, gs_got, swap(after(gs_got, activated), CORE))
    gs_peer = line(lambda rows: regroup(bits, rows, seq_size), gs_peer)
    def scatter_z(total):
        return lax.psum_scatter(total, "seq", scatter_dimension=0, tiled=True)

    def units(grads, weight, slopes):
        return multiply((grads,), (weight,), False, slope=slopes)

    def their_half(left, weight, by_columns=False):
        return half_dot(1 - core, left, weight, by_columns, low)

    def my_half(left, weight, by_columns=False):
        return half_dot(core, left, weight, by_columns, f32)

    def add_rounded(left, right):
        return (left.astype(f32) + right.astype(f32)).astype(low)

    shrink_part = line(
        lambda own, peer, rows, rows_peer: outer_rows_of(
            (own, peer), (rows, rows_peer), width // 2, range(2)
        ),
        gs_own,
        gs_peer,
        activated,
        activated_peer,
    )
    shrink_rows = scatter_z(shrink_part)
    grad_pre_peer, peer_sums = line(units, gs_peer, w_shrink, slope_peer)
    theirs = line(their_half, grad_pre_peer, w_expand)
    mine = line(my_half, grad_pre_peer, w_expand)
    peer_half = line(add_rounded, mine, swap(theirs, CORE))
    second_from_peer = swap(peer_half, ALONG_X)
    grad_pre, own_sums = line(units, gs_own, w_shrink, slope)
    theirs = line(their_half, grad_pre, w_expand)
    second_got = [swap(part, CORE) for part in jnp.split(theirs, 2)]
    second_mine = line(my_half, grad_pre, w_expand)
    def expand_part(d):
        return line(
            lambda *arrays: outer_rows_of(arrays[:2], arrays[2:], hidden_block, [along_y ^ d]),
            grad_pre,
            grad_pre_peer,
            second_rows,
            second_peer,
        )

    expand_across = expand_part(1)
    expand_got = swap(expand_across, ALONG_Y)

    grad_middle, grad_branch_half, middle_totals = line(
        lambda *arrays: by_rows(
            middle_back_kernel,
            half_start,
            half_len,
            list(zip(arrays, BACK_KINDS)),
            [("rows", f32), ("rows", low), ("totals", f32)],
            "middle_norm_back",
        ),
        cotangent_full,
        middle,
        second_mine,
        *second_got,
        second_from_peer,
        active,
        gain_two,
    )
    branch_got = swap(grad_branch_half, CORE)

    grad_branch = line(by_core, grad_branch_half, branch_got)
    grad_mixed = line(
        lambda grads, weight: multiply((grads,), (weight,), False, tile=256), grad_branch, w_out
    )
    out_part = line(
        lambda grads, rows: outer_sides(
            [2 * places[d] + sides[i] for d in range(4) for i in range(2)], grads, rows, depth_rows
        ),
        grad_branch,
        mixed,
    )
    out_parts = [out_part[d] for d in range(4)]
    out_corner = swap(out_parts[3], ALONG_X)
    out_got_x = swap(out_parts[1], ALONG_X)

    def attend_piece(d):
        return line(
            lambda rows, grads, flags: attend_back(rows, grads, flags, places[d]),
            qkv,
            grad_mixed,
            mask,
        )

    def qkv_part(d, rows, source):
        return line(
            lambda grads, inputs_low: outer_rows_of((grads,), (inputs_low,), rows, [source]),
            grad_qkv[d],
            first_rows,
        )

    grad_qkv = {3: attend_piece(3)}
    corner_got = swap(after(qkv_part(3, 2 * half_qkv, 0), out_corner), ALONG_X)
    grad_qkv[1] = attend_piece(1)
    out_got_y = swap(line(add_rounded, out_parts[2], out_corner), ALONG_Y)
    qkv_x = swap(qkv_part(1, 2 * half_qkv, 0), ALONG_X)
    grad_qkv[2] = attend_piece(2)
    across = qkv_part(2, 2 * half_qkv, 0)
    expand_here = expand_part(0)
    grad_qkv[0] = attend_piece(0)
    qkv_y = swap(line(add_rounded, across, corner_got), ALONG_Y)
    expand_sum = line(add_rounded, expand_here, expand_got)
    expand_rows = scatter_z(expand_sum)
    here = qkv_part(0, 2 * half_qkv, 0)
    grads_qkv = tuple(grad_qkv[d] for d in range(4))

    def first_half(which, dtype):
        return lambda *arrays: half_dot(which, arrays[:4], arrays[4], False, dtype, places=places)

    peer_theirs = line(lambda rows, weight: their_half(rows, weight, True), activated_peer, w_shrink)
    peer_got = swap(peer_theirs, CORE)
    first_theirs = line(first_half(1 - core, low), *grads_qkv, w_qkv)
    first_got = swap(first_theirs, CORE)
    peer_mine = line(lambda rows, weight: my_half(rows, weight, True), activated_peer, w_shrink)
    first_mine = line(first_half(core, f32), *grads_qkv, w_qkv)
    to_peer = line(
        lambda *parts: regroup_back(bits, *parts, seq_size, low), peer_mine, peer_got
    )
    from_peer = swap(to_peer, ALONG_X)
    half = shrink_rows.shape[0] // 2
    shrink_got = swap(line(lambda rows: rows[half:], shrink_rows), ALONG_Y)
    qkv_sum = line(
        lambda *parts: sum(part.astype(f32) for part in parts).astype(low), here, qkv_x, qkv_y
    )
    qkv_rows = scatter_z(qkv_sum)
    grad_half, first_totals = line(
        lambda *arrays: by_rows(
            first_back_kernel,
            half_start,
            half_len,
            list(zip(arrays, ("from", "rows", "rows", "rows", "vector"))),
            [("rows", low), ("totals", f32)],
            "first_norm_back",
        ),
        inputs,
        grad_middle,
        first_mine,
        first_got,
        gain_one,
    )
    tokens_parts = send(
        *line(lambda rows: by_parity(rows.reshape(2, local_len, width)), grad_half), True
    )

    def beside_own(peer, rows, flags, bias):
        return half_rows(rows, core) + half_rows(flags, core) * (peer.astype(f32) + bias)

    rest = line(beside_own, from_peer, middle, active, bias_shrink)

    def column_sum(matrix):
        return jnp.sum(matrix.astype(f32), axis=0)

    def all_devices(totals, rows):
        return totals.reshape(devices, rows)

    def core_devices(totals, rows):
        cut = totals.reshape(4, 1, seq_size, rows)
        return ordered(core, cut, jnp.zeros_like(cut), 1).reshape(devices, rows)

    def quarter_devices(totals, rows):
        cut = totals.reshape(2, 1, seq_size, rows)
        none = jnp.zeros_like(cut)
        quarters = [jnp.where(2 * along_x + core == q, cut, none) for q in range(4)]
        return jnp.concatenate(quarters, 1).reshape(devices, rows)

    def all_sums(first, middle_sums, shrunk_grads, own, peer, *grads):
        qkv_sums = jnp.stack([column_sum(part) for part in grads])[jnp.stack(places)]
        qkv_sums = qkv_sums.reshape(4 * seq_size, 3, heads_rows)
        sums = jnp.concatenate(
            [
                all_devices(first[0], heads_rows),
                all_devices(first[1], heads_rows),
                core_devices(qkv_sums[:, 0], heads_rows),
                core_devices(qkv_sums[:, 2], heads_rows),
                all_devices(middle_sums[2], heads_rows),
                all_devices(middle_sums[0], heads_rows),
                all_devices(middle_sums[1], heads_rows),
                all_devices(0.5 * column_sum(shrunk_grads), heads_rows),
                quarter_devices(own + peer, hidden_rows),
            ],
            axis=1,
        )
        return sums.reshape(dp_size, seq_size, -1)[jnp.arange(dp_size) ^ dp]

    def fold(values, got):
        return values[: got.shape[0]] + got

    sums = line(
        all_sums, first_totals, middle_totals, grad_shrunk, own_sums, peer_sums, *grads_qkv
    )
    theirs = line(lambda rows, weight: their_half(rows, weight, True), activated, w_shrink)
    shrunk_got = swap(theirs, CORE)
    sums = line(fold, sums, swap(sums[dp_size // 2 :], ALONG_Y))
    mine = line(lambda rows, weight: my_half(rows, weight, True), activated, w_shrink)
    sums = line(fold, sums, swap(sums[dp_size // 4 :], ALONG_X))
    shrunk = line(lambda *parts: regroup_back(bits, *parts, seq_size, f32), mine, shrunk_got)

    def finish(part, other, flags):
        out = other + half_rows(flags, core) * part
        return by_parity(out.astype(low).reshape(2, local_len, width))

    out_halves = send(*line(finish, shrunk, rest, active), True)
    sums = line(fold, sums, swap(sums[dp_size // 8 :], CORE))
    out_sum = line(
        lambda *parts: sum(part.astype(f32) for part in parts).astype(low),
        out_parts[0],
        out_got_x,
        out_got_y,
    )
    out_got = swap(line(lambda rows: rows[:, width // 2 :], out_sum), CORE)
    tokens_grad = line(paired, *tokens_parts)
    out_rows = line(
        lambda rows, got: weave_columns(core, rows[:, : width // 2], got, depth_rows),
        out_sum,
        out_got,
    )

    def with_vectors(totals, rows):
        totals = totals.reshape(seq_size, 1, -1).astype(low)
        totals = jnp.pad(totals, ((0, 0), (0, 15), (0, width - totals.shape[2])))
        rows = jnp.concatenate([rows.reshape(seq_size, -1, width), totals], 1)
        return rows.reshape(-1, width)

    out_rows = scatter_z(line(with_vectors, sums, out_rows))

    shrink_rows = line(lambda rows, got: add_rounded(rows[:half], got), shrink_rows, shrink_got)
    half = half // 2
    shrink_got = swap(line(lambda rows: rows[half:], shrink_rows), ALONG_X)
    expand_weight_grad = line(lambda rows: rows.astype(f32), expand_rows)
    qkv_weight_grad = line(lambda rows: rows.astype(f32), qkv_rows)
    shrink_rows = line(
        lambda rows, got: weave_columns(along_x, rows[:half], got, hidden_block),
        shrink_rows,
        shrink_got,
    )
    shrink_got = swap(line(lambda rows: rows[heads_rows:], shrink_rows), CORE)
    layer_out = line(paired, *out_halves)
    shrink_weight_grad = line(
        lambda rows, got: weave_columns(core, rows[:heads_rows], got, hidden_block).astype(f32),
        shrink_rows,
        shrink_got,
    )
    output_weight_grad, sums = line(
        lambda rows: (
            rows[:heads_rows].astype(f32),
            rows[heads_rows, : 8 * heads_rows + hidden_rows].astype(f32),
        ),
        out_rows,
    )

    def vector_grad(index):
        return sums[index * heads_rows : (index + 1) * heads_rows]

    return (
        layer_out,
        tokens_grad,
        vector_grad(0),
        vector_grad(1),
        qkv_weight_grad[:heads_rows],
        vector_grad(2),
        qkv_weight_grad[heads_rows : 2 * heads_rows],
        qkv_weight_grad[2 * heads_rows :],
        vector_grad(3),
        output_weight_grad,
        vector_grad(4),
        vector_grad(5),
        vector_grad(6),
        expand_weight_grad,
        sums[8 * heads_rows :],
        shrink_weight_grad,
        vector_grad(7),
    )


def general_device(
    tokens,
    exit_layer,
    first_gain,
    first_shift,
    query_weight,
    query_bias,
    key_weight,
    value_weight,
    value_bias,
    output_weight,
    output_bias,
    second_gain,
    second_shift,
    expand_weight,
    expand_bias,
    shrink_weight,
    shrink_bias,
    cotangent,
):
    seq_count, local_len, width = tokens.shape
    hidden_width = shrink_weight.shape[1]
    total_rows = seq_count * local_len
    heads = width // HEAD_DIM
    inputs = tokens.reshape(total_rows, width).astype(jnp.float32)
    active = (exit_layer > LAYER).astype(jnp.float32).reshape(total_rows, 1)
    gain_one, shift_one = (
        lax.all_gather(first_gain, ("dp", "seq"), axis=0, tiled=True),
        lax.all_gather(first_shift, ("dp", "seq"), axis=0, tiled=True),
    )
    gain_one = gain_one.astype(jnp.float32)
    shift_one = shift_one.astype(jnp.float32)
    normed_in = normalize(inputs)
    first_rows = (normed_in * gain_one + shift_one).astype(jnp.bfloat16)
    blank = jnp.zeros((total_rows, width), jnp.bfloat16)
    attention_init = (blank, blank, blank) + ()
    w_query = lax.all_gather(query_weight, ("dp", "seq"), axis=0, tiled=True)
    b_query = lax.all_gather(query_bias, ("dp", "seq"), axis=0, tiled=True)
    w_key = lax.all_gather(key_weight, ("dp", "seq"), axis=0, tiled=True)
    w_value = lax.all_gather(value_weight, ("dp", "seq"), axis=0, tiled=True)
    b_value = lax.all_gather(value_bias, ("dp", "seq"), axis=0, tiled=True)
    queries = place_cols(
        attention_init[0], project(first_rows, w_query) + b_query.astype(jnp.float32)
    )
    key_rows = place_cols(attention_init[1], project(first_rows, w_key))
    value_rows = place_cols(
        attention_init[2], project(first_rows, w_value) + b_value.astype(jnp.float32)
    )
    stored = attention_init[3:]
    gathered = (queries, key_rows, value_rows) + stored
    queries, key_rows, value_rows = (gathered[0], gathered[1], gathered[2])
    query_local = queries.reshape(seq_count, local_len, width)
    key_local = key_rows.reshape(seq_count, local_len, width)
    value_local = value_rows.reshape(seq_count, local_len, width)
    alive_local = active.reshape(seq_count, local_len)
    key_all, value_all, alive_all = (
        lax.all_gather(key_local, "seq", axis=1, tiled=True),
        lax.all_gather(value_local, "seq", axis=1, tiled=True),
        lax.all_gather(alive_local.astype(jnp.bfloat16), "seq", axis=1, tiled=True),
    )
    full_len = key_all.shape[1]
    offset = lax.axis_index("seq") * local_len
    query_pos = offset + jnp.arange(local_len, dtype=jnp.int32)
    key_pos = jnp.arange(full_len, dtype=jnp.int32)
    causal = key_pos[None, :] <= query_pos[:, None]
    allowed = causal[None, None] & (alive_all.astype(jnp.float32)[:, None, None, :] > 0.5)
    factor = HEAD_DIM ** (-0.5)
    group = min(8, heads)
    group_width = group * HEAD_DIM
    group_total = heads // group

    def group_parts(start_col):
        q_part = lax.dynamic_slice_in_dim(query_local, start_col, group_width, 2).reshape(
            seq_count, local_len, group, HEAD_DIM
        )
        k_part = lax.dynamic_slice_in_dim(key_all, start_col, group_width, 2).reshape(
            seq_count, full_len, group, HEAD_DIM
        )
        v_part = lax.dynamic_slice_in_dim(value_all, start_col, group_width, 2).reshape(
            seq_count, full_len, group, HEAD_DIM
        )
        scores = (
            jnp.einsum("sqhd,skhd->shqk", q_part, k_part, preferred_element_type=jnp.float32)
            * factor
        )
        scores = jnp.where(allowed, scores, jnp.float32(-1e30))
        return (q_part, k_part, v_part, scores)

    def forward_group(group_index, state):
        mixed_all, log_total = state
        start_col = group_index * group_width
        q_part, k_part, v_part, scores = group_parts(start_col)
        row_max = jnp.max(scores, axis=-1, keepdims=True)
        raised = jnp.exp(scores - row_max)
        totals = jnp.sum(raised, axis=-1, keepdims=True)
        weights_low = (raised / totals).astype(jnp.bfloat16)
        outcome = jnp.einsum(
            "shqk,skhd->sqhd", weights_low, v_part, preferred_element_type=jnp.float32
        )
        mixed_all = lax.dynamic_update_slice_in_dim(
            mixed_all,
            outcome.reshape(seq_count, local_len, group_width).astype(jnp.bfloat16),
            start_col,
            2,
        )
        log_total = lax.dynamic_update_slice_in_dim(
            log_total, (row_max + jnp.log(totals))[..., 0], group_index * group, 1
        )
        return (mixed_all, log_total)

    mixed_all, log_total = lax.fori_loop(
        0,
        group_total,
        forward_group,
        (
            jnp.zeros((seq_count, local_len, width), jnp.bfloat16),
            jnp.zeros((seq_count, heads, local_len), jnp.float32),
        ),
    )
    mixed = mixed_all.reshape(total_rows, width)
    vector_blank = jnp.zeros((width,), jnp.bfloat16)
    output_init = (jnp.zeros((total_rows, width), jnp.float32), vector_blank, vector_blank) + ()
    w_out = lax.all_gather(output_weight, ("dp", "seq"), axis=0, tiled=True)
    b_out = lax.all_gather(output_bias, ("dp", "seq"), axis=0, tiled=True)
    g_piece = lax.all_gather(second_gain, ("dp", "seq"), axis=0, tiled=True)
    s_piece = lax.all_gather(second_shift, ("dp", "seq"), axis=0, tiled=True)
    branch = place_cols(output_init[0], project(mixed, w_out) + b_out.astype(jnp.float32))
    gain_two = g_piece
    shift_two = s_piece
    stored = output_init[3:]
    folded = (branch, gain_two, shift_two) + stored
    branch = folded[0]
    gain_two = folded[1].astype(jnp.float32)
    shift_two = folded[2].astype(jnp.float32)
    middle = inputs + active * branch
    normed_mid = normalize(middle)
    second_rows = (normed_mid * gain_two + shift_two).astype(jnp.bfloat16)
    expand_init = (jnp.zeros((total_rows, hidden_width), jnp.float32),) + ()
    w_expand = lax.all_gather(expand_weight, ("dp", "seq"), axis=0, tiled=True)
    b_expand = lax.all_gather(expand_bias, ("dp", "seq"), axis=0, tiled=True)
    hidden_pre = place_cols(
        expand_init[0], project(second_rows, w_expand) + b_expand.astype(jnp.float32)
    )
    stored = expand_init[1:]
    expanded = (hidden_pre,) + stored
    hidden_pre = expanded[0]

    def gelu_exact(pre_values):
        return jax.nn.gelu(pre_values, approximate=False)

    activated_full, gelu_back = jax.vjp(gelu_exact, hidden_pre)
    activated = activated_full.astype(jnp.bfloat16)
    shrink_init = (jnp.zeros((total_rows, width), jnp.float32),) + ()
    w_shrink = lax.all_gather(shrink_weight, ("dp", "seq"), axis=0, tiled=True)
    b_shrink = lax.all_gather(shrink_bias, ("dp", "seq"), axis=0, tiled=True)
    shrunk = place_cols(shrink_init[0], project(activated, w_shrink) + b_shrink.astype(jnp.float32))
    stored = shrink_init[1:]
    shrunk_all = (shrunk,) + stored
    shrunk = shrunk_all[0]
    layer_out = (middle + active * shrunk).astype(jnp.bfloat16).reshape(seq_count, local_len, width)
    grad_out = cotangent.reshape(total_rows, width).astype(jnp.float32)
    grad_shrunk = (active * grad_out).astype(jnp.bfloat16)
    grad_units = through(
        grad_shrunk, lax.all_gather(shrink_weight, ("dp", "seq"), axis=0, tiled=True)
    )
    grad_pre = gelu_back(grad_units)[0].astype(jnp.bfloat16)
    grad_second = through(
        grad_pre, lax.all_gather(expand_weight, ("dp", "seq"), axis=0, tiled=True)
    )
    mid_value, mid_back = jax.vjp(normalize, middle)
    grad_middle = grad_out + mid_back(grad_second * gain_two)[0]
    grad_branch = (active * grad_middle).astype(jnp.bfloat16)
    grad_mixed = through(
        grad_branch, lax.all_gather(output_weight, ("dp", "seq"), axis=0, tiled=True)
    )
    grad_mixed_local = grad_mixed.astype(jnp.bfloat16).reshape(seq_count, local_len, width)

    def backward_group(group_index, state):
        grad_query_all, grad_key_all, grad_value_all = state
        start_col = group_index * group_width
        q_part, k_part, v_part, scores = group_parts(start_col)
        g_part = lax.dynamic_slice_in_dim(grad_mixed_local, start_col, group_width, 2).reshape(
            seq_count, local_len, group, HEAD_DIM
        )
        lse_part = lax.dynamic_slice_in_dim(log_total, group_index * group, group, 1)
        soft = jnp.exp(scores - lse_part[..., None])
        grad_probs = jnp.einsum(
            "sqhd,skhd->shqk", g_part, v_part, preferred_element_type=jnp.float32
        )
        value_term = jnp.einsum(
            "shqk,sqhd->skhd", soft.astype(jnp.bfloat16), g_part, preferred_element_type=jnp.float32
        )
        centered = jnp.sum(soft * grad_probs, axis=-1, keepdims=True)
        grad_scores = (soft * (grad_probs - centered)).astype(jnp.bfloat16)
        query_term = (
            jnp.einsum("shqk,skhd->sqhd", grad_scores, k_part, preferred_element_type=jnp.float32)
            * factor
        )
        key_term = (
            jnp.einsum("shqk,sqhd->skhd", grad_scores, q_part, preferred_element_type=jnp.float32)
            * factor
        )
        grad_query_all = lax.dynamic_update_slice_in_dim(
            grad_query_all, query_term.reshape(seq_count, local_len, group_width), start_col, 2
        )
        grad_key_all = lax.dynamic_update_slice_in_dim(
            grad_key_all, key_term.reshape(seq_count, full_len, group_width), start_col, 2
        )
        grad_value_all = lax.dynamic_update_slice_in_dim(
            grad_value_all, value_term.reshape(seq_count, full_len, group_width), start_col, 2
        )
        return (grad_query_all, grad_key_all, grad_value_all)

    grad_query_all, grad_key_all, grad_value_all = lax.fori_loop(
        0,
        group_total,
        backward_group,
        (
            jnp.zeros((seq_count, local_len, width), jnp.float32),
            jnp.zeros((seq_count, full_len, width), jnp.float32),
            jnp.zeros((seq_count, full_len, width), jnp.float32),
        ),
    )
    key_sum, value_sum = (
        lax.psum_scatter(grad_key_all, "seq", scatter_dimension=1, tiled=True),
        lax.psum_scatter(grad_value_all, "seq", scatter_dimension=1, tiled=True),
    )
    grad_query = grad_query_all.astype(jnp.bfloat16).reshape(total_rows, width)
    grad_key = key_sum.astype(jnp.bfloat16).reshape(total_rows, width)
    grad_value = value_sum.astype(jnp.bfloat16).reshape(total_rows, width)
    total = through(grad_query, lax.all_gather(query_weight, ("dp", "seq"), axis=0, tiled=True))
    total = total + through(grad_key, lax.all_gather(key_weight, ("dp", "seq"), axis=0, tiled=True))
    grad_first = total + through(
        grad_value, lax.all_gather(value_weight, ("dp", "seq"), axis=0, tiled=True)
    )
    in_value, in_back = jax.vjp(normalize, inputs)
    tokens_grad = (
        (grad_middle + in_back(grad_first * gain_one)[0])
        .astype(jnp.bfloat16)
        .reshape(seq_count, local_len, width)
    )
    first_scaled = grad_first * normed_in
    second_scaled = grad_second * normed_mid
    vectors = jnp.stack(
        [
            column_total(grad_query),
            column_total(grad_value),
            column_total(grad_branch),
            column_total(grad_shrunk),
            column_total(first_scaled),
            column_total(grad_first),
            column_total(second_scaled),
            column_total(grad_second),
        ],
        axis=1,
    )

    def scattered(grad_cols, inputs):
        return lax.psum_scatter(
            outer_rows(grad_cols, inputs), ("dp", "seq"), scatter_dimension=0, tiled=True
        )

    vector_sums = lax.psum_scatter(vectors, ("dp", "seq"), scatter_dimension=0, tiled=True)
    expand_bias_sums = lax.psum_scatter(
        column_total(grad_pre), ("dp", "seq"), scatter_dimension=0, tiled=True
    )
    shrink_sums = scattered(grad_shrunk, activated)
    grad_pre, second_rows, shrink_sums = lax.optimization_barrier(
        (grad_pre, second_rows, shrink_sums)
    )
    expand_sums = scattered(grad_pre, second_rows)
    grad_branch, grad_query, grad_key, grad_value, expand_sums = lax.optimization_barrier(
        (grad_branch, grad_query, grad_key, grad_value, expand_sums)
    )
    return (
        layer_out,
        tokens_grad,
        vector_sums[:, 4],
        vector_sums[:, 5],
        scattered(grad_query, first_rows),
        vector_sums[:, 0],
        scattered(grad_key, first_rows),
        scattered(grad_value, first_rows),
        vector_sums[:, 1],
        scattered(grad_branch, mixed),
        vector_sums[:, 2],
        vector_sums[:, 6],
        vector_sums[:, 7],
        expand_sums,
        expand_bias_sums,
        shrink_sums,
        vector_sums[:, 3],
    )


def solution(mesh):
    chips = mesh.shape["dp"] // 2
    if chips == 4 and mesh.shape["seq"] == 4:
        names = ("y", "x", "core", "seq")
        mesh = Mesh(mesh.devices.reshape(2, 2, 2, 4), names)
        dp, rows, per_device = names[:3], names, whole_sequence_device
    else:
        dp, rows, per_device = "dp", ("dp", "seq"), general_device
    in_specs = (
        P(dp, "seq", None),
        P(dp, "seq"),
        P(rows),
        P(rows),
        P(rows, None),
        P(rows),
        P(rows, None),
        P(rows, None),
        P(rows),
        P(rows, None),
        P(rows),
        P(rows),
        P(rows),
        P(rows, None),
        P(rows),
        P(rows, None),
        P(rows),
        P(dp, "seq", None),
    )
    out_specs = (
        P(dp, "seq", None),
        P(dp, "seq", None),
        P(rows),
        P(rows),
        P(rows, None),
        P(rows),
        P(rows, None),
        P(rows, None),
        P(rows),
        P(rows, None),
        P(rows),
        P(rows),
        P(rows),
        P(rows, None),
        P(rows),
        P(rows, None),
        P(rows),
    )
    return jax.shard_map(
        per_device, mesh=mesh, in_specs=in_specs, out_specs=out_specs, check_vma=False
    )
```

```python
import math

import jax
import jax.numpy as jnp
from jax import lax
from jax.experimental import pallas as pl
from jax.experimental.pallas import tpu as pltpu
from jax.sharding import Mesh, PartitionSpec as P

HEAD_DIM = 64
LAYER = 12


EPS = 1e-05


def normalize(values):
    center = values - jnp.mean(values, axis=-1, keepdims=True)
    spread = jnp.mean(center * center, axis=-1, keepdims=True)
    return center * lax.rsqrt(spread + EPS)


def project(left, weight):
    return lax.dot_general(
        left, weight, (((1,), (1,)), ((), ())), preferred_element_type=jnp.float32
    )


def through(left, weight):
    return jnp.dot(left, weight, preferred_element_type=jnp.float32)


def outer_rows(grad_cols, inputs):
    return lax.dot_general(
        grad_cols, inputs, (((0,), (0,)), ((), ())), preferred_element_type=jnp.float32
    )


def place_cols(buffer, piece):
    return piece.astype(buffer.dtype)


def column_total(matrix):
    return jnp.sum(matrix, axis=0, dtype=jnp.float32)


BRIEF = pl.CostEstimate(flops=1, bytes_accessed=1, transcendentals=0)

CORE, ALONG_X, ALONG_Y = "core", "x", "y"
DEVICES = ("y", "x", "core", "seq")


def swap(values, axis):
    return lax.ppermute(values, axis, [(0, 1), (1, 0)])


def pick(flag, first, second):
    return jnp.where(flag == 0, first, second)


def ordered(flag, own, other, axis):
    return pick(
        flag, jnp.concatenate([own, other], axis), jnp.concatenate([other, own], axis)
    )


def arrange(pieces, block, sources, targets):
    count = len(pieces)
    steps = len(sources)
    table = jnp.stack([jnp.asarray(target, jnp.int32) for target in targets])

    def kernel(table_ref, *refs):
        step = pl.program_id(0)
        for index in range(count):
            mine = [at for at, source in enumerate(sources) if source[0] == index]

            @pl.when((step >= mine[0]) & (step <= mine[-1]))
            def _():
                refs[count][...] = refs[index][...]

    def place_of(index):
        mine = [at for at, source in enumerate(sources) if source[0] == index]

        def block_of(step, table_ref):
            row, column = sources[mine[0]][1:]
            for at in mine[1:]:
                row = jnp.where(step >= at, sources[at][1], row)
                column = jnp.where(step >= at, sources[at][2], column)
            return row, column

        return block_of

    total = steps * block[0] * block[1]
    return pl.pallas_call(
        kernel,
        grid_spec=pltpu.PrefetchScalarGridSpec(
            num_scalar_prefetch=1,
            grid=(steps,),
            in_specs=[pl.BlockSpec(block, place_of(index)) for index in range(count)],
            out_specs=pl.BlockSpec(block, lambda step, table_ref: (table_ref[step], 0)),
        ),
        out_shape=jax.ShapeDtypeStruct((steps * block[0], block[1]), pieces[0].dtype),
        compiler_params=pltpu.CompilerParams(vmem_limit_bytes=28 << 20),
        cost_estimate=BRIEF,
        name="arrange",
    )(table, *pieces)


def split_kernel(table_ref, first, second, first_out, second_out):
    first_out[...] = first[...]
    second_out[...] = second[...]


def split_columns(core, matrix, block):
    rows, columns = matrix.shape
    count = columns // block // 2
    piece = jax.ShapeDtypeStruct((rows, columns // 2), matrix.dtype)
    return pl.pallas_call(
        split_kernel,
        grid_spec=pltpu.PrefetchScalarGridSpec(
            num_scalar_prefetch=1,
            grid=(count,),
            in_specs=[
                pl.BlockSpec((rows, block), lambda i, core_ref: (0, 2 * i + core_ref[0])),
                pl.BlockSpec((rows, block), lambda i, core_ref: (0, 2 * i + 1 - core_ref[0])),
            ],
            out_specs=[pl.BlockSpec((rows, block), lambda i, core_ref: (0, i))] * 2,
        ),
        out_shape=(piece, piece),
        compiler_params=pltpu.CompilerParams(vmem_limit_bytes=28 << 20),
        cost_estimate=BRIEF,
        name="split_columns",
    )(core.reshape(1), matrix, matrix)


def weave_kernel(core_ref, mine, theirs, out):
    block = mine.shape[1]

    @pl.when(core_ref[0] == 0)
    def _():
        out[:, :block] = mine[...]
        out[:, block:] = theirs[...]

    @pl.when(core_ref[0] == 1)
    def _():
        out[:, :block] = theirs[...]
        out[:, block:] = mine[...]


def weave_columns(core, mine, theirs, block):
    rows, columns = mine.shape
    return pl.pallas_call(
        weave_kernel,
        grid_spec=pltpu.PrefetchScalarGridSpec(
            num_scalar_prefetch=1,
            grid=(columns // block,),
            in_specs=[pl.BlockSpec((rows, block), lambda i, core_ref: (0, i))] * 2,
            out_specs=pl.BlockSpec((rows, 2 * block), lambda i, core_ref: (0, i)),
        ),
        out_shape=jax.ShapeDtypeStruct((rows, 2 * columns), mine.dtype),
        compiler_params=pltpu.CompilerParams(vmem_limit_bytes=28 << 20),
        cost_estimate=BRIEF,
        name="weave_columns",
    )(core.reshape(1), mine, theirs)


def outer_rows_of(lefts, rights, rows, sources, tile=512, runs=None):
    count, columns = rights[0].shape
    terms, blocks = len(lefts), len(sources)
    table = jnp.stack([jnp.asarray(index, jnp.int32) for index in [*sources, *(runs or [])]])

    def kernel(table_ref, *refs):
        total = 0.0
        for left, right in zip(refs[:terms], refs[terms : 2 * terms]):
            total = total + lax.dot_general(
                left[...], right[...], (((0,), (0,)), ((), ())), preferred_element_type=jnp.float32
            )
        total = total.astype(jnp.bfloat16)
        if runs is None:
            refs[-1][...] = total
        else:
            for at in range(len(runs)):
                start = pl.multiple_of(table_ref[blocks + at] * HEAD_DIM, HEAD_DIM)
                refs[-1][pl.ds(start, HEAD_DIM), :] = total[at * HEAD_DIM : (at + 1) * HEAD_DIM]

    return pl.pallas_call(
        kernel,
        grid_spec=pltpu.PrefetchScalarGridSpec(
            num_scalar_prefetch=1,
            grid=(blocks, columns // tile),
            in_specs=[pl.BlockSpec((count, rows), lambda i, j, ref: (0, ref[i]))] * terms
            + [pl.BlockSpec((count, tile), lambda i, j, ref: (0, j))] * terms,
            out_specs=pl.BlockSpec((rows, tile), lambda i, j, ref: (i, j)),
        ),
        out_shape=jax.ShapeDtypeStruct((blocks * rows, columns), jnp.bfloat16),
        compiler_params=pltpu.CompilerParams(vmem_limit_bytes=28 << 20),
        cost_estimate=BRIEF,
        name="outer_rows_of",
    )(table, *lefts, *rights)


def outer_sides(indices, left, right, rows):
    count, columns = right.shape
    pieces = len(indices) // 2
    table = jnp.stack([jnp.asarray(index, jnp.int32) for index in indices])

    def kernel(table_ref, left, right, *outs):
        step = pl.program_id(0)
        total = lax.dot_general(
            left[...], right[...], (((0,), (0,)), ((), ())), preferred_element_type=jnp.float32
        ).astype(jnp.bfloat16)
        for piece, out in enumerate(outs):

            @pl.when(step // 2 == piece)
            def _():
                out[...] = total

    def side_of(piece):
        return lambda step, table_ref: (0, jnp.clip(step - 2 * piece, 0, 1))

    return pl.pallas_call(
        kernel,
        grid_spec=pltpu.PrefetchScalarGridSpec(
            num_scalar_prefetch=1,
            grid=(2 * pieces,),
            in_specs=[
                pl.BlockSpec((count, rows), lambda step, table_ref: (0, table_ref[step])),
                pl.BlockSpec((count, columns), lambda step, table_ref: (0, 0)),
            ],
            out_specs=[pl.BlockSpec((rows, columns), side_of(piece)) for piece in range(pieces)],
        ),
        out_shape=[jax.ShapeDtypeStruct((rows, 2 * columns), jnp.bfloat16)] * pieces,
        compiler_params=pltpu.CompilerParams(vmem_limit_bytes=28 << 20),
        cost_estimate=BRIEF,
        name="outer_sides",
    )(table, left, right)


def regroup(bits, matrix, seq_size):
    rows, columns = matrix.shape
    block = 256

    def kernel(bits_ref, matrix, out):
        for flips in range(8):
            y_flip, x_flip, core_flip = flips // 4, flips // 2 % 2, flips % 2

            @pl.when(4 * bits_ref[0] + 2 * bits_ref[1] + bits_ref[2] == flips)
            def _():
                runs = [
                    (((y ^ y_flip) * 2 + (x ^ x_flip)) * 2 + (side ^ core_flip)) * seq_size + z
                    for z in range(seq_size)
                    for y in range(2)
                    for x in range(2)
                    for side in range(2)
                ]
                out[...] = jnp.concatenate(
                    [matrix[:, run * HEAD_DIM : (run + 1) * HEAD_DIM] for run in runs], axis=1
                )

    return pl.pallas_call(
        kernel,
        grid_spec=pltpu.PrefetchScalarGridSpec(
            num_scalar_prefetch=1,
            grid=(rows // block,),
            in_specs=[pl.BlockSpec((block, columns), lambda i, bits_ref: (i, 0))],
            out_specs=pl.BlockSpec((block, columns), lambda i, bits_ref: (i, 0)),
        ),
        out_shape=jax.ShapeDtypeStruct((rows, columns), matrix.dtype),
        compiler_params=pltpu.CompilerParams(vmem_limit_bytes=28 << 20),
        cost_estimate=BRIEF,
        name="regroup",
    )(bits, matrix)


def regroup_back(bits, mine, got, seq_size, dtype):
    rows, columns = mine.shape
    block = 128

    def kernel(bits_ref, mine, got, out):
        for flips in range(8):
            y_flip, x_flip, core_flip = flips // 4, flips // 2 % 2, flips % 2

            @pl.when(4 * bits_ref[0] + 2 * bits_ref[1] + bits_ref[2] == flips)
            def _():
                runs = [
                    ((z * 2 + (y ^ y_flip)) * 2 + (x ^ x_flip)) * 2 + (side ^ core_flip)
                    for y in range(2)
                    for x in range(2)
                    for side in range(2)
                    for z in range(seq_size)
                ]
                own = [mine[:, run * HEAD_DIM : (run + 1) * HEAD_DIM] for run in runs]
                runs = [run ^ 1 for run in runs]
                other = [got[:, run * HEAD_DIM : (run + 1) * HEAD_DIM] for run in runs]
                out[...] = (
                    jnp.concatenate(own, axis=1)
                    + jnp.concatenate(other, axis=1).astype(jnp.float32)
                ).astype(dtype)

    spec = pl.BlockSpec((block, columns), lambda i, bits_ref: (i, 0))
    return pl.pallas_call(
        kernel,
        grid_spec=pltpu.PrefetchScalarGridSpec(
            num_scalar_prefetch=1,
            grid=(rows // block,),
            in_specs=[spec, spec],
            out_specs=spec,
        ),
        out_shape=jax.ShapeDtypeStruct((rows, columns), dtype),
        compiler_params=pltpu.CompilerParams(vmem_limit_bytes=28 << 20),
        cost_estimate=BRIEF,
        name="regroup_back",
    )(bits, mine, got)


def half_dot(which, left, right, by_columns, dtype, tile=512, places=None):
    lefts = left if places is not None else (left,)
    rows, depth = lefts[0].shape
    columns = right.shape[0] if by_columns else right.shape[1]
    contract = 1 if by_columns else 0
    count = len(lefts)
    table = jnp.stack([which, *(places or [])])

    def kernel(table_ref, *refs):
        total = 0.0
        for index in range(count):
            total = total + lax.dot_general(
                refs[index][...],
                refs[count + index][...],
                (((1,), (contract,)), ((), ())),
                preferred_element_type=jnp.float32,
            )
        refs[-1][...] = total.astype(dtype)

    def right_block(index):
        if by_columns:
            return pl.BlockSpec((tile, depth), lambda i, table_ref: (i, 0))
        if places is None:
            return pl.BlockSpec((depth, tile), lambda i, table_ref: (0, i))
        return pl.BlockSpec((depth, tile), lambda i, table_ref: (table_ref[1 + index], i))

    return pl.pallas_call(
        kernel,
        grid_spec=pltpu.PrefetchScalarGridSpec(
            num_scalar_prefetch=1,
            grid=(columns // tile,),
            in_specs=[
                pl.BlockSpec((rows // 2, depth), lambda i, table_ref: (table_ref[0], 0))
            ]
            * count
            + [right_block(index) for index in range(count)],
            out_specs=pl.BlockSpec((rows // 2, tile), lambda i, table_ref: (0, i)),
        ),
        out_shape=jax.ShapeDtypeStruct((rows // 2, columns), dtype),
        compiler_params=pltpu.CompilerParams(vmem_limit_bytes=28 << 20),
        cost_estimate=BRIEF,
        name="half_dot",
    )(table, *lefts, *[right] * count)


def multiply(
    lefts, rights, by_columns, tile=512, bias=None, slope=None, lift=False, halves=False
):
    rows = lefts[0].shape[0]
    terms = len(lefts)
    columns = rights[0].shape[0] if by_columns else rights[0].shape[1]
    contract = 1 if by_columns else 0
    extra = [] if bias is None else [bias]
    extra += [] if slope is None else [slope]
    across = pl.BlockSpec((rows, tile), lambda i: (0, i))
    row = pl.BlockSpec((1, tile), lambda i: (0, i))
    wide = jax.ShapeDtypeStruct((rows, columns), jnp.bfloat16)
    outs = [(across, wide)]
    if halves:
        part = pl.BlockSpec((rows // 2, tile), lambda i: (0, i))
        outs = [(part, jax.ShapeDtypeStruct((rows // 2, columns), jnp.bfloat16))] * 2
    if lift:
        outs.append((across, wide))
    if slope is not None:
        outs.append((row, jax.ShapeDtypeStruct((1, columns), jnp.float32)))

    def kernel(*refs):
        total = 0.0
        for left, right in zip(refs[:terms], refs[terms : 2 * terms]):
            total = total + lax.dot_general(
                left[...],
                right[...],
                (((1,), (contract,)), ((), ())),
                preferred_element_type=jnp.float32,
            )
        rest = refs[2 * terms :]
        if bias is not None:
            total = total + rest[0][...]
        out = rest[len(extra)]
        if lift:
            lifted = 0.5 * (1.0 + lax.erf(total * (0.5**0.5)))
            bell = jnp.exp(-0.5 * total * total) * ((0.5 / math.pi) ** 0.5)
            out[...] = (total * lifted).astype(jnp.bfloat16)
            rest[len(extra) + 1][...] = (lifted + total * bell).astype(jnp.bfloat16)
        elif slope is not None:
            low = (total * rest[len(extra) - 1][...].astype(jnp.float32)).astype(jnp.bfloat16)
            out[...] = low
            rest[len(extra) + 1][...] = jnp.sum(low.astype(jnp.float32), axis=0, keepdims=True)
        elif halves:
            out[...] = total[: rows // 2].astype(jnp.bfloat16)
            rest[len(extra) + 1][...] = total[rows // 2 :].astype(jnp.bfloat16)
        else:
            out[...] = total.astype(jnp.bfloat16)

    def right_spec(right):
        if by_columns:
            return pl.BlockSpec((tile, right.shape[1]), lambda i: (i, 0))
        return pl.BlockSpec((right.shape[0], tile), lambda i: (0, i))

    result = pl.pallas_call(
        kernel,
        grid=(columns // tile,),
        in_specs=[pl.BlockSpec(left.shape, lambda i: (0, 0)) for left in lefts]
        + [right_spec(right) for right in rights]
        + ([] if bias is None else [row])
        + ([] if slope is None else [across]),
        out_specs=[spec for spec, _ in outs],
        out_shape=[shape for _, shape in outs],
        compiler_params=pltpu.CompilerParams(vmem_limit_bytes=28 << 20),
        cost_estimate=BRIEF,
        name="multiply",
    )(*lefts, *rights, *extra)
    return result if len(outs) > 1 else result[0]


def add_low(left, right):
    return (left.astype(jnp.float32) + right.astype(jnp.float32)).astype(jnp.bfloat16)


BLOCK = 256


def softmax_block(index, keys_wide, query_wide):
    start = index * BLOCK
    tiles = []
    if index > 0:
        tiles.append(
            lax.dot_general(
                keys_wide[:start],
                query_wide,
                (((1,), (1,)), ((), ())),
                preferred_element_type=jnp.float32,
            )
        )
    last = lax.dot_general(
        keys_wide[start : start + BLOCK],
        query_wide,
        (((1,), (1,)), ((), ())),
        preferred_element_type=jnp.float32,
    )
    key_pos = lax.broadcasted_iota(jnp.int32, last.shape, 0)
    query_pos = lax.broadcasted_iota(jnp.int32, last.shape, 1)
    tiles.append(jnp.where(key_pos <= query_pos, last, jnp.float32(-1e30)))
    peak = jnp.max(tiles[-1], axis=0, keepdims=True)
    if index > 0:
        peak = jnp.maximum(peak, jnp.max(tiles[0], axis=0, keepdims=True))
    tiles = [jnp.exp(tile - peak) for tile in tiles]
    total = sum(jnp.sum(tile, axis=0, keepdims=True) for tile in tiles)
    inverse = 1.0 / total
    return [tile * inverse for tile in tiles]


def widen(head, rows_ref, mask_ref):
    first = 3 * HEAD_DIM * head
    query = rows_ref[:, first : first + HEAD_DIM] * jnp.bfloat16(HEAD_DIM**-0.5)
    keys = rows_ref[:, first + HEAD_DIM : first + 2 * HEAD_DIM]
    values = rows_ref[:, first + 2 * HEAD_DIM : first + 3 * HEAD_DIM]
    even = jnp.full(query.shape, 1.0 / HEAD_DIM, jnp.bfloat16)
    query_wide = jnp.concatenate([query, even], axis=1)
    keys_wide = jnp.concatenate([keys, mask_ref[...]], axis=1)
    return query, keys, values, query_wide, keys_wide


def attend_kernel(rows_ref, mask_ref, out_ref):
    blocks = rows_ref.shape[0] // BLOCK
    results = [[], []]
    for head in range(2):
        _, _, values, query_wide, keys_wide = widen(head, rows_ref, mask_ref)
        for index in range(blocks):
            start, stop = index * BLOCK, (index + 1) * BLOCK
            tiles = softmax_block(index, keys_wide, query_wide[start:stop])
            low = jnp.concatenate([tile.astype(jnp.bfloat16) for tile in tiles], axis=0)
            outcome = lax.dot_general(
                values[:stop], low, (((0,), (0,)), ((), ())), preferred_element_type=jnp.float32
            )
            results[head].append(outcome.T)
    for index in range(blocks):
        both = jnp.concatenate([results[0][index], results[1][index]], axis=1)
        out_ref[index * BLOCK : (index + 1) * BLOCK, :] = both.astype(jnp.bfloat16)


def attend_back_kernel(rows_ref, grad_ref, mask_ref, out_ref, key_sum, value_sum):
    blocks = rows_ref.shape[0] // BLOCK
    columns = []
    for head in range(2):
        query, keys, values, query_wide, keys_wide = widen(head, rows_ref, mask_ref)
        grad = grad_ref[:, head * HEAD_DIM : (head + 1) * HEAD_DIM]
        query_parts = []
        for index in reversed(range(blocks)):
            start, stop = index * BLOCK, (index + 1) * BLOCK
            tiles = softmax_block(index, keys_wide, query_wide[start:stop])
            soft = jnp.concatenate(tiles, axis=0)
            grad_rows = grad[start:stop]
            grad_probs = lax.dot_general(
                values[:stop],
                grad_rows,
                (((1,), (1,)), ((), ())),
                preferred_element_type=jnp.float32,
            )
            weighted = soft * grad_probs
            delta = jnp.sum(weighted, axis=0, keepdims=True)
            grad_scores = (weighted - soft * delta).astype(jnp.bfloat16)
            value_term = jnp.dot(
                soft.astype(jnp.bfloat16), grad_rows, preferred_element_type=jnp.float32
            )
            key_term = jnp.dot(
                grad_scores, query[start:stop], preferred_element_type=jnp.float32
            )
            if index == blocks - 1:
                value_sum[...] = value_term
                key_sum[...] = key_term
            else:
                value_sum[:stop, :] += value_term
                key_sum[:stop, :] += key_term
            outcome = lax.dot_general(
                keys[:stop],
                grad_scores,
                (((0,), (0,)), ((), ())),
                preferred_element_type=jnp.float32,
            )
            query_parts.insert(0, outcome.T * jnp.float32(HEAD_DIM**-0.5))
        columns += [jnp.concatenate(query_parts, axis=0), key_sum[...], value_sum[...]]
    out_ref[...] = jnp.concatenate([part.astype(jnp.bfloat16) for part in columns], axis=1)


def attend(rows, mask):
    count, columns = rows.shape
    pairs = columns // (6 * HEAD_DIM)
    work = pairs * 2 * count * count * HEAD_DIM
    return pl.pallas_call(
        attend_kernel,
        grid=(pairs,),
        in_specs=[
            pl.BlockSpec((count, 6 * HEAD_DIM), lambda i: (0, i)),
            pl.BlockSpec((count, HEAD_DIM), lambda i: (0, 0)),
        ],
        out_specs=pl.BlockSpec((count, 2 * HEAD_DIM), lambda i: (0, i)),
        out_shape=jax.ShapeDtypeStruct((count, pairs * 2 * HEAD_DIM), jnp.bfloat16),
        compiler_params=pltpu.CompilerParams(vmem_limit_bytes=28 << 20),
        cost_estimate=BRIEF,
        name="attend",
    )(rows, mask)


def attend_back(rows, grad, mask, place):
    count, columns = rows.shape
    pairs = columns // (6 * HEAD_DIM) // 4

    def kernel(place_ref, *refs):
        attend_back_kernel(*refs)

    return pl.pallas_call(
        kernel,
        grid_spec=pltpu.PrefetchScalarGridSpec(
            num_scalar_prefetch=1,
            grid=(pairs,),
            in_specs=[
                pl.BlockSpec(
                    (count, 6 * HEAD_DIM), lambda i, place_ref: (0, pairs * place_ref[0] + i)
                ),
                pl.BlockSpec(
                    (count, 2 * HEAD_DIM), lambda i, place_ref: (0, pairs * place_ref[0] + i)
                ),
                pl.BlockSpec((count, HEAD_DIM), lambda i, place_ref: (0, 0)),
            ],
            out_specs=pl.BlockSpec((count, 6 * HEAD_DIM), lambda i, place_ref: (0, i)),
            scratch_shapes=[pltpu.VMEM((count, HEAD_DIM), jnp.float32)] * 2,
        ),
        out_shape=jax.ShapeDtypeStruct((count, columns // 4), jnp.bfloat16),
        compiler_params=pltpu.CompilerParams(vmem_limit_bytes=28 << 20),
        cost_estimate=BRIEF,
        name="attend_back",
    )(place.reshape(1), rows, grad, mask)


ROWS = 128


def normal_parts(values):
    center = values - jnp.mean(values, axis=-1, keepdims=True)
    spread_of = jnp.mean(center * center, axis=-1, keepdims=True)
    scale = lax.rsqrt(spread_of + EPS)
    return center * scale, scale


def normal_back(normed, scale, grad):
    mean_grad = jnp.mean(grad, axis=-1, keepdims=True)
    mean_product = jnp.mean(grad * normed, axis=-1, keepdims=True)
    return (grad - mean_grad - normed * mean_product) * scale


def first_kernel(start_ref, tokens, gain, shift, out):
    normed, _ = normal_parts(tokens[...].astype(jnp.float32))
    out[...] = (normed * gain[...] + shift[...]).astype(out.dtype)


def middle_kernel(
    start_ref,
    tokens,
    own_upper,
    own_lower,
    upper,
    lower,
    active,
    bias,
    gain,
    shift,
    middle_out,
    rows_out,
):
    in_upper = pl.program_id(0) < pl.num_programs(0) // 2
    own = jnp.where(in_upper, own_upper[...], own_lower[...])
    got = jnp.where(in_upper, upper[...], lower[...])
    branch = own.astype(jnp.float32) + got.astype(jnp.float32) + bias[...]
    middle = tokens[...].astype(jnp.float32) + active[...] * branch
    middle_out[...] = middle
    normed, _ = normal_parts(middle)
    rows_out[...] = (normed * gain[...] + shift[...]).astype(rows_out.dtype)


def add_totals(totals, parts):
    first = pl.program_id(0) == 0
    for index, part in enumerate(parts):
        total = jnp.sum(part, axis=0, keepdims=True)
        totals[index : index + 1, :] = total + jnp.where(
            first, 0.0, totals[index : index + 1, :]
        )


def middle_back_kernel(
    start_ref,
    cotangent,
    middle,
    own,
    upper,
    lower,
    peer,
    active,
    gain,
    grad_out,
    branch_out,
    totals,
):
    in_upper = pl.program_id(0) < pl.num_programs(0) // 2
    got = jnp.where(in_upper, upper[...], lower[...])
    grad_second = own[...] + got.astype(jnp.float32) + peer[...].astype(jnp.float32)
    normed, scale = normal_parts(middle[...])
    grad_middle = cotangent[...].astype(jnp.float32) + normal_back(
        normed, scale, grad_second * gain[...]
    )
    grad_out[...] = grad_middle
    grad_branch = (active[...] * grad_middle).astype(jnp.bfloat16)
    branch_out[...] = grad_branch
    add_totals(
        totals, (grad_second * normed, grad_second, grad_branch.astype(jnp.float32))
    )


def first_back_kernel(start_ref, tokens, grad_middle, own, got, gain, grad_out, totals):
    grad_first = own[...] + got[...].astype(jnp.float32)
    normed, scale = normal_parts(tokens[...].astype(jnp.float32))
    grad = grad_middle[...] + normal_back(normed, scale, grad_first * gain[...])
    grad_out[...] = grad.astype(grad_out.dtype)
    add_totals(totals, (grad_first * normed, grad_first))


def by_rows(kernel, start, count, arrays, outs, name):
    width = arrays[0][0].shape[1]
    specs = {
        "rows": pl.BlockSpec((ROWS, width), lambda i, start_ref: (i, 0)),
        "from": pl.BlockSpec((ROWS, width), lambda i, start_ref: (start_ref[0] + i, 0)),
        "vector": pl.BlockSpec((1, width), lambda i, start_ref: (0, 0)),
        "totals": pl.BlockSpec((8, width), lambda i, start_ref: (0, 0)),
        "upper": pl.BlockSpec(
            (ROWS, width), lambda i, start_ref: (jnp.minimum(i, count // ROWS // 2 - 1), 0)
        ),
        "lower": pl.BlockSpec(
            (ROWS, width), lambda i, start_ref: (jnp.maximum(i - count // ROWS // 2, 0), 0)
        ),
        "flag": pl.BlockSpec((ROWS, 1), lambda i, start_ref: (i, 0)),
        "flag from": pl.BlockSpec((ROWS, 1), lambda i, start_ref: (start_ref[0] + i, 0)),
    }
    shapes = [
        jax.ShapeDtypeStruct((8 if kind == "totals" else count, width), dtype)
        for kind, dtype in outs
    ]
    moved = sum(
        count * width * array.dtype.itemsize for array, kind in arrays if kind in ("rows", "from")
    ) + sum(math.prod(shape.shape) * shape.dtype.itemsize for shape in shapes)
    return pl.pallas_call(
        kernel,
        grid_spec=pltpu.PrefetchScalarGridSpec(
            num_scalar_prefetch=1,
            grid=(count // ROWS,),
            in_specs=[specs[kind] for _, kind in arrays],
            out_specs=[specs[kind] for kind, _ in outs],
        ),
        out_shape=shapes,
        compiler_params=pltpu.CompilerParams(vmem_limit_bytes=28 << 20),
        cost_estimate=BRIEF,
        name=name,
    )(start, *[array for array, _ in arrays])


def after(value, *others):
    return lax.optimization_barrier((value, others))[0]


MIDDLE_KINDS = ("rows", "upper", "lower", "upper", "lower", "flag", "vector", "vector", "vector")
BACK_KINDS = ("from", "from", "rows", "upper", "lower", "rows", "flag from", "vector")


class Line:
    def __init__(self):
        self.last = None

    def __call__(self, function, *arrays):
        if self.last is not None:
            arrays = lax.optimization_barrier((arrays, self.last))[0]
        result = function(*arrays)
        self.last = jax.tree.leaves(result)[0]
        return result


def whole_sequence_device(
    tokens,
    exit_layer,
    first_gain,
    first_shift,
    query_weight,
    query_bias,
    key_weight,
    value_weight,
    value_bias,
    output_weight,
    output_bias,
    second_gain,
    second_shift,
    expand_weight,
    expand_bias,
    shrink_weight,
    shrink_bias,
    cotangent,
):
    seq_count, local_len, width = tokens.shape
    heads_rows = query_weight.shape[0]
    hidden_rows = expand_weight.shape[0]
    seq_size = lax.axis_size("seq")
    dp_size = lax.axis_size(DEVICES) // seq_size
    depth, core = lax.axis_index("seq"), lax.axis_index("core")
    along_x, along_y = lax.axis_index("x"), lax.axis_index("y")
    place = 2 * along_y + along_x
    dp = 2 * place + core
    parity = depth % 2
    full_len = local_len * seq_size
    half_len = full_len // 2
    f32, low = jnp.float32, jnp.bfloat16

    def route(flip):
        pairs = []
        for i in range(dp_size):
            for j in range(seq_size):
                target = 2 * (i % 2) + (j % 2 if not flip else 1 - j % 2)
                pairs.append((i * seq_size + j, (i // 2 * 2 + j // 2) * seq_size + target))
        return pairs

    def send(first, second, back):
        routes = [[(b, a) if back else (a, b) for a, b in route(flip)] for flip in (False, True)]
        return lax.ppermute(first, DEVICES, routes[0]), lax.ppermute(second, DEVICES, routes[1])

    def by_parity(values):
        return pick(parity, values[0], values[1]), pick(parity, values[1], values[0])

    def paired(first, second):
        return ordered(parity, first[None], second[None], 0)

    def by_core(own, other):
        return ordered(core, own, other, 0)

    def half_rows(matrix, which):
        return lax.dynamic_slice_in_dim(matrix, which * half_len, half_len, 0)

    line = Line()
    depth_rows = heads_rows * seq_size
    hidden_block = hidden_rows * seq_size
    places = [place ^ d for d in range(4)]
    sides = [core, 1 - core]
    bits = jnp.stack([along_y, along_x, core])

    def through_z(shard):
        return lax.all_gather(shard, "seq", axis=0, tiled=True)

    devices = dp_size * seq_size
    all_dp = jnp.arange(dp_size, dtype=jnp.int32)[:, None]
    all_seq = jnp.arange(seq_size, dtype=jnp.int32)[None, :]
    relative = ((all_dp ^ dp) * seq_size + (depth - all_seq) % seq_size).reshape(-1)

    def shift_z(values, steps):
        return lax.ppermute(
            values, "seq", [(i, (i + steps) % seq_size) for i in range(seq_size)]
        )

    def stacked(own, other):
        return jnp.concatenate([own, other], 0)

    vectors = [first_gain, first_shift, query_bias, value_bias, output_bias, second_gain]
    vectors += [second_shift, shrink_bias, expand_bias]
    shard_qkv = line(
        lambda *parts: jnp.concatenate(parts, 0), query_weight, key_weight, value_weight
    )
    z_qkv = through_z(shard_qkv)
    vectors = line(lambda *parts: jnp.concatenate(parts)[None, None], *vectors)
    shifted = [shift_z(vectors, steps) for steps in range(1, seq_size)]
    alive = (exit_layer > LAYER).astype(low)
    flag_rows = jnp.broadcast_to(alive[:, None, :], (seq_count, 16, local_len))
    flag_rows = jnp.pad(flag_rows, ((0, 0), (0, 0), (0, width - local_len)))
    message = line(
        lambda *arrays: by_parity(jnp.concatenate(arrays, axis=1)), tokens, flag_rows, cotangent
    )
    vectors = line(lambda *parts: jnp.concatenate(parts, 1), vectors, *shifted)
    mine, theirs = line(lambda rows: split_columns(core, rows, hidden_block), shrink_weight)
    theirs = swap(theirs, CORE)
    vectors = line(stacked, vectors, swap(vectors, ALONG_Y))
    shard_shrink = line(stacked, mine, theirs)
    mine, theirs = line(lambda rows: split_columns(along_x, rows, hidden_block), shard_shrink)
    theirs = swap(theirs, ALONG_X)
    vectors = line(stacked, vectors, swap(vectors, ALONG_X))
    shard_shrink = line(stacked, mine, theirs)
    vectors = line(stacked, vectors, swap(vectors, CORE))
    vectors = line(
        lambda rows: rows.reshape(2, 2, 2, seq_size, -1)
        .transpose(2, 1, 0, 3, 4)
        .reshape(devices, -1)[relative]
        .astype(f32),
        vectors,
    )
    shrink_across = swap(shard_shrink, ALONG_Y)

    def vector(index):
        return vectors[:, index * heads_rows : (index + 1) * heads_rows].reshape(1, -1)

    def of_core(matrix):
        cut = matrix.reshape(4, 2, seq_size, -1)
        return lax.dynamic_index_in_dim(cut, core, 1, False).reshape(4 * seq_size, -1)

    def of_quarter(matrix):
        cut = matrix.reshape(2, 4, seq_size, -1)
        return lax.dynamic_index_in_dim(cut, 2 * along_x + core, 1, False)

    gain_one, shift_one = vector(0), vector(1)
    bias_query = of_core(vectors[:, 2 * heads_rows : 3 * heads_rows])
    bias_value = of_core(vectors[:, 3 * heads_rows : 4 * heads_rows])
    bias_rows = jnp.stack([bias_query, jnp.zeros_like(bias_query), bias_value], 1).reshape(1, -1)
    bias_out, gain_two, shift_two, bias_shrink = vector(4), vector(5), vector(6), vector(7)
    bias_expand = of_quarter(vectors[:, 8 * heads_rows :]).reshape(1, -1)

    half_qkv = 3 * depth_rows // 2

    z_qkv = after(z_qkv, vectors, shard_shrink)
    beside_qkv, across_qkv = swap(z_qkv, ALONG_X), swap(z_qkv, ALONG_Y)
    z_out = through_z(after(output_weight, z_qkv))
    arrived = send(*(after(part, z_out) for part in message), False)
    mine, theirs = line(lambda rows: split_columns(core, rows, depth_rows), z_out)
    rows_out = line(
        lambda own, other: jnp.concatenate([own, other], 1), mine, swap(theirs, CORE)
    )
    upper = line(lambda rows: rows[:half_qkv], beside_qkv)
    lower = line(lambda rows: rows[half_qkv:], across_qkv)
    upper, lower = swap(upper, ALONG_Y), swap(lower, ALONG_X)
    z_expand = through_z(after(expand_weight, *arrived))
    w_qkv = line(
        lambda *pieces: arrange(
            pieces,
            (half_qkv, width),
            [(p, r, 0) for p in range(3) for r in range(2)] + [(3, 0, 0), (4, 0, 0)],
            [2 * places[d] + r for d in range(4) for r in range(2)],
        ),
        z_qkv,
        beside_qkv,
        across_qkv,
        upper,
        lower,
    )
    half = line(paired, *arrived)
    joined = line(by_core, half, swap(half, CORE))
    inputs = joined[:, :local_len].reshape(full_len, width)
    alive = joined[:, local_len, :local_len].reshape(full_len, 1)
    cotangent_full = joined[:, local_len + 16 :].reshape(full_len, width)
    active = alive.astype(f32)
    mask = jnp.broadcast_to((alive - 1) * jnp.bfloat16(1e30), (full_len, HEAD_DIM))

    no_start = jnp.zeros((1,), jnp.int32)
    half_start = (core * (half_len // ROWS)).reshape(1)

    (first_rows,) = line(
        lambda *arrays: by_rows(
            first_kernel,
            no_start,
            full_len,
            list(zip(arrays, ("rows", "vector", "vector"))),
            [("rows", low)],
            "first_norm",
        ),
        inputs,
        gain_one,
        shift_one,
    )
    rows_out = after(rows_out, w_qkv)
    out_beside, out_across = swap(rows_out, ALONG_X), swap(rows_out, ALONG_Y)
    across_expand = swap(z_expand, ALONG_Y)

    qkv = line(
        lambda rows, weight: multiply((rows,), (weight,), True, bias=bias_rows), first_rows, w_qkv
    )
    out_corner = swap(line(lambda rows: rows * jnp.bfloat16(1), out_across), ALONG_X)
    grad_shrunk = line(
        lambda flags, grads: (flags * grads.astype(f32)).astype(low), active, cotangent_full
    )
    sent_gs = line(lambda rows: half_rows(rows, core), grad_shrunk)
    gs_got = swap(sent_gs, ALONG_X)
    mixed = line(attend, qkv, mask)
    w_out = line(
        lambda *pieces: arrange(
            pieces,
            (depth_rows, width // 2),
            [(p, 0, i) for p in range(4) for i in range(2)],
            [2 * places[d] + sides[i] for d in range(4) for i in range(2)],
        ),
        after(rows_out, z_expand),
        out_beside,
        out_across,
        out_corner,
    )
    branch = line(
        lambda rows, weight: multiply((rows,), (weight,), True, halves=True), mixed, w_out
    )
    branch_got = [swap(part, CORE) for part in branch]
    shard_shrink = line(stacked, shard_shrink, shrink_across)
    w_shrink = through_z(after(shard_shrink, z_expand, branch))
    middle, second_rows = line(
        lambda *arrays: by_rows(
            middle_kernel,
            no_start,
            full_len,
            list(zip(arrays, MIDDLE_KINDS)),
            [("rows", f32), ("rows", low)],
            "middle_norm",
        ),
        inputs,
        *branch,
        *branch_got,
        active,
        bias_out,
        gain_two,
        shift_two,
    )
    second_half = line(lambda rows: half_rows(rows, core), second_rows)
    second_got = swap(second_half, ALONG_X)
    gs_own = line(lambda rows: regroup(bits, rows, seq_size), grad_shrunk)
    w_expand = line(
        lambda *pieces: arrange(
            pieces,
            (hidden_block // 2, width),
            [(p, r, 0) for p in range(2) for r in range(2)],
            [2 * (along_y ^ p) + r for p in range(2) for r in range(2)],
        ),
        z_expand,
        across_expand,
    )

    def lift(rows, weight):
        return multiply((rows,), (weight,), True, bias=bias_expand, lift=True)

    activated, slope = line(lift, second_rows, w_expand)
    second_peer = line(by_core, second_got, swap(second_got, CORE))
    activated_peer, slope_peer = line(lift, second_peer, w_expand)

    gs_peer = line(by_core, gs_got, swap(after(gs_got, activated), CORE))
    gs_peer = line(lambda rows: regroup(bits, rows, seq_size), gs_peer)
    def scatter_z(total):
        return lax.psum_scatter(total, "seq", scatter_dimension=0, tiled=True)

    def units(grads, weight, slopes):
        return multiply((grads,), (weight,), False, slope=slopes)

    def their_half(left, weight, by_columns=False):
        return half_dot(1 - core, left, weight, by_columns, low)

    def my_half(left, weight, by_columns=False):
        return half_dot(core, left, weight, by_columns, f32)

    def add_rounded(left, right):
        return (left.astype(f32) + right.astype(f32)).astype(low)

    shrink_part = line(
        lambda own, peer, rows, rows_peer: outer_rows_of(
            (own, peer), (rows, rows_peer), width // 2, range(2)
        ),
        gs_own,
        gs_peer,
        activated,
        activated_peer,
    )
    shrink_rows = scatter_z(shrink_part)
    grad_pre_peer, peer_sums = line(units, gs_peer, w_shrink, slope_peer)
    theirs = line(their_half, grad_pre_peer, w_expand)
    mine = line(my_half, grad_pre_peer, w_expand)
    peer_half = line(add_rounded, mine, swap(theirs, CORE))
    second_from_peer = swap(peer_half, ALONG_X)
    grad_pre, own_sums = line(units, gs_own, w_shrink, slope)
    theirs = line(their_half, grad_pre, w_expand)
    second_got = [swap(part, CORE) for part in jnp.split(theirs, 2)]
    second_mine = line(my_half, grad_pre, w_expand)
    def expand_part(d):
        return line(
            lambda *arrays: outer_rows_of(arrays[:2], arrays[2:], hidden_block, [along_y ^ d]),
            grad_pre,
            grad_pre_peer,
            second_rows,
            second_peer,
        )

    expand_across = expand_part(1)
    expand_got = swap(expand_across, ALONG_Y)

    grad_middle, grad_branch_half, middle_totals = line(
        lambda *arrays: by_rows(
            middle_back_kernel,
            half_start,
            half_len,
            list(zip(arrays, BACK_KINDS)),
            [("rows", f32), ("rows", low), ("totals", f32)],
            "middle_norm_back",
        ),
        cotangent_full,
        middle,
        second_mine,
        *second_got,
        second_from_peer,
        active,
        gain_two,
    )
    branch_got = swap(grad_branch_half, CORE)

    grad_branch = line(by_core, grad_branch_half, branch_got)
    grad_mixed = line(
        lambda grads, weight: multiply((grads,), (weight,), False, tile=256), grad_branch, w_out
    )
    out_part = line(
        lambda grads, rows: outer_sides(
            [2 * places[d] + sides[i] for d in range(4) for i in range(2)], grads, rows, depth_rows
        ),
        grad_branch,
        mixed,
    )
    out_parts = [out_part[d] for d in range(4)]
    out_corner = swap(out_parts[3], ALONG_X)
    out_got_x = swap(out_parts[1], ALONG_X)

    def attend_piece(d):
        return line(
            lambda rows, grads, flags: attend_back(rows, grads, flags, places[d]),
            qkv,
            grad_mixed,
            mask,
        )

    def qkv_part(d, rows, source):
        return line(
            lambda grads, inputs_low: outer_rows_of((grads,), (inputs_low,), rows, [source]),
            grad_qkv[d],
            first_rows,
        )

    grad_qkv = {3: attend_piece(3)}
    corner_got = swap(after(qkv_part(3, 2 * half_qkv, 0), out_corner), ALONG_X)
    grad_qkv[1] = attend_piece(1)
    out_got_y = swap(line(add_rounded, out_parts[2], out_corner), ALONG_Y)
    qkv_x = swap(qkv_part(1, 2 * half_qkv, 0), ALONG_X)
    grad_qkv[2] = attend_piece(2)
    across = qkv_part(2, 2 * half_qkv, 0)
    expand_here = expand_part(0)
    grad_qkv[0] = attend_piece(0)
    qkv_y = swap(line(add_rounded, across, corner_got), ALONG_Y)
    expand_sum = line(add_rounded, expand_here, expand_got)
    expand_rows = scatter_z(expand_sum)
    here = qkv_part(0, 2 * half_qkv, 0)
    grads_qkv = tuple(grad_qkv[d] for d in range(4))

    def first_half(which, dtype):
        return lambda *arrays: half_dot(which, arrays[:4], arrays[4], False, dtype, places=places)

    peer_theirs = line(lambda rows, weight: their_half(rows, weight, True), activated_peer, w_shrink)
    peer_got = swap(peer_theirs, CORE)
    first_theirs = line(first_half(1 - core, low), *grads_qkv, w_qkv)
    first_got = swap(first_theirs, CORE)
    peer_mine = line(lambda rows, weight: my_half(rows, weight, True), activated_peer, w_shrink)
    first_mine = line(first_half(core, f32), *grads_qkv, w_qkv)
    to_peer = line(
        lambda *parts: regroup_back(bits, *parts, seq_size, low), peer_mine, peer_got
    )
    from_peer = swap(to_peer, ALONG_X)
    half = shrink_rows.shape[0] // 2
    shrink_got = swap(line(lambda rows: rows[half:], shrink_rows), ALONG_Y)
    qkv_sum = line(
        lambda *parts: sum(part.astype(f32) for part in parts).astype(low), here, qkv_x, qkv_y
    )
    qkv_rows = scatter_z(qkv_sum)
    grad_half, first_totals = line(
        lambda *arrays: by_rows(
            first_back_kernel,
            half_start,
            half_len,
            list(zip(arrays, ("from", "rows", "rows", "rows", "vector"))),
            [("rows", low), ("totals", f32)],
            "first_norm_back",
        ),
        inputs,
        grad_middle,
        first_mine,
        first_got,
        gain_one,
    )
    tokens_parts = send(
        *line(lambda rows: by_parity(rows.reshape(2, local_len, width)), grad_half), True
    )

    def beside_own(peer, rows, flags, bias):
        return half_rows(rows, core) + half_rows(flags, core) * (peer.astype(f32) + bias)

    theirs = line(lambda rows, weight: their_half(rows, weight, True), activated, w_shrink)
    shrunk_got = swap(theirs, CORE)
    mine = line(lambda rows, weight: my_half(rows, weight, True), activated, w_shrink)
    rest = line(beside_own, from_peer, middle, active, bias_shrink)

    def column_sum(matrix):
        return jnp.sum(matrix.astype(f32), axis=0)

    def all_devices(totals, rows):
        return totals.reshape(devices, rows)

    def core_devices(totals, rows):
        cut = totals.reshape(4, 1, seq_size, rows)
        return ordered(core, cut, jnp.zeros_like(cut), 1).reshape(devices, rows)

    def quarter_devices(totals, rows):
        cut = totals.reshape(2, 1, seq_size, rows)
        none = jnp.zeros_like(cut)
        quarters = [jnp.where(2 * along_x + core == q, cut, none) for q in range(4)]
        return jnp.concatenate(quarters, 1).reshape(devices, rows)

    def all_sums(first, middle_sums, shrunk_grads, own, peer, *grads):
        qkv_sums = jnp.stack([column_sum(part) for part in grads])[jnp.stack(places)]
        qkv_sums = qkv_sums.reshape(4 * seq_size, 3, heads_rows)
        sums = jnp.concatenate(
            [
                all_devices(first[0], heads_rows),
                all_devices(first[1], heads_rows),
                core_devices(qkv_sums[:, 0], heads_rows),
                core_devices(qkv_sums[:, 2], heads_rows),
                all_devices(middle_sums[2], heads_rows),
                all_devices(middle_sums[0], heads_rows),
                all_devices(middle_sums[1], heads_rows),
                all_devices(0.5 * column_sum(shrunk_grads), heads_rows),
                quarter_devices(own + peer, hidden_rows),
            ],
            axis=1,
        )
        return sums.reshape(dp_size, seq_size, -1)[jnp.arange(dp_size) ^ dp]

    def fold(values, got):
        return values[: got.shape[0]] + got

    sums = line(
        all_sums, first_totals, middle_totals, grad_shrunk, own_sums, peer_sums, *grads_qkv
    )
    sums = line(fold, sums, swap(sums[dp_size // 2 :], ALONG_Y))
    sums = line(fold, sums, swap(sums[dp_size // 4 :], ALONG_X))
    shrunk = line(lambda *parts: regroup_back(bits, *parts, seq_size, f32), mine, shrunk_got)

    sums = line(fold, sums, swap(sums[dp_size // 8 :], CORE))
    out_sum = line(
        lambda *parts: sum(part.astype(f32) for part in parts).astype(low),
        out_parts[0],
        out_got_x,
        out_got_y,
    )
    out_got = swap(line(lambda rows: rows[:, width // 2 :], out_sum), CORE)
    out_rows = line(
        lambda rows, got: weave_columns(core, rows[:, : width // 2], got, depth_rows),
        out_sum,
        out_got,
    )

    def with_vectors(totals, rows):
        totals = totals.reshape(seq_size, 1, -1).astype(low)
        totals = jnp.pad(totals, ((0, 0), (0, 15), (0, width - totals.shape[2])))
        rows = jnp.concatenate([rows.reshape(seq_size, -1, width), totals], 1)
        return rows.reshape(-1, width)

    out_rows = scatter_z(line(with_vectors, sums, out_rows))

    def finish(part, other, flags):
        out = other + half_rows(flags, core) * part
        return by_parity(out.astype(low).reshape(2, local_len, width))

    out_halves = send(*line(finish, shrunk, rest, active), True)
    tokens_grad = line(paired, *tokens_parts)
    shrink_rows = line(lambda rows, got: add_rounded(rows[:half], got), shrink_rows, shrink_got)
    half = half // 2
    shrink_got = swap(line(lambda rows: rows[half:], shrink_rows), ALONG_X)
    expand_weight_grad = line(lambda rows: rows.astype(f32), expand_rows)
    qkv_weight_grad = line(lambda rows: rows.astype(f32), qkv_rows)
    shrink_rows = line(
        lambda rows, got: weave_columns(along_x, rows[:half], got, hidden_block),
        shrink_rows,
        shrink_got,
    )
    shrink_got = swap(line(lambda rows: rows[heads_rows:], shrink_rows), CORE)
    layer_out = line(paired, *out_halves)
    shrink_weight_grad = line(
        lambda rows, got: weave_columns(core, rows[:heads_rows], got, hidden_block).astype(f32),
        shrink_rows,
        shrink_got,
    )
    output_weight_grad, sums = line(
        lambda rows: (
            rows[:heads_rows].astype(f32),
            rows[heads_rows, : 8 * heads_rows + hidden_rows].astype(f32),
        ),
        out_rows,
    )

    def vector_grad(index):
        return sums[index * heads_rows : (index + 1) * heads_rows]

    return (
        layer_out,
        tokens_grad,
        vector_grad(0),
        vector_grad(1),
        qkv_weight_grad[:heads_rows],
        vector_grad(2),
        qkv_weight_grad[heads_rows : 2 * heads_rows],
        qkv_weight_grad[2 * heads_rows :],
        vector_grad(3),
        output_weight_grad,
        vector_grad(4),
        vector_grad(5),
        vector_grad(6),
        expand_weight_grad,
        sums[8 * heads_rows :],
        shrink_weight_grad,
        vector_grad(7),
    )


def general_device(
    tokens,
    exit_layer,
    first_gain,
    first_shift,
    query_weight,
    query_bias,
    key_weight,
    value_weight,
    value_bias,
    output_weight,
    output_bias,
    second_gain,
    second_shift,
    expand_weight,
    expand_bias,
    shrink_weight,
    shrink_bias,
    cotangent,
):
    seq_count, local_len, width = tokens.shape
    hidden_width = shrink_weight.shape[1]
    total_rows = seq_count * local_len
    heads = width // HEAD_DIM
    inputs = tokens.reshape(total_rows, width).astype(jnp.float32)
    active = (exit_layer > LAYER).astype(jnp.float32).reshape(total_rows, 1)
    gain_one, shift_one = (
        lax.all_gather(first_gain, ("dp", "seq"), axis=0, tiled=True),
        lax.all_gather(first_shift, ("dp", "seq"), axis=0, tiled=True),
    )
    gain_one = gain_one.astype(jnp.float32)
    shift_one = shift_one.astype(jnp.float32)
    normed_in = normalize(inputs)
    first_rows = (normed_in * gain_one + shift_one).astype(jnp.bfloat16)
    blank = jnp.zeros((total_rows, width), jnp.bfloat16)
    attention_init = (blank, blank, blank) + ()
    w_query = lax.all_gather(query_weight, ("dp", "seq"), axis=0, tiled=True)
    b_query = lax.all_gather(query_bias, ("dp", "seq"), axis=0, tiled=True)
    w_key = lax.all_gather(key_weight, ("dp", "seq"), axis=0, tiled=True)
    w_value = lax.all_gather(value_weight, ("dp", "seq"), axis=0, tiled=True)
    b_value = lax.all_gather(value_bias, ("dp", "seq"), axis=0, tiled=True)
    queries = place_cols(
        attention_init[0], project(first_rows, w_query) + b_query.astype(jnp.float32)
    )
    key_rows = place_cols(attention_init[1], project(first_rows, w_key))
    value_rows = place_cols(
        attention_init[2], project(first_rows, w_value) + b_value.astype(jnp.float32)
    )
    stored = attention_init[3:]
    gathered = (queries, key_rows, value_rows) + stored
    queries, key_rows, value_rows = (gathered[0], gathered[1], gathered[2])
    query_local = queries.reshape(seq_count, local_len, width)
    key_local = key_rows.reshape(seq_count, local_len, width)
    value_local = value_rows.reshape(seq_count, local_len, width)
    alive_local = active.reshape(seq_count, local_len)
    key_all, value_all, alive_all = (
        lax.all_gather(key_local, "seq", axis=1, tiled=True),
        lax.all_gather(value_local, "seq", axis=1, tiled=True),
        lax.all_gather(alive_local.astype(jnp.bfloat16), "seq", axis=1, tiled=True),
    )
    full_len = key_all.shape[1]
    offset = lax.axis_index("seq") * local_len
    query_pos = offset + jnp.arange(local_len, dtype=jnp.int32)
    key_pos = jnp.arange(full_len, dtype=jnp.int32)
    causal = key_pos[None, :] <= query_pos[:, None]
    allowed = causal[None, None] & (alive_all.astype(jnp.float32)[:, None, None, :] > 0.5)
    factor = HEAD_DIM ** (-0.5)
    group = min(8, heads)
    group_width = group * HEAD_DIM
    group_total = heads // group

    def group_parts(start_col):
        q_part = lax.dynamic_slice_in_dim(query_local, start_col, group_width, 2).reshape(
            seq_count, local_len, group, HEAD_DIM
        )
        k_part = lax.dynamic_slice_in_dim(key_all, start_col, group_width, 2).reshape(
            seq_count, full_len, group, HEAD_DIM
        )
        v_part = lax.dynamic_slice_in_dim(value_all, start_col, group_width, 2).reshape(
            seq_count, full_len, group, HEAD_DIM
        )
        scores = (
            jnp.einsum("sqhd,skhd->shqk", q_part, k_part, preferred_element_type=jnp.float32)
            * factor
        )
        scores = jnp.where(allowed, scores, jnp.float32(-1e30))
        return (q_part, k_part, v_part, scores)

    def forward_group(group_index, state):
        mixed_all, log_total = state
        start_col = group_index * group_width
        q_part, k_part, v_part, scores = group_parts(start_col)
        row_max = jnp.max(scores, axis=-1, keepdims=True)
        raised = jnp.exp(scores - row_max)
        totals = jnp.sum(raised, axis=-1, keepdims=True)
        weights_low = (raised / totals).astype(jnp.bfloat16)
        outcome = jnp.einsum(
            "shqk,skhd->sqhd", weights_low, v_part, preferred_element_type=jnp.float32
        )
        mixed_all = lax.dynamic_update_slice_in_dim(
            mixed_all,
            outcome.reshape(seq_count, local_len, group_width).astype(jnp.bfloat16),
            start_col,
            2,
        )
        log_total = lax.dynamic_update_slice_in_dim(
            log_total, (row_max + jnp.log(totals))[..., 0], group_index * group, 1
        )
        return (mixed_all, log_total)

    mixed_all, log_total = lax.fori_loop(
        0,
        group_total,
        forward_group,
        (
            jnp.zeros((seq_count, local_len, width), jnp.bfloat16),
            jnp.zeros((seq_count, heads, local_len), jnp.float32),
        ),
    )
    mixed = mixed_all.reshape(total_rows, width)
    vector_blank = jnp.zeros((width,), jnp.bfloat16)
    output_init = (jnp.zeros((total_rows, width), jnp.float32), vector_blank, vector_blank) + ()
    w_out = lax.all_gather(output_weight, ("dp", "seq"), axis=0, tiled=True)
    b_out = lax.all_gather(output_bias, ("dp", "seq"), axis=0, tiled=True)
    g_piece = lax.all_gather(second_gain, ("dp", "seq"), axis=0, tiled=True)
    s_piece = lax.all_gather(second_shift, ("dp", "seq"), axis=0, tiled=True)
    branch = place_cols(output_init[0], project(mixed, w_out) + b_out.astype(jnp.float32))
    gain_two = g_piece
    shift_two = s_piece
    stored = output_init[3:]
    folded = (branch, gain_two, shift_two) + stored
    branch = folded[0]
    gain_two = folded[1].astype(jnp.float32)
    shift_two = folded[2].astype(jnp.float32)
    middle = inputs + active * branch
    normed_mid = normalize(middle)
    second_rows = (normed_mid * gain_two + shift_two).astype(jnp.bfloat16)
    expand_init = (jnp.zeros((total_rows, hidden_width), jnp.float32),) + ()
    w_expand = lax.all_gather(expand_weight, ("dp", "seq"), axis=0, tiled=True)
    b_expand = lax.all_gather(expand_bias, ("dp", "seq"), axis=0, tiled=True)
    hidden_pre = place_cols(
        expand_init[0], project(second_rows, w_expand) + b_expand.astype(jnp.float32)
    )
    stored = expand_init[1:]
    expanded = (hidden_pre,) + stored
    hidden_pre = expanded[0]

    def gelu_exact(pre_values):
        return jax.nn.gelu(pre_values, approximate=False)

    activated_full, gelu_back = jax.vjp(gelu_exact, hidden_pre)
    activated = activated_full.astype(jnp.bfloat16)
    shrink_init = (jnp.zeros((total_rows, width), jnp.float32),) + ()
    w_shrink = lax.all_gather(shrink_weight, ("dp", "seq"), axis=0, tiled=True)
    b_shrink = lax.all_gather(shrink_bias, ("dp", "seq"), axis=0, tiled=True)
    shrunk = place_cols(shrink_init[0], project(activated, w_shrink) + b_shrink.astype(jnp.float32))
    stored = shrink_init[1:]
    shrunk_all = (shrunk,) + stored
    shrunk = shrunk_all[0]
    layer_out = (middle + active * shrunk).astype(jnp.bfloat16).reshape(seq_count, local_len, width)
    grad_out = cotangent.reshape(total_rows, width).astype(jnp.float32)
    grad_shrunk = (active * grad_out).astype(jnp.bfloat16)
    grad_units = through(
        grad_shrunk, lax.all_gather(shrink_weight, ("dp", "seq"), axis=0, tiled=True)
    )
    grad_pre = gelu_back(grad_units)[0].astype(jnp.bfloat16)
    grad_second = through(
        grad_pre, lax.all_gather(expand_weight, ("dp", "seq"), axis=0, tiled=True)
    )
    mid_value, mid_back = jax.vjp(normalize, middle)
    grad_middle = grad_out + mid_back(grad_second * gain_two)[0]
    grad_branch = (active * grad_middle).astype(jnp.bfloat16)
    grad_mixed = through(
        grad_branch, lax.all_gather(output_weight, ("dp", "seq"), axis=0, tiled=True)
    )
    grad_mixed_local = grad_mixed.astype(jnp.bfloat16).reshape(seq_count, local_len, width)

    def backward_group(group_index, state):
        grad_query_all, grad_key_all, grad_value_all = state
        start_col = group_index * group_width
        q_part, k_part, v_part, scores = group_parts(start_col)
        g_part = lax.dynamic_slice_in_dim(grad_mixed_local, start_col, group_width, 2).reshape(
            seq_count, local_len, group, HEAD_DIM
        )
        lse_part = lax.dynamic_slice_in_dim(log_total, group_index * group, group, 1)
        soft = jnp.exp(scores - lse_part[..., None])
        grad_probs = jnp.einsum(
            "sqhd,skhd->shqk", g_part, v_part, preferred_element_type=jnp.float32
        )
        value_term = jnp.einsum(
            "shqk,sqhd->skhd", soft.astype(jnp.bfloat16), g_part, preferred_element_type=jnp.float32
        )
        centered = jnp.sum(soft * grad_probs, axis=-1, keepdims=True)
        grad_scores = (soft * (grad_probs - centered)).astype(jnp.bfloat16)
        query_term = (
            jnp.einsum("shqk,skhd->sqhd", grad_scores, k_part, preferred_element_type=jnp.float32)
            * factor
        )
        key_term = (
            jnp.einsum("shqk,sqhd->skhd", grad_scores, q_part, preferred_element_type=jnp.float32)
            * factor
        )
        grad_query_all = lax.dynamic_update_slice_in_dim(
            grad_query_all, query_term.reshape(seq_count, local_len, group_width), start_col, 2
        )
        grad_key_all = lax.dynamic_update_slice_in_dim(
            grad_key_all, key_term.reshape(seq_count, full_len, group_width), start_col, 2
        )
        grad_value_all = lax.dynamic_update_slice_in_dim(
            grad_value_all, value_term.reshape(seq_count, full_len, group_width), start_col, 2
        )
        return (grad_query_all, grad_key_all, grad_value_all)

    grad_query_all, grad_key_all, grad_value_all = lax.fori_loop(
        0,
        group_total,
        backward_group,
        (
            jnp.zeros((seq_count, local_len, width), jnp.float32),
            jnp.zeros((seq_count, full_len, width), jnp.float32),
            jnp.zeros((seq_count, full_len, width), jnp.float32),
        ),
    )
    key_sum, value_sum = (
        lax.psum_scatter(grad_key_all, "seq", scatter_dimension=1, tiled=True),
        lax.psum_scatter(grad_value_all, "seq", scatter_dimension=1, tiled=True),
    )
    grad_query = grad_query_all.astype(jnp.bfloat16).reshape(total_rows, width)
    grad_key = key_sum.astype(jnp.bfloat16).reshape(total_rows, width)
    grad_value = value_sum.astype(jnp.bfloat16).reshape(total_rows, width)
    total = through(grad_query, lax.all_gather(query_weight, ("dp", "seq"), axis=0, tiled=True))
    total = total + through(grad_key, lax.all_gather(key_weight, ("dp", "seq"), axis=0, tiled=True))
    grad_first = total + through(
        grad_value, lax.all_gather(value_weight, ("dp", "seq"), axis=0, tiled=True)
    )
    in_value, in_back = jax.vjp(normalize, inputs)
    tokens_grad = (
        (grad_middle + in_back(grad_first * gain_one)[0])
        .astype(jnp.bfloat16)
        .reshape(seq_count, local_len, width)
    )
    first_scaled = grad_first * normed_in
    second_scaled = grad_second * normed_mid
    vectors = jnp.stack(
        [
            column_total(grad_query),
            column_total(grad_value),
            column_total(grad_branch),
            column_total(grad_shrunk),
            column_total(first_scaled),
            column_total(grad_first),
            column_total(second_scaled),
            column_total(grad_second),
        ],
        axis=1,
    )

    def scattered(grad_cols, inputs):
        return lax.psum_scatter(
            outer_rows(grad_cols, inputs), ("dp", "seq"), scatter_dimension=0, tiled=True
        )

    vector_sums = lax.psum_scatter(vectors, ("dp", "seq"), scatter_dimension=0, tiled=True)
    expand_bias_sums = lax.psum_scatter(
        column_total(grad_pre), ("dp", "seq"), scatter_dimension=0, tiled=True
    )
    shrink_sums = scattered(grad_shrunk, activated)
    grad_pre, second_rows, shrink_sums = lax.optimization_barrier(
        (grad_pre, second_rows, shrink_sums)
    )
    expand_sums = scattered(grad_pre, second_rows)
    grad_branch, grad_query, grad_key, grad_value, expand_sums = lax.optimization_barrier(
        (grad_branch, grad_query, grad_key, grad_value, expand_sums)
    )
    return (
        layer_out,
        tokens_grad,
        vector_sums[:, 4],
        vector_sums[:, 5],
        scattered(grad_query, first_rows),
        vector_sums[:, 0],
        scattered(grad_key, first_rows),
        scattered(grad_value, first_rows),
        vector_sums[:, 1],
        scattered(grad_branch, mixed),
        vector_sums[:, 2],
        vector_sums[:, 6],
        vector_sums[:, 7],
        expand_sums,
        expand_bias_sums,
        shrink_sums,
        vector_sums[:, 3],
    )


def solution(mesh):
    chips = mesh.shape["dp"] // 2
    if chips == 4 and mesh.shape["seq"] == 4:
        names = ("y", "x", "core", "seq")
        mesh = Mesh(mesh.devices.reshape(2, 2, 2, 4), names)
        dp, rows, per_device = names[:3], names, whole_sequence_device
    else:
        dp, rows, per_device = "dp", ("dp", "seq"), general_device
    in_specs = (
        P(dp, "seq", None),
        P(dp, "seq"),
        P(rows),
        P(rows),
        P(rows, None),
        P(rows),
        P(rows, None),
        P(rows, None),
        P(rows),
        P(rows, None),
        P(rows),
        P(rows),
        P(rows),
        P(rows, None),
        P(rows),
        P(rows, None),
        P(rows),
        P(dp, "seq", None),
    )
    out_specs = (
        P(dp, "seq", None),
        P(dp, "seq", None),
        P(rows),
        P(rows),
        P(rows, None),
        P(rows),
        P(rows, None),
        P(rows, None),
        P(rows),
        P(rows, None),
        P(rows),
        P(rows),
        P(rows),
        P(rows, None),
        P(rows),
        P(rows, None),
        P(rows),
    )
    return jax.shard_map(
        per_device, mesh=mesh, in_specs=in_specs, out_specs=out_specs, check_vma=False
    )
```
